512 devices in a mesh: grp: 4 (over x_hi, core), row: 16 (over z), col: 8 (over x_lo, y).
Axes of the slice: x: 4 (x_hi: 2, x_lo: 2; x = x_hi * 2 + x_lo), y: 4, z: 16, core: 2. Of those that a mesh axis runs over, the one named last changes fastest.
Arguments:
- tokens_in: bfloat16 [1024, 6144], P('col', 'row'), may hold values from -6 to 6
- cotangent: bfloat16 [1024, 6144], P('col', 'grp'), may hold values from -6 to 6
- sample_rows: int32 [256], P('col'), may hold values from 0 to 1023, as said below
- act_inverse: bfloat16 [6144, 6144], P('grp', 'row'), as said below
- grad_inverse: bfloat16 [6144, 6144], P('grp', 'col'), as said below
Outputs:
- precond: float32 [6144, 6144], P(('grp', 'row'), 'col')
- act_cov: float32 [6144, 6144], P(('row', 'col'), 'grp')
- grad_cov: float32 [6144, 6144], P(('row', 'col'), 'grp')
The draws below stay inside these ranges and needn't reach their ends.
Inputs may be any that keep to these rules, and one draw needn't show every extreme that they name: `sample_rows`: for each block c, entries c * 32 to (c + 1) * 32 - 1 are distinct token rows of that block, between c * 128 and (c + 1) * 128 - 1. `act_inverse`: Symmetric. `grad_inverse`: Symmetric.
All inputs are finite; a program needn't handle non-finite values.
Results may differ from the reference program's by a relative error of at most 0.03.
Values may be sent and summed in bfloat16 or wider, within the bound.
No kernel may reach another device: no remote copies, remote signals or barrier semaphores. Data moves between devices by JAX's collectives and lax.ppermute only.
A program may use at most 64 MiB of HBM per device.

```python
import jax
import jax.numpy as jnp
from jax import lax

D = 6144
TOK_DEV = 128
SAMP_DEV = 32
TOKENS = 1024
SAMPLES = 256
N_ROW = 16


def inverse_factor(key, spread):
    noise = jax.random.normal(jax.random.fold_in(key, 11), (D, D), jnp.float32)
    mixed = (noise + noise.T) * (spread / D ** 0.5)
    level = jnp.exp(jax.random.uniform(jax.random.fold_in(key, 12), (D,), jnp.float32, -0.7, 0.7))
    return (mixed + jnp.diag(level)).astype(jnp.bfloat16)


def draw_act_inverse(key, part):
    key = jax.random.fold_in(key, 1)
    return inverse_factor(key, 0.35)


def draw_grad_inverse(key, part):
    key = jax.random.fold_in(key, 2)
    return inverse_factor(key, 0.3)


def draw_sample_rows(key, part):
    key = jax.random.fold_in(key, 3)
    count = TOKENS // TOK_DEV
    keys = jax.random.split(key, count)
    orders = jax.vmap(lambda k: jax.random.permutation(k, TOK_DEV))(keys)[:, :SAMP_DEV]
    blocks = jnp.arange(count, dtype=jnp.int32)
    target = jnp.where(blocks == 0, 0, jnp.where(blocks == count - 1, TOK_DEV - 1, orders[:, 0]))
    shifted = (orders - orders[:, :1] + target[:, None] + TOK_DEV) % TOK_DEV
    return (shifted + blocks[:, None] * TOK_DEV).reshape(count * SAMP_DEV).astype(jnp.int32)


def level_of(rng, extent, cuts, low, largest):
    gain, own = 1.0, jax.random.fold_in(rng, 6)
    for dim, blocks in cuts:
        heights = jnp.exp(jax.random.uniform(jax.random.fold_in(own, dim), (blocks,), jnp.float32, low / len(cuts), largest / len(cuts)))
        gain = gain * jnp.repeat(heights, extent[dim] // blocks).reshape([-1 if axis == dim else 1 for axis in range(len(extent))])
    return gain


def scatter_about(own_key, shape, deviation, limit, cuts=(), kind=jnp.bfloat16):
    gain = level_of(own_key, shape, cuts, -0.22, 0.18) if cuts else 1.0
    result = jax.random.normal(own_key, shape, jnp.float32) * deviation * gain
    return jnp.minimum(jnp.maximum(result, -limit), limit).astype(kind)


def setup_inputs(seed: int = 0) -> dict:
    arg_keys = jax.random.split(jax.random.key(seed), 6)
    return {
        "tokens_in": scatter_about(arg_keys[0], (TOKENS, D), 1.0, 6.0, ((0, 8), (1, 16))),
        "cotangent": scatter_about(arg_keys[1], (TOKENS, D), 1.0, 6.0, ((0, 8), (1, 4))),
        "sample_rows": draw_sample_rows(jax.random.fold_in(arg_keys[5], 71), 0),
        "act_inverse": draw_act_inverse(jax.random.fold_in(arg_keys[5], 71), 0),
        "grad_inverse": draw_grad_inverse(jax.random.fold_in(arg_keys[5], 71), 0),
    }


def reference(tokens_in, cotangent, sample_rows, act_inverse, grad_inverse):
    blocks_x = tokens_in.reshape(TOKENS // TOK_DEV, TOK_DEV, D)
    blocks_g = cotangent.reshape(TOKENS // TOK_DEV, TOK_DEV, D)

    def grad_step(total, pair):
        part = lax.dot_general(pair[0], pair[1], (((0,), (0,)), ((), ())), preferred_element_type=jnp.float32)
        part = lax.optimization_barrier(part.astype(jnp.bfloat16)).astype(jnp.float32)
        return total + part, None

    summed, unused = lax.scan(grad_step, jnp.zeros((D, D), jnp.float32), (blocks_x, blocks_g))
    grad_weight = summed.astype(jnp.bfloat16)
    right = jnp.dot(grad_weight, grad_inverse, preferred_element_type=jnp.float32).astype(jnp.bfloat16)
    inner = D // N_ROW

    def left_step(total, block):
        begin = block.astype(jnp.int32) * inner
        cols = lax.dynamic_slice_in_dim(act_inverse, begin, inner, 1)
        rows = lax.dynamic_slice_in_dim(right, begin, inner, 0)
        part = jnp.dot(cols, rows, preferred_element_type=jnp.float32)
        part = lax.optimization_barrier(part.astype(jnp.bfloat16)).astype(jnp.float32)
        return total + part, None

    precond, unused = lax.scan(left_step, jnp.zeros((D, D), jnp.float32), jnp.arange(N_ROW, dtype=jnp.int32))
    picked_x = jnp.take(tokens_in, sample_rows, axis=0)
    picked_g = jnp.take(cotangent, sample_rows, axis=0)
    dims = (((0,), (0,)), ((), ()))
    act_cov = lax.dot_general(picked_x, picked_x, dims, preferred_element_type=jnp.float32) / SAMPLES
    grad_cov = lax.dot_general(picked_g, picked_g, dims, preferred_element_type=jnp.float32) / SAMPLES
    return precond, act_cov, grad_cov
```

```python
import jax
import jax.numpy as jnp
from jax import lax
from jax.sharding import PartitionSpec as P

BF = jnp.bfloat16
F32 = jnp.float32
LANES = 128


def body(tokens_in, cotangent, sample_rows, act_inverse, grad_inverse):
    n_row = lax.axis_size("row")
    n_col = lax.axis_size("col")
    n_grp = lax.axis_size("grp")
    grp = lax.axis_index("grp")
    row = lax.axis_index("row")
    col = lax.axis_index("col")
    tok, feat_row = tokens_in.shape
    feat_grp = cotangent.shape[1]
    samp = sample_rows.shape[0]
    total = samp * n_col
    quarter = samp // n_grp
    tile = feat_row // n_col
    out_rows = feat_grp // n_row

    half = tok // 2
    g_lo = lax.all_gather(cotangent[:half], "col", axis=0)
    g_hi = lax.all_gather(cotangent[half:], "col", axis=0)

    part = lax.dot_general(
        act_inverse, tokens_in, (((1,), (1,)), ((), ())), preferred_element_type=F32
    ).astype(BF)
    part = part.reshape(n_row, out_rows, tok)
    offsets = sample_rows - col * tok
    own = lax.dynamic_slice_in_dim(offsets, grp * quarter, quarter, 0)
    picked_x = jnp.take(tokens_in, own, axis=0)
    strips = feat_row // LANES
    x_send = picked_x.reshape(quarter, strips, LANES).transpose(1, 0, 2)
    x_send = x_send.reshape(1, strips * quarter, LANES)
    x_send = jnp.broadcast_to(x_send, (n_row, strips * quarter, LANES))
    first = lax.all_to_all(jnp.concatenate([part, x_send], axis=1), "row", 0, 0)
    left = jnp.sum(first[:, :out_rows].astype(F32), axis=0).astype(BF)
    x_all = first[:, out_rows:].reshape(n_grp, -1, LANES)
    x_rows = x_all.shape[1]

    picked_g = jnp.take(cotangent, offsets, axis=0)
    own_g = lax.dynamic_slice_in_dim(picked_g, (row % n_grp) * feat_row, feat_row, 1)
    side_g = own_g.reshape(samp, n_col, tile).transpose(1, 0, 2)
    side_x = picked_x.reshape(quarter, n_col, tile).transpose(1, 0, 2)
    side_x = jnp.pad(side_x, ((0, 0), (0, samp - quarter), (0, 0)))
    place = jnp.broadcast_to(offsets.astype(BF)[None, :, None], (n_col, samp, LANES - 2 * tile))
    side = jnp.concatenate([side_g, side_x, place], axis=2)

    both = (n_grp, n_col)
    send = jnp.concatenate(
        [
            jnp.broadcast_to(left, both + left.shape),
            jnp.broadcast_to(x_all[:, None], both + x_all.shape[1:]),
            jnp.broadcast_to(side[None], both + side.shape[1:]),
        ],
        axis=2,
    )
    send = send.reshape((n_grp * n_col,) + send.shape[2:])
    got = lax.all_to_all(send, ("grp", "col"), 0, 0)
    got = got.reshape(both + got.shape[1:])
    lefts = got[:, :, :out_rows]
    samples_x = got[:, :, out_rows : out_rows + x_rows]
    sides = got[:, :, out_rows + x_rows :]

    v_lo = jnp.einsum("ctf,fn->ctn", g_lo, grad_inverse, preferred_element_type=F32).astype(BF)
    v_hi = jnp.einsum("ctf,fn->ctn", g_hi, grad_inverse, preferred_element_type=F32).astype(BF)
    v_all = jnp.concatenate([v_lo, v_hi], axis=1)
    term = jnp.einsum("gcat,ctn->gan", lefts, v_all, preferred_element_type=F32).astype(BF)
    term = lax.all_to_all(term, "grp", 0, 0)
    precond = jnp.sum(term.astype(F32), axis=0)

    scale = 1.0 / total
    x_full = samples_x.reshape(n_grp, n_col, x_rows // quarter, quarter, LANES)
    x_left = sides[:, :, :quarter, tile : 2 * tile]
    act_cov = jnp.einsum("gcsa,gcwsf->awf", x_left, x_full, preferred_element_type=F32)
    act_cov = act_cov.reshape(tile, feat_grp) * scale

    mine = lax.dynamic_index_in_dim(sides, row // n_grp, 0, keepdims=False)
    hot = mine[:, :, 2 * tile : 2 * tile + 1] == jnp.arange(tok, dtype=F32).astype(BF)
    spread = jnp.einsum(
        "cst,csa->cta", hot.astype(BF), mine[:, :, :tile], preferred_element_type=F32
    ).astype(BF)
    grad_cov = jnp.einsum(
        "cta,ctf->af", spread[:, :half], g_lo, preferred_element_type=F32
    ) + jnp.einsum("cta,ctf->af", spread[:, half:], g_hi, preferred_element_type=F32)
    return (precond, act_cov, grad_cov * scale)


def solution(mesh):
    return jax.shard_map(
        body,
        mesh=mesh,
        in_specs=(P("col", "row"), P("col", "grp"), P("col"), P("grp", "row"), P("grp", "col")),
        out_specs=(P(("grp", "row"), "col"), P(("row", "col"), "grp"), P(("row", "col"), "grp")),
        check_vma=False,
    )
```

```python
import jax
import jax.numpy as jnp
from jax import lax
from jax.sharding import PartitionSpec as P

BF = jnp.bfloat16
F32 = jnp.float32
LANES = 128


def body(tokens_in, cotangent, sample_rows, act_inverse, grad_inverse):
    n_row = lax.axis_size("row")
    n_col = lax.axis_size("col")
    n_grp = lax.axis_size("grp")
    grp = lax.axis_index("grp")
    row = lax.axis_index("row")
    col = lax.axis_index("col")
    tok, feat_row = tokens_in.shape
    feat_grp = cotangent.shape[1]
    samp = sample_rows.shape[0]
    total = samp * n_col
    quarter = samp // n_grp
    tile = feat_row // n_col
    out_rows = feat_grp // n_row

    g_all = lax.all_to_all(
        jnp.broadcast_to(cotangent, (n_col,) + cotangent.shape), "col", 0, 0
    )

    part = lax.dot_general(
        act_inverse, tokens_in, (((1,), (1,)), ((), ())), preferred_element_type=F32
    ).astype(BF)
    part = part.reshape(n_row, out_rows, tok)
    offsets = sample_rows - col * tok
    own = lax.dynamic_slice_in_dim(offsets, grp * quarter, quarter, 0)
    picked_x = jnp.take(tokens_in, own, axis=0)
    strips = feat_row // LANES
    x_send = picked_x.reshape(quarter, strips, LANES).transpose(1, 0, 2)
    x_send = x_send.reshape(1, strips * quarter, LANES)
    x_send = jnp.broadcast_to(x_send, (n_row, strips * quarter, LANES))
    first = lax.all_to_all(jnp.concatenate([part, x_send], axis=1), "row", 0, 0)
    left = jnp.sum(first[:, :out_rows].astype(F32), axis=0).astype(BF)
    x_all = first[:, out_rows:].reshape(n_grp, -1, LANES)
    x_rows = x_all.shape[1]

    picked_g = jnp.take(cotangent, offsets, axis=0)
    per = feat_grp // feat_row
    own_g = lax.dynamic_slice_in_dim(picked_g, (row % per) * feat_row, feat_row, 1)
    side_g = own_g.reshape(samp, n_col, tile).transpose(1, 0, 2)
    side_x = picked_x.reshape(quarter, n_col, tile).transpose(1, 0, 2)
    side_x = jnp.pad(side_x, ((0, 0), (0, samp - quarter), (0, 0)))
    place = jnp.broadcast_to(offsets.astype(BF)[None, :, None], (n_col, samp, LANES - 2 * tile))
    side = jnp.concatenate([side_g, side_x, place], axis=2)

    both = (n_grp, n_col)
    send = jnp.concatenate(
        [
            jnp.broadcast_to(left, both + left.shape),
            jnp.broadcast_to(x_all[:, None], both + x_all.shape[1:]),
            jnp.broadcast_to(side[None], both + side.shape[1:]),
        ],
        axis=2,
    )
    send = send.reshape((n_grp * n_col,) + send.shape[2:])
    got = lax.all_to_all(send, ("grp", "col"), 0, 0)
    got = got.reshape(both + got.shape[1:])
    lefts = got[:, :, :out_rows]
    samples_x = got[:, :, out_rows : out_rows + x_rows]
    sides = got[:, :, out_rows + x_rows :]

    v_all = jnp.einsum("ctf,fn->ctn", g_all, grad_inverse, preferred_element_type=F32).astype(BF)
    term = jnp.einsum("gcat,ctn->gan", lefts, v_all, preferred_element_type=F32).astype(BF)
    term = lax.all_to_all(term, "grp", 0, 0)
    precond = jnp.sum(term.astype(F32), axis=0)

    scale = 1.0 / total
    x_full = samples_x.reshape(n_grp, n_col, x_rows // quarter, quarter, LANES)
    x_left = sides[:, :, :quarter, tile : 2 * tile]
    act_cov = jnp.einsum("gcsa,gcwsf->awf", x_left, x_full, preferred_element_type=F32)
    act_cov = act_cov.reshape(tile, feat_grp) * scale

    mine = lax.dynamic_index_in_dim(sides, row // per, 0, keepdims=False)
    hot = mine[:, :, 2 * tile : 2 * tile + 1] == jnp.arange(tok, dtype=F32).astype(BF)
    spread = jnp.einsum(
        "cst,csa->cta", hot.astype(BF), mine[:, :, :tile], preferred_element_type=F32
    ).astype(BF)
    grad_cov = jnp.einsum("cta,ctf->af", spread, g_all, preferred_element_type=F32)
    return (precond, act_cov, grad_cov * scale)


def solution(mesh):
    return jax.shard_map(
        body,
        mesh=mesh,
        in_specs=(P("col", "row"), P("col", "grp"), P("col"), P("grp", "row"), P("grp", "col")),
        out_specs=(P(("grp", "row"), "col"), P(("row", "col"), "grp"), P(("row", "col"), "grp")),
        check_vma=False,
    )
```

```python
import jax
import jax.numpy as jnp
from jax import lax
from jax.sharding import PartitionSpec as P

BF = jnp.bfloat16
F32 = jnp.float32
LANES = 128


def body(tokens_in, cotangent, sample_rows, act_inverse, grad_inverse):
    n_row = lax.axis_size("row")
    n_col = lax.axis_size("col")
    n_grp = lax.axis_size("grp")
    grp = lax.axis_index("grp")
    row = lax.axis_index("row")
    col = lax.axis_index("col")
    tok, feat_row = tokens_in.shape
    feat_grp = cotangent.shape[1]
    samp = sample_rows.shape[0]
    total = samp * n_col
    quarter = samp // n_grp
    tile = feat_row // n_col
    out_rows = feat_grp // n_row


    part = lax.dot_general(
        act_inverse, tokens_in, (((1,), (1,)), ((), ())), preferred_element_type=F32
    ).astype(BF)
    part = part.reshape(n_row, out_rows, tok)
    offsets = sample_rows - col * tok
    own = lax.dynamic_slice_in_dim(offsets, grp * quarter, quarter, 0)
    picked_x = jnp.take(tokens_in, own, axis=0)
    strips = feat_row // LANES
    x_send = picked_x.reshape(quarter, strips, LANES).transpose(1, 0, 2)
    x_send = x_send.reshape(1, strips * quarter, LANES)
    x_send = jnp.broadcast_to(x_send, (n_row, strips * quarter, LANES))
    payload, own_cot = lax.optimization_barrier(
        (jnp.concatenate([part, x_send], axis=1), cotangent)
    )
    first = lax.all_to_all(payload, "row", 0, 0)
    blocks = [cotangent] + [
        lax.ppermute(own_cot, "col", [(i, (i + k) % n_col) for i in range(n_col)])
        for k in range(1, n_col)
    ]
    left = jnp.sum(first[:, :out_rows].astype(F32), axis=0).astype(BF)
    x_all = first[:, out_rows:].reshape(n_grp, -1, LANES)
    x_rows = x_all.shape[1]

    picked_g = jnp.take(cotangent, offsets, axis=0)
    per = feat_grp // feat_row
    own_g = lax.dynamic_slice_in_dim(picked_g, (row % per) * feat_row, feat_row, 1)
    side_g = own_g.reshape(samp, n_col, tile).transpose(1, 0, 2)
    side_x = picked_x.reshape(quarter, n_col, tile).transpose(1, 0, 2)
    side_x = jnp.pad(side_x, ((0, 0), (0, samp - quarter), (0, 0)))
    place = jnp.broadcast_to(offsets.astype(BF)[None, :, None], (n_col, samp, LANES - 2 * tile))
    side = jnp.concatenate([side_g, side_x, place], axis=2)

    both = (n_grp, n_col)
    send = jnp.concatenate(
        [
            jnp.broadcast_to(left, both + left.shape),
            jnp.broadcast_to(x_all[:, None], both + x_all.shape[1:]),
            jnp.broadcast_to(side[None], both + side.shape[1:]),
        ],
        axis=2,
    )
    send = send.reshape((n_grp * n_col,) + send.shape[2:])
    got = lax.all_to_all(send, ("grp", "col"), 0, 0)
    got = got.reshape(both + got.shape[1:])
    lefts = got[:, :, :out_rows]
    samples_x = got[:, :, out_rows : out_rows + x_rows]
    sides = got[:, :, out_rows + x_rows :]

    term = jnp.zeros((n_grp, out_rows, grad_inverse.shape[1]), F32)
    for k, block in enumerate(blocks):
        source = (col - k) % n_col
        v_blk = jnp.dot(block, grad_inverse, preferred_element_type=F32).astype(BF)
        u_blk = lax.dynamic_index_in_dim(lefts, source, 1, keepdims=False)
        term = term + jnp.einsum("gat,tn->gan", u_blk, v_blk, preferred_element_type=F32)
    term = term.astype(BF)
    term = lax.all_to_all(term, "grp", 0, 0)
    precond = jnp.sum(term.astype(F32), axis=0)

    scale = 1.0 / total
    x_full = samples_x.reshape(n_grp, n_col, x_rows // quarter, quarter, LANES)
    x_left = sides[:, :, :quarter, tile : 2 * tile]
    act_cov = jnp.einsum("gcsa,gcwsf->awf", x_left, x_full, preferred_element_type=F32)
    act_cov = act_cov.reshape(tile, feat_grp) * scale

    mine = lax.dynamic_index_in_dim(sides, row // per, 0, keepdims=False)
    hot = mine[:, :, 2 * tile : 2 * tile + 1] == jnp.arange(tok, dtype=F32).astype(BF)
    spread = jnp.einsum(
        "cst,csa->cta", hot.astype(BF), mine[:, :, :tile], preferred_element_type=F32
    ).astype(BF)
    grad_cov = jnp.zeros((tile, feat_grp), F32)
    for k, block in enumerate(blocks):
        mask = lax.dynamic_index_in_dim(spread, (col - k) % n_col, 0, keepdims=False)
        grad_cov = grad_cov + jnp.einsum("ta,tf->af", mask, block, preferred_element_type=F32)
    return (precond, act_cov, grad_cov * scale)


def solution(mesh):
    return jax.shard_map(
        body,
        mesh=mesh,
        in_specs=(P("col", "row"), P("col", "grp"), P("col"), P("grp", "row"), P("grp", "col")),
        out_specs=(P(("grp", "row"), "col"), P(("row", "col"), "grp"), P(("row", "col"), "grp")),
        check_vma=False,
    )
```

```python
import jax
import jax.numpy as jnp
from jax import lax
from jax.experimental import pallas as pl
from jax.experimental.pallas import tpu as pltpu
from jax.sharding import PartitionSpec as P

BF = jnp.bfloat16
F32 = jnp.float32
LANES = 128


def final_kernel(col_ref, u_ref, *refs):
    v_refs, out_ref = refs[:-1], refs[-1]
    n_col = len(v_refs)
    groups, unused, rows, tok = u_ref.shape
    col = col_ref[0]
    total = None
    for k in range(0, n_col, 2):
        sides = []
        for j in (k, k + 1):
            source = lax.rem(col - j + n_col, n_col)
            sides.append(u_ref[:, source].reshape(groups * rows, tok))
        u_pair = jnp.concatenate(sides, axis=1)
        v_pair = jnp.concatenate([v_refs[k][...], v_refs[k + 1][...]], axis=0)
        term = jnp.dot(u_pair, v_pair, preferred_element_type=F32)
        total = term if total is None else total + term
    out_ref[...] = total.reshape(out_ref.shape).astype(out_ref.dtype)


def final_product(col, got, v_blocks, out_rows):
    n_grp, n_col, unused, tok = got.shape
    width = v_blocks[0].shape[1]
    return pl.pallas_call(
        final_kernel,
        out_shape=jax.ShapeDtypeStruct((n_grp, out_rows, width), BF),
        grid=(1,),
        in_specs=[
            pl.BlockSpec(memory_space=pltpu.SMEM),
            pl.BlockSpec((n_grp, n_col, out_rows, tok), lambda i: (0, 0, 0, 0)),
        ]
        + [pl.BlockSpec((tok, width), lambda i: (0, 0))] * n_col,
        out_specs=pl.BlockSpec((n_grp, out_rows, width), lambda i: (0, 0, 0)),
        compiler_params=pltpu.CompilerParams(vmem_limit_bytes=32 * 1024 * 1024),
        cost_estimate=pl.CostEstimate(
            flops=2 * n_grp * out_rows * n_col * tok * width,
            bytes_accessed=4 * 1024 * 1024,
            transcendentals=0,
        ),
    )(jnp.reshape(col, (1,)).astype(jnp.int32), got, *v_blocks)


def body(tokens_in, cotangent, sample_rows, act_inverse, grad_inverse):
    n_row = lax.axis_size("row")
    n_col = lax.axis_size("col")
    n_grp = lax.axis_size("grp")
    grp = lax.axis_index("grp")
    row = lax.axis_index("row")
    col = lax.axis_index("col")
    tok, feat_row = tokens_in.shape
    feat_grp = cotangent.shape[1]
    samp = sample_rows.shape[0]
    total = samp * n_col
    quarter = samp // n_grp
    tile = feat_row // n_col
    out_rows = feat_grp // n_row


    part = lax.dot_general(
        act_inverse, tokens_in, (((1,), (1,)), ((), ())), preferred_element_type=F32
    ).astype(BF)
    part = part.reshape(n_row, out_rows, tok)
    offsets = sample_rows - col * tok
    own = lax.dynamic_slice_in_dim(offsets, grp * quarter, quarter, 0)
    picked_x = jnp.take(tokens_in, own, axis=0)
    strips = feat_row // LANES
    x_send = picked_x.reshape(quarter, strips, LANES).transpose(1, 0, 2)
    x_send = x_send.reshape(1, strips * quarter, LANES)
    x_send = jnp.broadcast_to(x_send, (n_row, strips * quarter, LANES))
    payload, own_cot = lax.optimization_barrier(
        (jnp.concatenate([part, x_send], axis=1), cotangent)
    )
    first = lax.all_to_all(payload, "row", 0, 0)
    def shifted(block, k):
        return lax.ppermute(block, "col", [(i, (i + k) % n_col) for i in range(n_col)])

    early = {k: shifted(own_cot, k) for k in (1, 3, 4, 5)}
    first, own_cot, early = lax.optimization_barrier((first, own_cot, early))
    late = {k: shifted(own_cot, k) for k in (2, 6, 7)}
    blocks = [own_cot] + [early[k] if k in early else late[k] for k in range(1, n_col)]
    left = jnp.sum(first[:, :out_rows].astype(F32), axis=0).astype(BF)
    x_all = first[:, out_rows:].reshape(n_grp, -1, LANES)
    x_rows = x_all.shape[1]

    picked_g = jnp.take(cotangent, offsets, axis=0)
    per = feat_grp // feat_row
    own_g = lax.dynamic_slice_in_dim(picked_g, (row % per) * feat_row, feat_row, 1)
    side_g = own_g.reshape(samp, n_col, tile).transpose(1, 0, 2)
    side_x = picked_x.reshape(quarter, n_col, tile).transpose(1, 0, 2)
    side_x = jnp.pad(side_x, ((0, 0), (0, samp - quarter), (0, 0)))
    place = jnp.broadcast_to(offsets.astype(BF)[None, :, None], (n_col, samp, LANES - 2 * tile))
    side = jnp.concatenate([side_g, side_x, place], axis=2)

    both = (n_grp, n_col)
    send = jnp.concatenate(
        [
            jnp.broadcast_to(left, both + left.shape),
            jnp.broadcast_to(x_all[:, None], both + x_all.shape[1:]),
            jnp.broadcast_to(side[None], both + side.shape[1:]),
        ],
        axis=2,
    )
    send = send.reshape((n_grp * n_col,) + send.shape[2:])
    got = lax.all_to_all(send, ("grp", "col"), 0, 0)
    got = got.reshape(both + got.shape[1:])
    samples_x = got[:, :, out_rows : out_rows + x_rows]
    sides = got[:, :, out_rows + x_rows :]

    v_blocks = [
        jnp.dot(block, grad_inverse, preferred_element_type=F32).astype(BF) for block in blocks
    ]
    term = final_product(col, got, v_blocks, out_rows)
    term = lax.all_to_all(term, "grp", 0, 0)
    precond = jnp.sum(term.astype(F32), axis=0)

    scale = 1.0 / total
    x_full = samples_x.reshape(n_grp, n_col, x_rows // quarter, quarter, LANES)
    x_left = sides[:, :, :quarter, tile : 2 * tile]
    act_cov = jnp.einsum("gcsa,gcwsf->awf", x_left, x_full, preferred_element_type=F32)
    act_cov = act_cov.reshape(tile, feat_grp) * scale

    mine = lax.dynamic_index_in_dim(sides, row // per, 0, keepdims=False)
    hot = mine[:, :, 2 * tile : 2 * tile + 1] == jnp.arange(tok, dtype=F32).astype(BF)
    spread = jnp.einsum(
        "cst,csa->cta", hot.astype(BF), mine[:, :, :tile], preferred_element_type=F32
    ).astype(BF)
    grad_cov = jnp.zeros((tile, feat_grp), F32)
    for k, block in enumerate(blocks):
        mask = lax.dynamic_index_in_dim(spread, (col - k) % n_col, 0, keepdims=False)
        grad_cov = grad_cov + jnp.einsum("ta,tf->af", mask, block, preferred_element_type=F32)
    return (precond, act_cov, grad_cov * scale)


def solution(mesh):
    return jax.shard_map(
        body,
        mesh=mesh,
        in_specs=(P("col", "row"), P("col", "grp"), P("col"), P("grp", "row"), P("grp", "col")),
        out_specs=(P(("grp", "row"), "col"), P(("row", "col"), "grp"), P(("row", "col"), "grp")),
        check_vma=False,
    )
```

```python
import functools

import jax
import jax.numpy as jnp
from jax import lax
from jax.experimental import pallas as pl
from jax.experimental.pallas import tpu as pltpu
from jax.sharding import PartitionSpec as P

BF = jnp.bfloat16
F32 = jnp.float32
LANES = 128
FIRST = (((0,), (0,)), ((), ()))
LAST = (((1,), (1,)), ((), ()))
SMEM = pl.BlockSpec(memory_space=pltpu.SMEM)
VMEM = pl.BlockSpec(memory_space=pltpu.VMEM)


def call(kernel, inputs, outs, flops, scratch=()):
    moved = sum(x.size * x.dtype.itemsize for x in list(inputs) + list(outs))
    return pl.pallas_call(
        kernel,
        out_shape=outs,
        in_specs=[SMEM if x.dtype == jnp.int32 else VMEM for x in inputs],
        out_specs=[VMEM] * len(outs),
        scratch_shapes=list(scratch),
        compiler_params=pltpu.CompilerParams(vmem_limit_bytes=40 * 1024 * 1024),
        cost_estimate=pl.CostEstimate(flops=flops, bytes_accessed=moved, transcendentals=0),
    )(*inputs)


def rows_hot(targets, tok):
    shape = (len(targets), tok)
    sub = lax.broadcasted_iota(jnp.int32, shape, 0)
    lane = lax.broadcasted_iota(jnp.int32, shape, 1)
    want = jnp.zeros(shape, jnp.int32)
    for i, target in enumerate(targets):
        want = jnp.where(sub == i, target, want)
    return jnp.where(want == lane, 1.0, 0.0).astype(BF)


def first_kernel(at, picks, x_ref, a_ref, out_ref):
    n_row, unused, tok = out_ref.shape
    part = lax.dot_general(a_ref[...], x_ref[...], LAST, preferred_element_type=F32)
    out_rows = part.shape[0] // n_row
    out_ref[:, :out_rows, :] = part.astype(BF).reshape(n_row, out_rows, tok)
    quarter = picks.shape[0]
    hot = rows_hot([picks[i] for i in range(quarter)], tok)
    chosen = jnp.dot(hot, x_ref[...], preferred_element_type=F32)
    strips = [chosen[:, k : k + LANES] for k in range(0, chosen.shape[1], LANES)]
    block = jnp.concatenate(strips, axis=0).astype(BF)
    out_ref[:, out_rows:, :] = jnp.broadcast_to(block[None], (n_row,) + block.shape)


def pick_kernel(at, picks, g_ref, out_ref):
    tok = g_ref.shape[0]
    samp = picks.shape[0]
    ours = [32 * (i // 8) + 8 * at[1] + i % 8 for i in range(out_ref.shape[0] - samp)]
    hot = rows_hot(ours + [picks[i] for i in range(samp)], tok)
    out_ref[...] = jnp.dot(hot, g_ref[...], preferred_element_type=F32).astype(BF)


def side_kernel(at, picks, x_ref, gy_ref, out_ref):
    n_col, samp, unused = out_ref.shape
    tok, feat = x_ref.shape
    tile = feat // n_col
    quarter = picks.shape[0]
    hot = rows_hot([picks[i] for i in range(quarter)], tok)
    chosen = jnp.dot(hot, x_ref[...], preferred_element_type=F32)
    begin = pl.multiple_of(at[2] * feat, LANES)
    own = gy_ref[gy_ref.shape[0] - samp :, pl.ds(begin, feat)].astype(F32)
    chosen = jnp.concatenate([chosen, jnp.zeros((samp - quarter, feat), F32)], axis=0)
    empty = jnp.zeros((samp, LANES - 2 * tile), F32)
    for c in range(n_col):
        span = slice(c * tile, (c + 1) * tile)
        out_ref[c] = jnp.concatenate([own[:, span], chosen[:, span], empty], axis=1).astype(BF)


def right_kernel(at, b_ref, *refs):
    n_grp = 4
    blocks, outs, held = refs[: -n_grp - 1], refs[-n_grp - 1 : -1], refs[-1]
    each = blocks[0].shape[0] // 2
    rows = jnp.concatenate([block[:each, :] for block in blocks], axis=0)
    term = jnp.dot(rows, b_ref[...], preferred_element_type=F32)
    size = each // n_grp
    held[...] = term.reshape(held.shape)
    for x in range(n_grp):
        piece = held[:, at[0] ^ x]
        outs[x][...] = piece.reshape(len(blocks) * size, -1).astype(BF)


def second_kernel(got_ref, side_ref, out_ref):
    n_grp, n_col, unused, unused = out_ref.shape
    n_row, depth, tok = got_ref.shape
    strip = depth - (depth // 32) * 32
    out_rows = depth - strip
    total = got_ref[0, :out_rows, :].astype(F32)
    for r in range(1, n_row):
        total = total + got_ref[r, :out_rows, :].astype(F32)
    total = jnp.concatenate([total, jnp.zeros((LANES - out_rows, tok), F32)], axis=0)
    turned = jnp.transpose(total).astype(BF)
    size = tok // n_grp
    per = n_row // n_grp
    x_rows = per * strip
    for g in range(n_grp):
        u_block = turned[g * size : (g + 1) * size]
        x_block = got_ref[g * per : (g + 1) * per, out_rows:, :].astype(F32)
        x_block = x_block.reshape(x_rows, tok).astype(BF)
        for c in range(n_col):
            out_ref[g, c, :size, :] = u_block
            out_ref[g, c, size : size + x_rows, :] = x_block
            out_ref[g, c, size + x_rows :, :] = side_ref[c]


def final_kernel(at, got_ref, *refs):
    v_refs, out_ref, held = refs[:-2], refs[-2], refs[-1]
    n_col, spread, size, width = held.shape
    n_grp, out_rows, unused = out_ref.shape
    for j in range(spread):
        plane = lax.rem(at[1] - j + spread, spread)
        block = v_refs[j][...].astype(F32)
        for k in range(n_col):
            source = lax.rem(at[3] - k + n_col, n_col)
            held[source, plane] = block[k * size : (k + 1) * size]
    tokens = n_col * spread * size
    right = held[...].reshape(tokens, width).astype(BF)
    for g in range(n_grp):
        left = got_ref[g, :, : spread * size, :].reshape(tokens, LANES)
        term = lax.dot_general(left, right, FIRST, preferred_element_type=F32)
        out_ref[g] = term[:out_rows].astype(BF)


def factor_kernel(at, got_ref, *refs):
    blocks, act_ref, grad_ref = refs[:-2], refs[-2], refs[-1]
    n_grp, n_col, depth, unused = got_ref.shape
    tile, width = act_ref.shape
    samp = blocks[0].shape[0] // 2
    quarter = samp // n_grp
    total = samp * n_col
    scale = 1.0 / total
    side = depth - samp
    begin = side - quarter * (width // LANES)
    left = got_ref[:, :, side : side + 16, :].astype(F32)[:, :, :quarter, :]
    left = left.reshape(total, LANES).astype(BF)
    span = got_ref[:, :, begin:side, :].astype(F32)
    for t in range(width // LANES):
        strip = span[:, :, t * quarter : (t + 1) * quarter, :].reshape(total, LANES).astype(BF)
        term = lax.dot_general(left, strip, FIRST, preferred_element_type=F32)
        act_ref[:, t * LANES : (t + 1) * LANES] = term[tile : 2 * tile] * scale
    lefts, rights = [], []
    for k, block in enumerate(blocks):
        source = lax.rem(at[3] - k + n_col, n_col)
        lefts.append(got_ref[at[4], source, side:, :])
        rights.append(block[samp:, :])
    left = jnp.concatenate(lefts, axis=0)
    right = jnp.concatenate(rights, axis=0)
    grad_ref[...] = lax.dot_general(left, right, FIRST, preferred_element_type=F32)[:tile] * scale


def body(tokens_in, cotangent, sample_rows, act_inverse, grad_inverse):
    n_row = lax.axis_size("row")
    n_col = lax.axis_size("col")
    n_grp = lax.axis_size("grp")
    grp = lax.axis_index("grp")
    row = lax.axis_index("row")
    col = lax.axis_index("col")
    tok, feat_row = tokens_in.shape
    feat_grp = cotangent.shape[1]
    width = grad_inverse.shape[1]
    samp = sample_rows.shape[0]
    quarter = samp // n_grp
    tile = feat_row // n_col
    out_rows = feat_grp // n_row
    per = feat_grp // feat_row
    strip = quarter * feat_row // LANES
    spread = 4
    size = tok // n_grp // spread
    shape = jax.ShapeDtypeStruct

    at = jnp.stack([grp, row % spread, row % per, col, row // per]).astype(jnp.int32)
    offsets = sample_rows - col * tok
    own = lax.dynamic_slice_in_dim(offsets, grp * quarter, quarter, 0)

    payload = call(
        first_kernel,
        (at, own, tokens_in, act_inverse),
        [shape((n_row, out_rows + strip, tok), BF)],
        2 * feat_grp * feat_row * tok,
    )[0]
    payload, cot = lax.optimization_barrier((payload, cotangent))
    first = lax.all_to_all(payload, "row", 0, 0)

    picked = call(
        pick_kernel,
        (at, offsets, cot),
        [shape((n_grp * size + samp, feat_grp), BF)],
        2 * 64 * tok * feat_grp,
    )[0]
    blocks = [picked] + [
        lax.ppermute(picked, "col", [(i, (i + k) % n_col) for i in range(n_col)])
        for k in range(1, n_col)
    ]
    side = call(
        side_kernel,
        (at, own, tokens_in, picked),
        [shape((n_col, samp, LANES), BF)],
        2 * samp * tok * feat_row,
    )[0]
    first, blocks = lax.optimization_barrier((first, blocks))

    send = call(
        second_kernel,
        (first, side),
        [shape((n_grp, n_col, size * spread + strip * n_row // n_grp + samp, LANES), BF)],
        1000000,
    )[0]
    parts = call(
        right_kernel,
        (at, grad_inverse, *blocks),
        [shape((n_col * size, width), BF)] * n_grp,
        2 * n_col * n_grp * size * feat_grp * width,
        [pltpu.VMEM((n_col, n_grp, size, width), F32)],
    )
    send, parts = lax.optimization_barrier((send, parts))
    got = lax.all_to_all(send.reshape((n_grp * n_col,) + send.shape[2:]), ("grp", "col"), 0, 0)
    got = got.reshape(send.shape)
    total = parts[0].astype(F32)
    for x in range(1, n_grp):
        moved = lax.ppermute(parts[x], "grp", [(i, i ^ x) for i in range(n_grp)])
        total = total + moved.astype(F32)
    right = total.astype(BF)
    rights = [right] + [
        lax.ppermute(
            right, "row", [(i, i - i % spread + (i + j) % spread) for i in range(n_row)]
        )
        for j in range(1, spread)
    ]

    term = call(
        final_kernel,
        (at, got, *rights),
        [shape((n_grp, out_rows, width), BF)],
        2 * n_grp * LANES * n_col * spread * size * width,
        [pltpu.VMEM((n_col, spread, size, width), F32)],
    )[0]
    term, got, blocks = lax.optimization_barrier((term, got, blocks))
    term = lax.all_to_all(term, "grp", 0, 0)
    precond = jnp.sum(term.astype(F32), axis=0)
    act_cov, grad_cov = call(
        factor_kernel,
        (at, got, *blocks),
        [shape((tile, feat_grp), F32)] * 2,
        4 * LANES * samp * n_col * feat_grp,
    )
    return (precond, act_cov, grad_cov)


def solution(mesh):
    return jax.shard_map(
        body,
        mesh=mesh,
        in_specs=(P("col", "row"), P("col", "grp"), P("col"), P("grp", "row"), P("grp", "col")),
        out_specs=(P(("grp", "row"), "col"), P(("row", "col"), "grp"), P(("row", "col"), "grp")),
        check_vma=False,
    )
```

```python
import functools

import jax
import jax.numpy as jnp
from jax import lax
from jax.experimental import pallas as pl
from jax.experimental.pallas import tpu as pltpu
from jax.sharding import PartitionSpec as P

BF = jnp.bfloat16
F32 = jnp.float32
LANES = 128
FIRST = (((0,), (0,)), ((), ()))
LAST = (((1,), (1,)), ((), ()))
SMEM = pl.BlockSpec(memory_space=pltpu.SMEM)
VMEM = pl.BlockSpec(memory_space=pltpu.VMEM)


def call(kernel, inputs, outs, flops, scratch=()):
    moved = sum(x.size * x.dtype.itemsize for x in list(inputs) + list(outs))
    return pl.pallas_call(
        kernel,
        out_shape=outs,
        in_specs=[SMEM if x.dtype == jnp.int32 else VMEM for x in inputs],
        out_specs=[VMEM] * len(outs),
        scratch_shapes=list(scratch),
        compiler_params=pltpu.CompilerParams(vmem_limit_bytes=40 * 1024 * 1024),
        cost_estimate=pl.CostEstimate(flops=flops, bytes_accessed=moved, transcendentals=0),
    )(*inputs)


def source_of(col, k):
    return 4 * ((col // 4) ^ (k % 2)) + lax.rem(col % 4 - k // 2 + 4, 4)


def rows_hot(targets, tok):
    shape = (len(targets), tok)
    sub = lax.broadcasted_iota(jnp.int32, shape, 0)
    lane = lax.broadcasted_iota(jnp.int32, shape, 1)
    want = jnp.zeros(shape, jnp.int32)
    for i, target in enumerate(targets):
        want = jnp.where(sub == i, target, want)
    return jnp.where(want == lane, 1.0, 0.0).astype(BF)


def first_kernel(at, picks, x_ref, a_ref, out_ref):
    n_row, unused, tok = out_ref.shape
    part = lax.dot_general(a_ref[...], x_ref[...], LAST, preferred_element_type=F32)
    out_rows = part.shape[0] // n_row
    out_ref[:, :out_rows, :] = part.astype(BF).reshape(n_row, out_rows, tok)
    quarter = picks.shape[0]
    hot = rows_hot([picks[i] for i in range(quarter)], tok)
    chosen = jnp.dot(hot, x_ref[...], preferred_element_type=F32)
    strips = [chosen[:, k : k + LANES] for k in range(0, chosen.shape[1], LANES)]
    block = jnp.concatenate(strips, axis=0).astype(BF)
    out_ref[:, out_rows:, :] = jnp.broadcast_to(block[None], (n_row,) + block.shape)


def pick_kernel(at, picks, g_ref, out_ref):
    tok = g_ref.shape[0]
    samp = picks.shape[0]
    ours = [32 * (i // 8) + 8 * at[1] + i % 8 for i in range(out_ref.shape[0] - samp)]
    hot = rows_hot(ours + [picks[i] for i in range(samp)], tok)
    out_ref[...] = jnp.dot(hot, g_ref[...], preferred_element_type=F32).astype(BF)


def side_kernel(at, picks, x_ref, gy_ref, out_ref):
    n_col, samp, unused = out_ref.shape
    tok, feat = x_ref.shape
    tile = feat // n_col
    quarter = picks.shape[0]
    hot = rows_hot([picks[i] for i in range(quarter)], tok)
    chosen = jnp.dot(hot, x_ref[...], preferred_element_type=F32)
    begin = pl.multiple_of(at[2] * feat, LANES)
    own = gy_ref[gy_ref.shape[0] - samp :, pl.ds(begin, feat)].astype(F32)
    chosen = jnp.concatenate([chosen, jnp.zeros((samp - quarter, feat), F32)], axis=0)
    empty = jnp.zeros((samp, LANES - 2 * tile), F32)
    for c in range(n_col):
        span = slice(c * tile, (c + 1) * tile)
        out_ref[c] = jnp.concatenate([own[:, span], chosen[:, span], empty], axis=1).astype(BF)


def right_kernel(at, b_ref, *refs):
    blocks, keep_ref, give_ref, held = refs[:-3], refs[-3], refs[-2], refs[-1]
    n_blk, n_grp, size, width = held.shape
    rows = jnp.concatenate([block[...] for block in blocks], axis=0)
    term = jnp.dot(rows, b_ref[...], preferred_element_type=F32)
    held[...] = term.reshape(held.shape)
    half = n_blk * size
    for x in range(n_grp):
        piece = held[:, at[0] ^ x].reshape(half, width).astype(BF)
        out = give_ref if x % 2 else keep_ref
        out[(x // 2) * half : (x // 2 + 1) * half, :] = piece


def second_kernel(got_ref, side_ref, out_ref):
    n_grp, n_col, unused, unused = out_ref.shape
    n_row, depth, tok = got_ref.shape
    strip = depth - (depth // 32) * 32
    out_rows = depth - strip
    total = got_ref[0, :out_rows, :].astype(F32)
    for r in range(1, n_row):
        total = total + got_ref[r, :out_rows, :].astype(F32)
    total = jnp.concatenate([total, jnp.zeros((LANES - out_rows, tok), F32)], axis=0)
    turned = jnp.transpose(total).astype(BF)
    size = tok // n_grp
    per = n_row // n_grp
    x_rows = per * strip
    for g in range(n_grp):
        u_block = turned[g * size : (g + 1) * size]
        x_block = got_ref[g * per : (g + 1) * per, out_rows:, :].astype(F32)
        x_block = x_block.reshape(x_rows, tok).astype(BF)
        for c in range(n_col):
            out_ref[g, c, :size, :] = u_block
            out_ref[g, c, size : size + x_rows, :] = x_block
            out_ref[g, c, size + x_rows :, :] = side_ref[c]


def final_kernel(at, got_ref, *refs):
    v_refs, out_ref, held = refs[:-2], refs[-2], refs[-1]
    n_col, spread, size, width = held.shape
    n_grp, out_rows, unused = out_ref.shape
    for j in range(spread):
        plane = lax.rem(at[1] - j + spread, spread)
        block = v_refs[j][...].astype(F32)
        for k in range(n_col):
            held[source_of(at[3], k), plane] = block[k * size : (k + 1) * size]
    tokens = n_col * spread * size
    right = held[...].reshape(tokens, width).astype(BF)
    for g in range(n_grp):
        left = got_ref[g, :, : spread * size, :].reshape(tokens, LANES)
        term = lax.dot_general(left, right, FIRST, preferred_element_type=F32)
        out_ref[g] = term[:out_rows].astype(BF)


def factor_kernel(at, got_ref, *refs):
    blocks, act_ref, grad_ref = refs[:-2], refs[-2], refs[-1]
    n_grp, n_col, depth, unused = got_ref.shape
    tile, width = act_ref.shape
    samp = blocks[0].shape[0] // 2
    quarter = samp // n_grp
    total = samp * n_col
    scale = 1.0 / total
    side = depth - samp
    begin = side - quarter * (width // LANES)
    left = got_ref[:, :, side : side + 16, :].astype(F32)[:, :, :quarter, :]
    left = left.reshape(total, LANES).astype(BF)
    span = got_ref[:, :, begin:side, :].astype(F32)
    for t in range(width // LANES):
        strip = span[:, :, t * quarter : (t + 1) * quarter, :].reshape(total, LANES).astype(BF)
        term = lax.dot_general(left, strip, FIRST, preferred_element_type=F32)
        act_ref[:, t * LANES : (t + 1) * LANES] = term[tile : 2 * tile] * scale
    lefts, rights = [], []
    for k in range(n_col):
        lefts.append(got_ref[at[4], source_of(at[3], k), side:, :])
    for block in blocks:
        rights.append(block[...])
    left = jnp.concatenate(lefts, axis=0)
    right = jnp.concatenate(rights, axis=0)
    grad_ref[...] = lax.dot_general(left, right, FIRST, preferred_element_type=F32)[:tile] * scale


def body(tokens_in, cotangent, sample_rows, act_inverse, grad_inverse):
    n_row = lax.axis_size("row")
    n_col = lax.axis_size("col")
    n_grp = lax.axis_size("grp")
    grp = lax.axis_index("grp")
    row = lax.axis_index("row")
    col = lax.axis_index("col")
    tok, feat_row = tokens_in.shape
    feat_grp = cotangent.shape[1]
    width = grad_inverse.shape[1]
    samp = sample_rows.shape[0]
    quarter = samp // n_grp
    tile = feat_row // n_col
    out_rows = feat_grp // n_row
    per = feat_grp // feat_row
    strip = quarter * feat_row // LANES
    spread = 4
    size = tok // n_grp // spread
    shape = jax.ShapeDtypeStruct

    at = jnp.stack([grp, row % spread, row % per, col, row // per]).astype(jnp.int32)
    offsets = sample_rows - col * tok
    own = lax.dynamic_slice_in_dim(offsets, grp * quarter, quarter, 0)

    payload = call(
        first_kernel,
        (at, own, tokens_in, act_inverse),
        [shape((n_row, out_rows + strip, tok), BF)],
        2 * feat_grp * feat_row * tok,
    )[0]
    first = lax.all_to_all(payload, "row", 0, 0)

    def along_y(block, k):
        return lax.ppermute(
            block, "col", [(i, i - i % 4 + (i + k) % 4) for i in range(n_col)]
        )

    picked = call(
        pick_kernel,
        (at, offsets, cotangent),
        [shape((n_grp * size + samp, feat_grp), BF)],
        2 * 64 * tok * feat_grp,
    )[0]
    beside = lax.ppermute(picked, "col", [(i, (i + 4) % n_col) for i in range(n_col)])
    cut = n_grp * size
    pair = jnp.concatenate([picked[:cut], beside[:cut]], axis=0)
    pairs = [pair] + [along_y(pair, k) for k in range(1, 4)]
    keep, give = call(
        right_kernel,
        (at, grad_inverse, *pairs),
        [shape((2 * n_col * size, width), BF)] * 2,
        2 * n_col * n_grp * size * feat_grp * width,
        [pltpu.VMEM((n_col, n_grp, size, width), F32)],
    )
    taken = lax.ppermute(give, "grp", [(i, i ^ 1) for i in range(n_grp)])
    halves = keep.astype(F32) + taken.astype(F32)
    half = n_col * size
    taken = lax.ppermute(halves[half:].astype(BF), "grp", [(i, i ^ 2) for i in range(n_grp)])
    right = (halves[:half] + taken.astype(F32)).astype(BF)

    keep, picked_y, beside_y = lax.optimization_barrier((keep, picked[cut:], beside[cut:]))
    samples = jnp.concatenate([picked_y, beside_y], axis=0)
    samples = [samples] + [along_y(samples, k) for k in range(1, 4)]
    side = call(
        side_kernel,
        (at, own, tokens_in, picked),
        [shape((n_col, samp, LANES), BF)],
        2 * samp * tok * feat_row,
    )[0]
    send = call(
        second_kernel,
        (first, side),
        [shape((n_grp, n_col, size * spread + strip * n_row // n_grp + samp, LANES), BF)],
        1000000,
    )[0]
    got = lax.all_to_all(send.reshape((n_grp * n_col,) + send.shape[2:]), ("grp", "col"), 0, 0)
    got = got.reshape(send.shape)
    rights = [right] + [
        lax.ppermute(
            right, "row", [(i, i - i % spread + (i + j) % spread) for i in range(n_row)]
        )
        for j in range(1, spread)
    ]

    term = call(
        final_kernel,
        (at, got, *rights),
        [shape((n_grp, out_rows, width), BF)],
        2 * n_grp * LANES * n_col * spread * size * width,
        [pltpu.VMEM((n_col, spread, size, width), F32)],
    )[0]
    term, got, samples = lax.optimization_barrier((term, got, samples))
    term = lax.all_to_all(term, "grp", 0, 0)
    precond = jnp.sum(term.astype(F32), axis=0)
    act_cov, grad_cov = call(
        factor_kernel,
        (at, got, *samples),
        [shape((tile, feat_grp), F32)] * 2,
        4 * LANES * samp * n_col * feat_grp,
    )
    return (precond, act_cov, grad_cov)


def solution(mesh):
    return jax.shard_map(
        body,
        mesh=mesh,
        in_specs=(P("col", "row"), P("col", "grp"), P("col"), P("grp", "row"), P("grp", "col")),
        out_specs=(P(("grp", "row"), "col"), P(("row", "col"), "grp"), P(("row", "col"), "grp")),
        check_vma=False,
    )
```

```python
import functools

import jax
import jax.numpy as jnp
from jax import lax
from jax.experimental import pallas as pl
from jax.experimental.pallas import tpu as pltpu
from jax.sharding import PartitionSpec as P

BF = jnp.bfloat16
F32 = jnp.float32
LANES = 128
FIRST = (((0,), (0,)), ((), ()))
LAST = (((1,), (1,)), ((), ()))
SMEM = pl.BlockSpec(memory_space=pltpu.SMEM)
VMEM = pl.BlockSpec(memory_space=pltpu.VMEM)


def call(kernel, inputs, outs, flops, scratch=()):
    moved = sum(x.size * x.dtype.itemsize for x in list(inputs) + list(outs))
    return pl.pallas_call(
        kernel,
        out_shape=outs,
        in_specs=[SMEM if x.dtype == jnp.int32 else VMEM for x in inputs],
        out_specs=[VMEM] * len(outs),
        scratch_shapes=list(scratch),
        compiler_params=pltpu.CompilerParams(vmem_limit_bytes=40 * 1024 * 1024),
        cost_estimate=pl.CostEstimate(flops=flops, bytes_accessed=moved, transcendentals=0),
    )(*inputs)


def source_of(col, k):
    return 4 * ((col // 4) ^ (k % 2)) + lax.rem(col % 4 - k // 2 + 4, 4)


def rows_hot(targets, tok):
    shape = (len(targets), tok)
    sub = lax.broadcasted_iota(jnp.int32, shape, 0)
    lane = lax.broadcasted_iota(jnp.int32, shape, 1)
    want = jnp.zeros(shape, jnp.int32)
    for i, target in enumerate(targets):
        want = jnp.where(sub == i, target, want)
    return jnp.where(want == lane, 1.0, 0.0).astype(BF)


def first_kernel(at, picks, x_ref, a_ref, out_ref):
    n_row, unused, tok = out_ref.shape
    part = lax.dot_general(a_ref[...], x_ref[...], LAST, preferred_element_type=F32)
    out_rows = part.shape[0] // n_row
    out_ref[:, :out_rows, :] = part.astype(BF).reshape(n_row, out_rows, tok)
    quarter = picks.shape[0]
    hot = rows_hot([picks[i] for i in range(quarter)], tok)
    chosen = jnp.dot(hot, x_ref[...], preferred_element_type=F32)
    strips = [chosen[:, k : k + LANES] for k in range(0, chosen.shape[1], LANES)]
    block = jnp.concatenate(strips, axis=0).astype(BF)
    out_ref[:, out_rows:, :] = jnp.broadcast_to(block[None], (n_row,) + block.shape)


def pick_kernel(at, picks, g_ref, out_ref):
    tok = g_ref.shape[0]
    samp = picks.shape[0]
    ours = [64 * (i // 16) + 16 * at[1] + i % 16 for i in range(out_ref.shape[0] - samp)]
    hot = rows_hot(ours + [picks[i] for i in range(samp)], tok)
    out_ref[...] = jnp.dot(hot, g_ref[...], preferred_element_type=F32).astype(BF)


def side_kernel(at, picks, x_ref, gy_ref, out_ref):
    n_col, samp, unused = out_ref.shape
    tok, feat = x_ref.shape
    tile = feat // n_col
    quarter = picks.shape[0]
    hot = rows_hot([picks[i] for i in range(quarter)], tok)
    chosen = jnp.dot(hot, x_ref[...], preferred_element_type=F32)
    begin = pl.multiple_of(at[2] * feat, LANES)
    own = gy_ref[gy_ref.shape[0] - samp :, pl.ds(begin, feat)].astype(F32)
    chosen = jnp.concatenate([chosen, jnp.zeros((samp - quarter, feat), F32)], axis=0)
    empty = jnp.zeros((samp, LANES - 2 * tile), F32)
    for c in range(n_col):
        span = slice(c * tile, (c + 1) * tile)
        out_ref[c] = jnp.concatenate([own[:, span], chosen[:, span], empty], axis=1).astype(BF)


def right_kernel(at, b_ref, *refs):
    blocks, keep_ref, give_ref, held = refs[:-3], refs[-3], refs[-2], refs[-1]
    n_blk, unused, size, width = held.shape
    rows = jnp.concatenate([block[...] for block in blocks], axis=0)
    term = jnp.dot(rows, b_ref[...], preferred_element_type=F32)
    held[...] = term.reshape(held.shape)
    core = at[0] % 2
    keep_ref[...] = held[:, core].reshape(n_blk * size, width).astype(BF)
    give_ref[...] = held[:, 1 - core].reshape(n_blk * size, width).astype(BF)


def second_kernel(got_ref, side_ref, out_ref):
    n_grp, n_col, unused, unused = out_ref.shape
    n_row, depth, tok = got_ref.shape
    strip = depth - (depth // 32) * 32
    out_rows = depth - strip
    total = got_ref[0, :out_rows, :].astype(F32)
    for r in range(1, n_row):
        total = total + got_ref[r, :out_rows, :].astype(F32)
    total = jnp.concatenate([total, jnp.zeros((LANES - out_rows, tok), F32)], axis=0)
    turned = jnp.transpose(total).astype(BF)
    size = tok // 2
    per = n_row // n_grp
    x_rows = per * strip
    for g in range(n_grp):
        u_block = turned[(g % 2) * size : (g % 2 + 1) * size]
        x_block = got_ref[g * per : (g + 1) * per, out_rows:, :].astype(F32)
        x_block = x_block.reshape(x_rows, tok).astype(BF)
        for c in range(n_col):
            out_ref[g, c, :size, :] = u_block
            out_ref[g, c, size : size + x_rows, :] = x_block
            out_ref[g, c, size + x_rows :, :] = side_ref[c]


def final_kernel(at, got_ref, *refs):
    v_refs, out_ref, held = refs[:-2], refs[-2], refs[-1]
    n_col, spread, size, width = held.shape
    n_grp, out_rows, unused = out_ref.shape
    for j in range(spread):
        plane = lax.rem(at[1] - j + spread, spread)
        block = v_refs[j][...].astype(F32)
        for k in range(n_col):
            held[source_of(at[3], k), plane] = block[k * size : (k + 1) * size]
    tokens = n_col * spread * size
    right = held[...].reshape(tokens, width).astype(BF)
    for g in range(n_grp):
        left = got_ref[g, :, : spread * size, :].reshape(tokens, LANES)
        term = lax.dot_general(left, right, FIRST, preferred_element_type=F32)
        out_ref[g] = term[:out_rows].astype(BF)


def factor_kernel(at, got_ref, *refs):
    blocks, act_ref, grad_ref = refs[:-2], refs[-2], refs[-1]
    n_grp, n_col, depth, unused = got_ref.shape
    tile, width = act_ref.shape
    samp = blocks[0].shape[0] // 2
    quarter = samp // n_grp
    total = samp * n_col
    scale = 1.0 / total
    side = depth - samp
    begin = side - quarter * (width // LANES)
    left = got_ref[:, :, side : side + 16, :].astype(F32)[:, :, :quarter, :]
    left = left.reshape(total, LANES).astype(BF)
    span = got_ref[:, :, begin:side, :].astype(F32)
    for t in range(width // LANES):
        strip = span[:, :, t * quarter : (t + 1) * quarter, :].reshape(total, LANES).astype(BF)
        term = lax.dot_general(left, strip, FIRST, preferred_element_type=F32)
        act_ref[:, t * LANES : (t + 1) * LANES] = term[tile : 2 * tile] * scale
    lefts, rights = [], []
    for k in range(n_col):
        lefts.append(got_ref[at[4], source_of(at[3], k), side:, :])
    for block in blocks:
        rights.append(block[...])
    left = jnp.concatenate(lefts, axis=0)
    right = jnp.concatenate(rights, axis=0)
    grad_ref[...] = lax.dot_general(left, right, FIRST, preferred_element_type=F32)[:tile] * scale


def body(tokens_in, cotangent, sample_rows, act_inverse, grad_inverse):
    n_row = lax.axis_size("row")
    n_col = lax.axis_size("col")
    n_grp = lax.axis_size("grp")
    grp = lax.axis_index("grp")
    row = lax.axis_index("row")
    col = lax.axis_index("col")
    tok, feat_row = tokens_in.shape
    feat_grp = cotangent.shape[1]
    width = grad_inverse.shape[1]
    samp = sample_rows.shape[0]
    quarter = samp // n_grp
    tile = feat_row // n_col
    out_rows = feat_grp // n_row
    per = feat_grp // feat_row
    strip = quarter * feat_row // LANES
    spread = 4
    size = tok // 2 // spread
    shape = jax.ShapeDtypeStruct

    at = jnp.stack([grp, row % spread, row % per, col, row // per]).astype(jnp.int32)
    offsets = sample_rows - col * tok
    own = lax.dynamic_slice_in_dim(offsets, grp * quarter, quarter, 0)

    payload = call(
        first_kernel,
        (at, own, tokens_in, act_inverse),
        [shape((n_row, out_rows + strip, tok), BF)],
        2 * feat_grp * feat_row * tok,
    )[0]
    first = lax.all_to_all(payload, "row", 0, 0)

    def along_y(block, k):
        return lax.ppermute(
            block, "col", [(i, i - i % 4 + (i + k) % 4) for i in range(n_col)]
        )

    picked = call(
        pick_kernel,
        (at, offsets, cotangent),
        [shape((2 * size + samp, feat_grp), BF)],
        2 * 64 * tok * feat_grp,
    )[0]
    beside = lax.ppermute(picked, "col", [(i, (i + 4) % n_col) for i in range(n_col)])
    cut = 2 * size
    pair = jnp.concatenate([picked[:cut], beside[:cut]], axis=0)
    pairs = [pair] + [along_y(pair, k) for k in range(1, 4)]
    keep, give = call(
        right_kernel,
        (at, grad_inverse, *pairs),
        [shape((n_col * size, width), BF)] * 2,
        4 * n_col * size * feat_grp * width,
        [pltpu.VMEM((n_col, 2, size, width), F32)],
    )
    taken = lax.ppermute(give, "grp", [(i, i ^ 1) for i in range(n_grp)])
    right = (keep.astype(F32) + taken.astype(F32)).astype(BF)
    rights = [right] + [
        lax.ppermute(
            right, "row", [(i, i - i % spread + (i + j) % spread) for i in range(n_row)]
        )
        for j in range(1, spread)
    ]
    rights, picked_y, beside_y = lax.optimization_barrier((rights, picked[cut:], beside[cut:]))
    samples = jnp.concatenate([picked_y, beside_y], axis=0)
    samples = [samples] + [along_y(samples, k) for k in range(1, 4)]
    side = call(
        side_kernel,
        (at, own, tokens_in, picked),
        [shape((n_col, samp, LANES), BF)],
        2 * samp * tok * feat_row,
    )[0]
    send = call(
        second_kernel,
        (first, side),
        [shape((n_grp, n_col, size * spread + strip * n_row // n_grp + samp, LANES), BF)],
        1000000,
    )[0]
    got = lax.all_to_all(send.reshape((n_grp * n_col,) + send.shape[2:]), ("grp", "col"), 0, 0)
    got = got.reshape(send.shape)

    term = call(
        final_kernel,
        (at, got, *rights),
        [shape((n_grp, out_rows, width), BF)],
        2 * n_grp * LANES * n_col * spread * size * width,
        [pltpu.VMEM((n_col, spread, size, width), F32)],
    )[0]
    term, got, samples = lax.optimization_barrier((term, got, samples))
    term = lax.all_to_all(term, "grp", 0, 0)
    precond = jnp.sum(term.astype(F32), axis=0)
    act_cov, grad_cov = call(
        factor_kernel,
        (at, got, *samples),
        [shape((tile, feat_grp), F32)] * 2,
        4 * LANES * samp * n_col * feat_grp,
    )
    return (precond, act_cov, grad_cov)


def solution(mesh):
    return jax.shard_map(
        body,
        mesh=mesh,
        in_specs=(P("col", "row"), P("col", "grp"), P("col"), P("grp", "row"), P("grp", "col")),
        out_specs=(P(("grp", "row"), "col"), P(("row", "col"), "grp"), P(("row", "col"), "grp")),
        check_vma=False,
    )
```

```python
import functools

import jax
import jax.numpy as jnp
from jax import lax
from jax.experimental import pallas as pl
from jax.experimental.pallas import tpu as pltpu
from jax.sharding import PartitionSpec as P

BF = jnp.bfloat16
F32 = jnp.float32
LANES = 128
FIRST = (((0,), (0,)), ((), ()))
LAST = (((1,), (1,)), ((), ()))
SMEM = pl.BlockSpec(memory_space=pltpu.SMEM)
VMEM = pl.BlockSpec(memory_space=pltpu.VMEM)


def call(kernel, inputs, outs, flops, scratch=()):
    moved = sum(x.size * x.dtype.itemsize for x in list(inputs) + list(outs))
    return pl.pallas_call(
        kernel,
        out_shape=outs,
        in_specs=[SMEM if x.dtype == jnp.int32 else VMEM for x in inputs],
        out_specs=[VMEM] * len(outs),
        scratch_shapes=list(scratch),
        compiler_params=pltpu.CompilerParams(vmem_limit_bytes=40 * 1024 * 1024),
        cost_estimate=pl.CostEstimate(flops=flops, bytes_accessed=moved, transcendentals=0),
    )(*inputs)


def source_of(col, k):
    return 4 * ((col // 4) ^ (k % 2)) + lax.rem(col % 4 - k // 2 + 4, 4)


def rows_hot(targets, tok):
    shape = (len(targets), tok)
    sub = lax.broadcasted_iota(jnp.int32, shape, 0)
    lane = lax.broadcasted_iota(jnp.int32, shape, 1)
    want = jnp.zeros(shape, jnp.int32)
    for i, target in enumerate(targets):
        want = jnp.where(sub == i, target, want)
    return jnp.where(want == lane, 1.0, 0.0).astype(BF)


def first_kernel(at, picks, x_ref, a_ref, out_ref):
    n_row, unused, tok = out_ref.shape
    part = lax.dot_general(a_ref[...], x_ref[...], LAST, preferred_element_type=F32)
    out_rows = part.shape[0] // n_row
    out_ref[:, :out_rows, :] = part.astype(BF).reshape(n_row, out_rows, tok)
    quarter = picks.shape[0]
    hot = rows_hot([picks[i] for i in range(quarter)], tok)
    chosen = jnp.dot(hot, x_ref[...], preferred_element_type=F32)
    strips = [chosen[:, k : k + LANES] for k in range(0, chosen.shape[1], LANES)]
    block = jnp.concatenate(strips, axis=0).astype(BF)
    out_ref[:, out_rows:, :] = jnp.broadcast_to(block[None], (n_row,) + block.shape)


def pick_kernel(at, picks, g_ref, out_ref):
    tok = g_ref.shape[0]
    samp = picks.shape[0]
    ours = [64 * (i // 16) + 16 * at[1] + i % 16 for i in range(out_ref.shape[0] - samp)]
    hot = rows_hot(ours + [picks[i] for i in range(samp)], tok)
    out_ref[...] = jnp.dot(hot, g_ref[...], preferred_element_type=F32).astype(BF)


def side_kernel(at, picks, x_ref, gy_ref, out_ref):
    n_col, samp, unused = out_ref.shape
    tok, feat = x_ref.shape
    tile = feat // n_col
    quarter = picks.shape[0]
    hot = rows_hot([picks[i] for i in range(quarter)], tok)
    chosen = jnp.dot(hot, x_ref[...], preferred_element_type=F32)
    begin = pl.multiple_of(at[2] * feat, LANES)
    own = gy_ref[gy_ref.shape[0] - samp :, pl.ds(begin, feat)].astype(F32)
    chosen = jnp.concatenate([chosen, jnp.zeros((samp - quarter, feat), F32)], axis=0)
    empty = jnp.zeros((samp, LANES - 2 * tile), F32)
    for c in range(n_col):
        span = slice(c * tile, (c + 1) * tile)
        out_ref[c] = jnp.concatenate([own[:, span], chosen[:, span], empty], axis=1).astype(BF)


def right_kernel(at, b_ref, *refs):
    blocks, keep_ref, give_ref, held = refs[:-3], refs[-3], refs[-2], refs[-1]
    n_blk, unused, size, width = held.shape
    rows = jnp.concatenate([block[...] for block in blocks], axis=0)
    term = jnp.dot(rows, b_ref[...], preferred_element_type=F32)
    held[...] = term.reshape(held.shape)
    core = at[0] % 2
    keep_ref[...] = held[:, core].reshape(n_blk * size, width).astype(BF)
    give_ref[...] = held[:, 1 - core].reshape(n_blk * size, width).astype(BF)


def second_kernel(got_ref, side_ref, out_ref):
    n_grp, n_col, unused, unused = out_ref.shape
    n_row, depth, tok = got_ref.shape
    strip = depth - (depth // 32) * 32
    out_rows = depth - strip
    total = got_ref[0, :out_rows, :].astype(F32)
    for r in range(1, n_row):
        total = total + got_ref[r, :out_rows, :].astype(F32)
    total = jnp.concatenate([total, jnp.zeros((LANES - out_rows, tok), F32)], axis=0)
    turned = jnp.transpose(total).astype(BF)
    size = tok // 2
    per = n_row // n_grp
    x_rows = per * strip
    for g in range(n_grp):
        u_block = turned[(g % 2) * size : (g % 2 + 1) * size]
        x_block = got_ref[g * per : (g + 1) * per, out_rows:, :].astype(F32)
        x_block = x_block.reshape(x_rows, tok).astype(BF)
        for c in range(n_col):
            out_ref[g, c, :size, :] = u_block
            out_ref[g, c, size : size + x_rows, :] = x_block
            out_ref[g, c, size + x_rows :, :] = side_ref[c]


def final_kernel(at, got_ref, *refs):
    v_refs, out_ref, held = refs[:-2], refs[-2], refs[-1]
    n_col, spread, size, width = held.shape
    n_grp, out_rows, unused = out_ref.shape
    for j in range(spread):
        plane = lax.rem(at[1] - j + spread, spread)
        block = v_refs[j][...].astype(F32)
        for k in range(n_col):
            held[source_of(at[3], k), plane] = block[k * size : (k + 1) * size]
    tokens = n_col * spread * size
    right = held[...].reshape(tokens, width).astype(BF)
    for g in range(n_grp):
        left = got_ref[g, :, : spread * size, :].reshape(tokens, LANES)
        term = lax.dot_general(left, right, FIRST, preferred_element_type=F32)
        out_ref[g] = term[:out_rows].astype(BF)


def factor_kernel(at, got_ref, *refs):
    blocks, act_ref, grad_ref = refs[:-2], refs[-2], refs[-1]
    n_grp, n_col, depth, unused = got_ref.shape
    tile, width = act_ref.shape
    samp = blocks[0].shape[0] // 2
    quarter = samp // n_grp
    total = samp * n_col
    scale = 1.0 / total
    side = depth - samp
    begin = side - quarter * (width // LANES)
    left = got_ref[:, :, side : side + 16, :].astype(F32)[:, :, :quarter, :]
    left = left.reshape(total, LANES).astype(BF)
    span = got_ref[:, :, begin:side, :].astype(F32)
    for t in range(width // LANES):
        strip = span[:, :, t * quarter : (t + 1) * quarter, :].reshape(total, LANES).astype(BF)
        term = lax.dot_general(left, strip, FIRST, preferred_element_type=F32)
        act_ref[:, t * LANES : (t + 1) * LANES] = term[tile : 2 * tile] * scale
    lefts, rights = [], []
    for k in range(n_col):
        lefts.append(got_ref[at[4], source_of(at[3], k), side:, :])
    for block in blocks:
        rights.append(block[...])
    left = jnp.concatenate(lefts, axis=0)
    right = jnp.concatenate(rights, axis=0)
    grad_ref[...] = lax.dot_general(left, right, FIRST, preferred_element_type=F32)[:tile] * scale


def body(tokens_in, cotangent, sample_rows, act_inverse, grad_inverse):
    n_row = lax.axis_size("row")
    n_col = lax.axis_size("col")
    n_grp = lax.axis_size("grp")
    grp = lax.axis_index("grp")
    row = lax.axis_index("row")
    col = lax.axis_index("col")
    tok, feat_row = tokens_in.shape
    feat_grp = cotangent.shape[1]
    width = grad_inverse.shape[1]
    samp = sample_rows.shape[0]
    quarter = samp // n_grp
    tile = feat_row // n_col
    out_rows = feat_grp // n_row
    per = feat_grp // feat_row
    strip = quarter * feat_row // LANES
    spread = 4
    size = tok // 2 // spread
    shape = jax.ShapeDtypeStruct

    at = jnp.stack([grp, row % spread, row % per, col, row // per]).astype(jnp.int32)
    offsets = sample_rows - col * tok
    own = lax.dynamic_slice_in_dim(offsets, grp * quarter, quarter, 0)

    payload = call(
        first_kernel,
        (at, own, tokens_in, act_inverse),
        [shape((n_row, out_rows + strip, tok), BF)],
        2 * feat_grp * feat_row * tok,
    )[0]
    first = lax.all_to_all(payload, "row", 0, 0)

    def along_y(block, k):
        return lax.ppermute(
            block, "col", [(i, i - i % 4 + (i + k) % 4) for i in range(n_col)]
        )

    picked = call(
        pick_kernel,
        (at, offsets, cotangent),
        [shape((2 * size + samp, feat_grp), BF)],
        2 * 64 * tok * feat_grp,
    )[0]
    beside = lax.ppermute(picked, "col", [(i, (i + 4) % n_col) for i in range(n_col)])
    cut = 2 * size
    pair = jnp.concatenate([picked[:cut], beside[:cut]], axis=0)
    pairs = [pair] + [along_y(pair, k) for k in range(1, 4)]
    keep, give = call(
        right_kernel,
        (at, grad_inverse, *pairs),
        [shape((n_col * size, width), BF)] * 2,
        4 * n_col * size * feat_grp * width,
        [pltpu.VMEM((n_col, 2, size, width), F32)],
    )
    first, unused = lax.optimization_barrier((first, give))
    taken = lax.ppermute(give, "grp", [(i, i ^ 1) for i in range(n_grp)])
    right = (keep.astype(F32) + taken.astype(F32)).astype(BF)
    rights = [right] + [
        lax.ppermute(
            right, "row", [(i, i - i % spread + (i + j) % spread) for i in range(n_row)]
        )
        for j in range(1, spread)
    ]
    rights, picked_y, beside_y = lax.optimization_barrier((rights, picked[cut:], beside[cut:]))
    samples = jnp.concatenate([picked_y, beside_y], axis=0)
    samples = [samples] + [along_y(samples, k) for k in range(1, 4)]
    side = call(
        side_kernel,
        (at, own, tokens_in, picked),
        [shape((n_col, samp, LANES), BF)],
        2 * samp * tok * feat_row,
    )[0]
    send = call(
        second_kernel,
        (first, side),
        [shape((n_grp, n_col, size * spread + strip * n_row // n_grp + samp, LANES), BF)],
        1000000,
    )[0]
    got = lax.all_to_all(send.reshape((n_grp * n_col,) + send.shape[2:]), ("grp", "col"), 0, 0)
    got = got.reshape(send.shape)

    term = call(
        final_kernel,
        (at, got, *rights),
        [shape((n_grp, out_rows, width), BF)],
        2 * n_grp * LANES * n_col * spread * size * width,
        [pltpu.VMEM((n_col, spread, size, width), F32)],
    )[0]
    got, unused = lax.optimization_barrier((got, term))
    term = lax.all_to_all(term, "grp", 0, 0)
    precond = jnp.sum(term.astype(F32), axis=0)
    act_cov, grad_cov = call(
        factor_kernel,
        (at, got, *samples),
        [shape((tile, feat_grp), F32)] * 2,
        4 * LANES * samp * n_col * feat_grp,
    )
    return (precond, act_cov, grad_cov)


def solution(mesh):
    return jax.shard_map(
        body,
        mesh=mesh,
        in_specs=(P("col", "row"), P("col", "grp"), P("col"), P("grp", "row"), P("grp", "col")),
        out_specs=(P(("grp", "row"), "col"), P(("row", "col"), "grp"), P(("row", "col"), "grp")),
        check_vma=False,
    )
```

```python
import functools

import jax
import jax.numpy as jnp
from jax import lax
from jax.experimental import pallas as pl
from jax.experimental.pallas import tpu as pltpu
from jax.sharding import PartitionSpec as P

BF = jnp.bfloat16
F32 = jnp.float32
LANES = 128
FIRST = (((0,), (0,)), ((), ()))
LAST = (((1,), (1,)), ((), ()))
SMEM = pl.BlockSpec(memory_space=pltpu.SMEM)
VMEM = pl.BlockSpec(memory_space=pltpu.VMEM)
SHIFTS = (0, 2, 1, -1)


def call(kernel, inputs, outs, flops, scratch=(), place=VMEM):
    moved = sum(x.size * x.dtype.itemsize for x in list(inputs) + list(outs))
    return pl.pallas_call(
        kernel,
        out_shape=outs,
        in_specs=[SMEM if x.dtype == jnp.int32 else place for x in inputs],
        out_specs=[VMEM] * len(outs),
        scratch_shapes=list(scratch),
        compiler_params=pltpu.CompilerParams(vmem_limit_bytes=40 * 1024 * 1024),
        cost_estimate=pl.CostEstimate(flops=flops, bytes_accessed=moved, transcendentals=0),
    )(*inputs)


def source_of(k):
    col = lax.axis_index("col")
    return 4 * ((col // 4) ^ (k % 2)) + lax.rem(col % 4 - k // 2 + 4, 4)


def own_picks(picks, count, tok):
    begin = lax.axis_index("grp") * count
    first = lax.axis_index("col") * tok
    return [picks[begin + i] - first for i in range(count)]


def rows_hot(targets, tok):
    shape = (len(targets), tok)
    sub = lax.broadcasted_iota(jnp.int32, shape, 0)
    lane = lax.broadcasted_iota(jnp.int32, shape, 1)
    want = jnp.zeros(shape, jnp.int32)
    for i, target in enumerate(targets):
        want = jnp.where(sub == i, target, want)
    return jnp.where(want == lane, 1.0, 0.0).astype(BF)


def first_kernel(picks, x_hbm, a_hbm, out_ref, x_ref, a_ref, sems):
    n_row, depth, tok = out_ref.shape
    parts = sems.shape[0] - 1
    step = a_ref.shape[0] // parts
    copies = [pltpu.make_async_copy(x_hbm, x_ref, sems.at[parts])]
    for p in range(parts):
        span = pl.ds(p * step, step)
        copies.append(pltpu.make_async_copy(a_hbm.at[span], a_ref.at[span], sems.at[p]))
    for copy in copies:
        copy.start()
    out_rows = a_ref.shape[0] // n_row
    quarter = picks.shape[0] // 4
    hot = rows_hot(own_picks(picks, quarter, tok), tok)
    copies[0].wait()
    chosen = jnp.dot(hot, x_ref[...], preferred_element_type=F32)
    strips = [chosen[:, k : k + LANES] for k in range(0, chosen.shape[1], LANES)]
    block = jnp.concatenate(strips, axis=0).astype(BF)
    out_ref[:, out_rows:, :] = jnp.broadcast_to(block[None], (n_row,) + block.shape)
    each = step // out_rows
    for p in range(parts):
        copies[p + 1].wait()
        rows = a_ref[p * step : (p + 1) * step, :]
        part = lax.dot_general(rows, x_ref[...], LAST, preferred_element_type=F32)
        out_ref[p * each : (p + 1) * each, :out_rows, :] = part.astype(BF).reshape(
            each, out_rows, tok
        )


def pick_kernel(picks, g_ref, out_ref):
    tok = g_ref.shape[0]
    samp = picks.shape[0]
    plane = lax.axis_index("row") % 4
    first = lax.axis_index("col") * tok
    count = out_ref.shape[0] - samp
    ours = [64 * (i // 16) + 16 * plane + i % 16 for i in range(count)]
    hot = rows_hot(ours + [picks[i] - first for i in range(samp)], tok)
    out_ref[...] = jnp.dot(hot, g_ref[...], preferred_element_type=F32).astype(BF)


def side_kernel(picks, x_ref, gy_ref, out_ref):
    n_col, depth, unused = out_ref.shape
    tok, feat = x_ref.shape
    samp = picks.shape[0]
    tile = feat // n_col
    quarter = samp // 4
    hot = rows_hot(own_picks(picks, quarter, tok), tok)
    chosen = jnp.dot(hot, x_ref[...], preferred_element_type=F32)
    begin = pl.multiple_of((lax.axis_index("row") % 4) * feat, LANES)
    own = gy_ref[gy_ref.shape[0] - samp :, pl.ds(begin, feat)].astype(F32)
    empty = jnp.zeros((samp - 3 * quarter, 16), F32)
    for c in range(n_col):
        at = c * tile
        top = own[:, at : at + 32]
        cuts = [chosen[:, at + k : at + k + 16] for k in range(0, tile, 16)]
        low = jnp.concatenate(
            [own[:, at + 32 : at + tile], jnp.concatenate(cuts + [empty], axis=0)], axis=1
        )
        block = jnp.concatenate([top, low], axis=0)
        block = jnp.concatenate([jnp.zeros((depth, LANES - 32), F32), block], axis=1)
        out_ref[c] = block.astype(BF)


def right_kernel(b_ref, *refs):
    blocks, keep_ref, give_ref, held = refs[:-3], refs[-3], refs[-2], refs[-1]
    n_blk, unused, size, width = held.shape
    rows = jnp.concatenate([block[...] for block in blocks], axis=0)
    term = jnp.dot(rows, b_ref[...], preferred_element_type=F32)
    held[...] = term.reshape(held.shape)
    core = lax.axis_index("grp") % 2
    keep_ref[...] = held[:, core].reshape(n_blk * size, width).astype(BF)
    give_ref[...] = held[:, 1 - core].reshape(n_blk * size, width).astype(BF)


def second_kernel(got_ref, side_ref, out_ref):
    n_grp, n_col, unused, unused = out_ref.shape
    n_row, depth, tok = got_ref.shape
    strip = depth - (depth // 32) * 32
    out_rows = depth - strip
    total = got_ref[0, :out_rows, :].astype(F32)
    for r in range(1, n_row):
        total = total + got_ref[r, :out_rows, :].astype(F32)
    total = jnp.concatenate([total, jnp.zeros((LANES - out_rows, tok), F32)], axis=0)
    turned = jnp.transpose(total).astype(BF)
    size = tok // 2
    per = n_row // n_grp
    x_rows = per * strip
    for g in range(n_grp):
        u_block = turned[(g % 2) * size : (g % 2 + 1) * size]
        x_block = got_ref[g * per : (g + 1) * per, out_rows:, :].astype(F32)
        x_block = x_block.reshape(x_rows, tok).astype(BF)
        for c in range(n_col):
            out_ref[g, c, :size, :] = u_block + side_ref[c]
            out_ref[g, c, size:, :] = x_block


def final_kernel(got_ref, *refs):
    v_refs, out_ref, held = refs[:-2], refs[-2], refs[-1]
    n_col, spread, size, width = held.shape
    n_grp, out_rows, unused = out_ref.shape
    row = lax.axis_index("row")
    for j, shift in enumerate(SHIFTS):
        plane = lax.rem(row - shift + spread, spread)
        block = v_refs[j][...].astype(F32)
        for k in range(n_col):
            held[source_of(k), plane] = block[k * size : (k + 1) * size]
    tokens = n_col * spread * size
    right = held[...].reshape(tokens, width).astype(BF)
    for g in range(n_grp):
        left = got_ref[g, :, : spread * size, :].reshape(tokens, LANES)
        term = lax.dot_general(left, right, FIRST, preferred_element_type=F32)
        out_ref[g] = term[:out_rows].astype(BF)


def factor_kernel(got_ref, *refs):
    blocks, act_ref, grad_ref = refs[:-2], refs[-2], refs[-1]
    n_grp, n_col, depth, unused = got_ref.shape
    tile, width = act_ref.shape
    samp = blocks[0].shape[0] // 2
    quarter = samp // n_grp
    total = samp * n_col
    scale = 1.0 / total
    begin = depth - quarter * (width // LANES)
    span = got_ref[:, :, begin:, :].astype(F32)
    strips = []
    for t in range(width // LANES):
        strip = span[:, :, t * quarter : (t + 1) * quarter, :].reshape(total, LANES)
        strips.append(strip.astype(BF))
    right = jnp.concatenate(strips, axis=1)
    lefts = got_ref[:, :, samp : 2 * samp, :].astype(F32)
    for k in range(tile // 16):
        left = lefts[:, :, k * quarter : (k + 1) * quarter, :].reshape(total, LANES).astype(BF)
        term = lax.dot_general(left, right, FIRST, preferred_element_type=F32)
        act_ref[16 * k : 16 * (k + 1), :] = term[LANES - 16 :] * scale
    owner = lax.axis_index("row") // 4
    sides = [got_ref[owner, source_of(k), : 2 * samp, :] for k in range(n_col)]
    right = jnp.concatenate([block[...] for block in blocks], axis=0)
    left = jnp.concatenate([side[:samp] for side in sides], axis=0)
    term = lax.dot_general(left, right, FIRST, preferred_element_type=F32)
    grad_ref[:32, :] = term[LANES - 32 :] * scale
    left = jnp.concatenate([side[samp:] for side in sides], axis=0)
    term = lax.dot_general(left, right, FIRST, preferred_element_type=F32)
    grad_ref[32:, :] = term[LANES - 32 : LANES - 16] * scale


def body(tokens_in, cotangent, sample_rows, act_inverse, grad_inverse):
    n_row = lax.axis_size("row")
    n_col = lax.axis_size("col")
    n_grp = lax.axis_size("grp")
    tok, feat_row = tokens_in.shape
    feat_grp = cotangent.shape[1]
    width = grad_inverse.shape[1]
    samp = sample_rows.shape[0]
    quarter = samp // n_grp
    tile = feat_row // n_col
    out_rows = feat_grp // n_row
    strip = quarter * feat_row // LANES
    spread = 4
    size = tok // 2 // spread
    shape = jax.ShapeDtypeStruct

    payload = call(
        first_kernel,
        (sample_rows, tokens_in, act_inverse),
        [shape((n_row, out_rows + strip, tok), BF)],
        2 * feat_grp * feat_row * tok,
        [
            pltpu.VMEM(tokens_in.shape, BF),
            pltpu.VMEM(act_inverse.shape, BF),
            pltpu.SemaphoreType.DMA((5,)),
        ],
        pl.BlockSpec(memory_space=pl.ANY),
    )[0]
    first = lax.all_to_all(payload, "row", 0, 0)

    def along_y(block, k):
        return lax.ppermute(
            block, "col", [(i, i - i % 4 + (i + k) % 4) for i in range(n_col)]
        )

    picked = call(
        pick_kernel,
        (sample_rows, cotangent),
        [shape((2 * size + samp, feat_grp), BF)],
        2 * 64 * tok * feat_grp,
    )[0]
    beside = lax.ppermute(picked, "col", [(i, (i + 4) % n_col) for i in range(n_col)])
    cut = 2 * size
    pair = jnp.concatenate([picked[:cut], beside[:cut]], axis=0)
    pairs = [pair] + [along_y(pair, k) for k in range(1, 4)]
    keep, give = call(
        right_kernel,
        (grad_inverse, *pairs),
        [shape((n_col * size, width), BF)] * 2,
        4 * n_col * size * feat_grp * width,
        [pltpu.VMEM((n_col, 2, size, width), F32)],
    )
    first, unused = lax.optimization_barrier((first, give))
    taken = lax.ppermute(give, "grp", [(i, i ^ 1) for i in range(n_grp)])
    right = (keep.astype(F32) + taken.astype(F32)).astype(BF)
    rights = [right] + [
        lax.ppermute(right, "row", [(i, (i + j) % n_row) for i in range(n_row)])
        for j in SHIFTS[1:]
    ]
    unused, picked_y, beside_y = lax.optimization_barrier(
        (rights[2], picked[cut:], beside[cut:])
    )
    samples = jnp.concatenate([picked_y, beside_y], axis=0)
    samples = [samples] + [along_y(samples, k) for k in range(1, 4)]
    side = call(
        side_kernel,
        (sample_rows, tokens_in, picked),
        [shape((n_col, 2 * samp, LANES), BF)],
        2 * samp * tok * feat_row,
    )[0]
    send = call(
        second_kernel,
        (first, side),
        [shape((n_grp, n_col, size * spread + strip * n_row // n_grp, LANES), BF)],
        1000000,
    )[0]
    got = lax.all_to_all(send.reshape((n_grp * n_col,) + send.shape[2:]), ("grp", "col"), 0, 0)
    got = got.reshape(send.shape)

    term = call(
        final_kernel,
        (got, *rights),
        [shape((n_grp, out_rows, width), BF)],
        2 * n_grp * LANES * n_col * spread * size * width,
        [pltpu.VMEM((n_col, spread, size, width), F32)],
    )[0]
    got, unused = lax.optimization_barrier((got, term))
    term = lax.all_to_all(term, "grp", 0, 0)
    precond = jnp.sum(term.astype(F32), axis=0)
    act_cov, grad_cov = call(
        factor_kernel,
        (got, *samples),
        [shape((tile, feat_grp), F32)] * 2,
        4 * LANES * samp * n_col * feat_grp,
    )
    return (precond, act_cov, grad_cov)


def solution(mesh):
    return jax.shard_map(
        body,
        mesh=mesh,
        in_specs=(P("col", "row"), P("col", "grp"), P("col"), P("grp", "row"), P("grp", "col")),
        out_specs=(P(("grp", "row"), "col"), P(("row", "col"), "grp"), P(("row", "col"), "grp")),
        check_vma=False,
    )
```

```python
import functools

import jax
import jax.numpy as jnp
from jax import lax
from jax.experimental import pallas as pl
from jax.experimental.pallas import tpu as pltpu
from jax.sharding import PartitionSpec as P

BF = jnp.bfloat16
F32 = jnp.float32
LANES = 128
FIRST = (((0,), (0,)), ((), ()))
LAST = (((1,), (1,)), ((), ()))
SMEM = pl.BlockSpec(memory_space=pltpu.SMEM)
VMEM = pl.BlockSpec(memory_space=pltpu.VMEM)
SHIFTS = (0, 2, 1, -1)


def call(kernel, inputs, outs, flops, scratch=(), place=VMEM, limit=40):
    moved = sum(x.size * x.dtype.itemsize for x in list(inputs) + list(outs))
    return pl.pallas_call(
        kernel,
        out_shape=outs,
        in_specs=[SMEM if x.dtype == jnp.int32 else place for x in inputs],
        out_specs=[VMEM] * len(outs),
        scratch_shapes=list(scratch),
        compiler_params=pltpu.CompilerParams(vmem_limit_bytes=limit * 1024 * 1024),
        cost_estimate=pl.CostEstimate(flops=flops, bytes_accessed=moved, transcendentals=0),
    )(*inputs)


def source_of(k):
    col = lax.axis_index("col")
    return 4 * ((col // 4) ^ (k % 2)) + lax.rem(col % 4 - k // 2 + 4, 4)


def own_picks(picks, count, tok):
    begin = lax.axis_index("grp") * count
    first = lax.axis_index("col") * tok
    return [picks[begin + i] - first for i in range(count)]


def rows_hot(targets, tok):
    shape = (len(targets), tok)
    sub = lax.broadcasted_iota(jnp.int32, shape, 0)
    lane = lax.broadcasted_iota(jnp.int32, shape, 1)
    want = jnp.zeros(shape, jnp.int32)
    for i, target in enumerate(targets):
        want = jnp.where(sub == i, target, want)
    return jnp.where(want == lane, 1.0, 0.0).astype(BF)


def first_kernel(picks, x_hbm, a_hbm, out_ref, x_ref, a_ref, sems):
    n_row, depth, tok = out_ref.shape
    parts = sems.shape[0] - 1
    step = a_ref.shape[0] // parts
    copies = [pltpu.make_async_copy(x_hbm, x_ref, sems.at[parts])]
    for p in range(parts):
        span = pl.ds(p * step, step)
        copies.append(pltpu.make_async_copy(a_hbm.at[span], a_ref.at[span], sems.at[p]))
    for copy in copies:
        copy.start()
    out_rows = a_ref.shape[0] // n_row
    quarter = picks.shape[0] // 4
    hot = rows_hot(own_picks(picks, quarter, tok), tok)
    copies[0].wait()
    chosen = jnp.dot(hot, x_ref[...], preferred_element_type=F32)
    strips = [chosen[:, k : k + LANES] for k in range(0, chosen.shape[1], LANES)]
    block = jnp.concatenate(strips, axis=0).astype(BF)
    out_ref[:, out_rows:, :] = jnp.broadcast_to(block[None], (n_row,) + block.shape)
    each = step // out_rows
    for p in range(parts):
        copies[p + 1].wait()
        rows = a_ref[p * step : (p + 1) * step, :]
        part = lax.dot_general(rows, x_ref[...], LAST, preferred_element_type=F32)
        out_ref[p * each : (p + 1) * each, :out_rows, :] = part.astype(BF).reshape(
            each, out_rows, tok
        )


def pick_kernel(picks, g_ref, out_ref):
    tok = g_ref.shape[0]
    samp = picks.shape[0]
    plane = lax.axis_index("row") % 4
    first = lax.axis_index("col") * tok
    count = out_ref.shape[0] - samp
    ours = [64 * (i // 16) + 16 * plane + i % 16 for i in range(count)]
    hot = rows_hot(ours + [picks[i] - first for i in range(samp)], tok)
    out_ref[...] = jnp.dot(hot, g_ref[...], preferred_element_type=F32).astype(BF)


def right_kernel(b_ref, gy_ref, *refs):
    blocks, keep_ref, give_ref, held = refs[:-3], refs[-3], refs[-2], refs[-1]
    n_blk, unused, size, width = held.shape
    rows = jnp.concatenate([block[...] for block in blocks], axis=0)
    term = jnp.dot(rows, b_ref[...], preferred_element_type=F32)
    held[...] = term.reshape(held.shape)
    core = lax.axis_index("grp") % 2
    cut = n_blk * size
    keep_ref[:cut, :] = held[:, core].reshape(cut, width)
    give_ref[:cut, :] = held[:, 1 - core].reshape(cut, width).astype(BF)
    feat = width // 2
    samp = 2 * (give_ref.shape[0] - cut)
    begin = pl.multiple_of((lax.axis_index("row") % 4) * feat, LANES)
    own = gy_ref[gy_ref.shape[0] - samp :, pl.ds(begin, feat)]
    own = jnp.concatenate([own[: samp // 2], own[samp // 2 :]], axis=1)
    keep_ref[cut:, :] = own.astype(F32)
    give_ref[cut:, :] = own


def gather_kernel(got_ref, u_ref, x_ref):
    n_grp, x_rows, unused = x_ref.shape
    n_row, depth, tok = got_ref.shape
    out_rows = u_ref.shape[0]
    total = got_ref[0, :out_rows, :].astype(F32)
    for r in range(1, n_row):
        total = total + got_ref[r, :out_rows, :].astype(F32)
    u_ref[...] = total.astype(BF)
    per = n_row // n_grp
    for g in range(n_grp):
        block = got_ref[g * per : (g + 1) * per, out_rows:, :].astype(F32)
        x_ref[g] = block.reshape(x_rows, tok).astype(BF)


def second_kernel(picks, u_ref, x_ref, y_ref, tokens_ref, out_ref):
    n_col, depth, unused = out_ref.shape
    out_rows, tok = u_ref.shape
    feat = tokens_ref.shape[1]
    samp = picks.shape[0]
    tile = feat // n_col
    begin = lax.axis_index("col") * tok
    hot = rows_hot([picks[i] - begin for i in range(samp)], tok)
    chosen = jnp.dot(hot, tokens_ref[...], preferred_element_type=F32)
    own = y_ref[...].astype(F32)
    own = jnp.concatenate([own[:, :feat], own[:, feat:]], axis=0)
    empty = jnp.zeros((samp, LANES - 2 * tile), F32)
    u_block = u_ref[...]
    x_block = x_ref[...].reshape(x_ref.shape[0] * x_ref.shape[1], LANES)
    for c in range(n_col):
        span = slice(c * tile, (c + 1) * tile)
        out_ref[c, :out_rows, :] = u_block
        out_ref[c, out_rows : depth - samp, :] = x_block
        side = jnp.concatenate([own[:, span], chosen[:, span], empty], axis=1)
        out_ref[c, depth - samp :, :] = side.astype(BF)


def final_kernel(got_ref, pair_ref, *refs):
    v_refs, out_ref, held = refs[:-2], refs[-2], refs[-1]
    n_col, unused, spread, size, width = held.shape
    out_rows = out_ref.shape[0]
    row = lax.axis_index("row")
    core = lax.axis_index("grp") % 2
    cut = n_col * size
    for j, shift in enumerate(SHIFTS):
        plane = lax.rem(row - shift + spread, spread)
        for k in range(n_col):
            span = slice(k * size, (k + 1) * size)
            held[source_of(k), core, plane] = v_refs[j][span, :]
            span = slice(j * cut + k * size, j * cut + (k + 1) * size)
            held[source_of(k), 1 - core, plane] = pair_ref[span, :]
    tokens = 2 * spread * size
    total = None
    for c in range(0, n_col, 2):
        left = jnp.concatenate([got_ref[c, :out_rows, :], got_ref[c + 1, :out_rows, :]], axis=1)
        right = held[c : c + 2].reshape(2 * tokens, width)
        term = jnp.dot(left, right, preferred_element_type=F32)
        total = term if total is None else total + term
    out_ref[...] = total


def factor_kernel(got_ref, *refs):
    blocks, act_ref, grad_ref = refs[:-2], refs[-2], refs[-1]
    n_col, depth, unused = got_ref.shape
    tile, width = act_ref.shape
    samp = blocks[0].shape[0] // 2
    quarter = samp // 4
    total = samp * n_col
    scale = 1.0 / total
    count = 4 * quarter * (width // LANES)
    span = got_ref[:, depth - samp - count : depth - samp, :].astype(F32)
    span = span.reshape(n_col, 4, count // 4, LANES)
    strips = []
    for t in range(width // LANES):
        strip = span[:, :, t * quarter : (t + 1) * quarter, :].reshape(total, LANES)
        strips.append(strip.astype(BF))
    right = jnp.concatenate(strips, axis=1)
    left = got_ref[:, depth - samp :, :].reshape(total, LANES)
    term = lax.dot_general(left, right, FIRST, preferred_element_type=F32)
    act_ref[...] = term[tile : 2 * tile] * scale
    sides = [got_ref[source_of(k), depth - samp :, :] for k in range(n_col)]
    left = jnp.concatenate(sides, axis=0)
    right = jnp.concatenate([block[...] for block in blocks], axis=0)
    term = lax.dot_general(left, right, FIRST, preferred_element_type=F32)
    grad_ref[...] = term[:tile] * scale


def body(tokens_in, cotangent, sample_rows, act_inverse, grad_inverse):
    n_row = lax.axis_size("row")
    n_col = lax.axis_size("col")
    n_grp = lax.axis_size("grp")
    tok, feat_row = tokens_in.shape
    feat_grp = cotangent.shape[1]
    width = grad_inverse.shape[1]
    samp = sample_rows.shape[0]
    quarter = samp // n_grp
    tile = feat_row // n_col
    out_rows = feat_grp // n_row
    strip = quarter * feat_row // LANES
    spread = 4
    size = tok // 2 // spread
    shape = jax.ShapeDtypeStruct

    picked = call(
        pick_kernel,
        (sample_rows, cotangent),
        [shape((2 * size + samp, feat_grp), BF)],
        2 * 64 * tok * feat_grp,
    )[0]
    beside = lax.ppermute(picked, "col", [(i, (i + 4) % n_col) for i in range(n_col)])
    picked, x_in = lax.optimization_barrier((picked, tokens_in))
    payload = call(
        first_kernel,
        (sample_rows, x_in, act_inverse),
        [shape((n_row, out_rows + strip, tok), BF)],
        2 * feat_grp * feat_row * tok,
        [
            pltpu.VMEM(tokens_in.shape, BF),
            pltpu.VMEM(act_inverse.shape, BF),
            pltpu.SemaphoreType.DMA((5,)),
        ],
        pl.BlockSpec(memory_space=pl.ANY),
        limit=56,
    )[0]
    first = lax.all_to_all(payload, "row", 0, 0)

    def along_y(block, k):
        return lax.ppermute(
            block, "col", [(i, i - i % 4 + (i + k) % 4) for i in range(n_col)]
        )

    cut = 2 * size
    pair = jnp.concatenate([picked[:cut], beside[:cut]], axis=0)
    pairs = [pair] + [along_y(pair, k) for k in range(1, 4)]
    half = n_col * size
    extra = samp // 2
    keep, give = call(
        right_kernel,
        (grad_inverse, picked, *pairs),
        [shape((half + extra, width), F32), shape((half + extra, width), BF)],
        4 * n_col * size * feat_grp * width,
        [pltpu.VMEM((n_col, 2, size, width), F32)],
    )
    first, unused = lax.optimization_barrier((first, give))

    owner = lax.axis_index("row") // 4
    grp = lax.axis_index("grp")
    taken = lax.ppermute(give, "grp", [(i, i ^ 1) for i in range(n_grp)]).astype(F32)
    own_y = jnp.where(grp % 2 == owner % 2, keep[half:], taken[half:])
    keep = jnp.concatenate([keep[:half] + taken[:half], own_y], axis=0)
    taken = lax.ppermute(keep.astype(BF), "grp", [(i, i ^ 2) for i in range(n_grp)]).astype(F32)
    own_y = jnp.where(grp // 2 == owner // 2, keep[half:], taken[half:]).astype(BF)
    right = (keep[:half] + taken[:half]).astype(BF)
    rights = [right] + [
        lax.ppermute(right, "row", [(i, (i + j) % n_row) for i in range(n_row)])
        for j in SHIFTS[1:]
    ]
    other = lax.ppermute(
        jnp.concatenate(rights, axis=0), "grp", [(i, i ^ 1) for i in range(n_grp)]
    )

    unused, picked_y, beside_y = lax.optimization_barrier((keep, picked[cut:], beside[cut:]))
    samples = jnp.concatenate([picked_y, beside_y], axis=0)
    samples = [samples] + [along_y(samples, k) for k in range(1, 4)]

    u_own, x_send = call(
        gather_kernel,
        (first,),
        [shape((out_rows, tok), BF), shape((n_grp, strip * n_row // n_grp, LANES), BF)],
        1000000,
    )
    x_got = lax.all_to_all(x_send, "grp", 0, 0)
    send = call(
        second_kernel,
        (sample_rows, u_own, x_got, own_y, tokens_in),
        [shape((n_col, out_rows + strip * n_row + samp, LANES), BF)],
        2 * samp * tok * feat_row,
    )[0]
    got = lax.all_to_all(send, "col", 0, 0)

    precond = call(
        final_kernel,
        (got, other, *rights),
        [shape((out_rows, width), F32)],
        2 * out_rows * n_col * tok * width,
        [pltpu.VMEM((n_col, 2, spread, size, width), BF)],
    )[0]
    act_cov, grad_cov = call(
        factor_kernel,
        (got, *samples),
        [shape((tile, feat_grp), F32)] * 2,
        4 * LANES * samp * n_col * feat_grp,
    )
    return (precond, act_cov, grad_cov)


def solution(mesh):
    return jax.shard_map(
        body,
        mesh=mesh,
        in_specs=(P("col", "row"), P("col", "grp"), P("col"), P("grp", "row"), P("grp", "col")),
        out_specs=(P(("grp", "row"), "col"), P(("row", "col"), "grp"), P(("row", "col"), "grp")),
        check_vma=False,
    )
```

```python
import functools

import jax
import jax.numpy as jnp
from jax import lax
from jax.experimental import pallas as pl
from jax.experimental.pallas import tpu as pltpu
from jax.sharding import PartitionSpec as P

BF = jnp.bfloat16
F32 = jnp.float32
LANES = 128
FIRST = (((0,), (0,)), ((), ()))
LAST = (((1,), (1,)), ((), ()))
SMEM = pl.BlockSpec(memory_space=pltpu.SMEM)
VMEM = pl.BlockSpec(memory_space=pltpu.VMEM)
SHIFTS = (0, 2, 1, -1)


def call(kernel, inputs, outs, flops, scratch=(), place=VMEM, limit=40):
    moved = sum(x.size * x.dtype.itemsize for x in list(inputs) + list(outs))
    return pl.pallas_call(
        kernel,
        out_shape=outs,
        in_specs=[SMEM if x.dtype == jnp.int32 else place for x in inputs],
        out_specs=[VMEM] * len(outs),
        scratch_shapes=list(scratch),
        compiler_params=pltpu.CompilerParams(vmem_limit_bytes=limit * 1024 * 1024),
        cost_estimate=pl.CostEstimate(flops=flops, bytes_accessed=moved, transcendentals=0),
    )(*inputs)


def source_of(k):
    col = lax.axis_index("col")
    return 4 * ((col // 4) ^ (k % 2)) + lax.rem(col % 4 - k // 2 + 4, 4)


def own_picks(picks, count, tok):
    begin = lax.axis_index("grp") * count
    first = lax.axis_index("col") * tok
    return [picks[begin + i] - first for i in range(count)]


def rows_hot(targets, tok):
    shape = (len(targets), tok)
    sub = lax.broadcasted_iota(jnp.int32, shape, 0)
    lane = lax.broadcasted_iota(jnp.int32, shape, 1)
    want = jnp.zeros(shape, jnp.int32)
    for i, target in enumerate(targets):
        want = jnp.where(sub == i, target, want)
    return jnp.where(want == lane, 1.0, 0.0).astype(BF)


def first_kernel(picks, x_hbm, a_hbm, out_ref, x_ref, a_ref, sems):
    n_row, depth, tok = out_ref.shape
    parts = sems.shape[0] - 1
    step = a_ref.shape[0] // parts
    copies = [pltpu.make_async_copy(x_hbm, x_ref, sems.at[parts])]
    for p in range(parts):
        span = pl.ds(p * step, step)
        copies.append(pltpu.make_async_copy(a_hbm.at[span], a_ref.at[span], sems.at[p]))
    for copy in copies:
        copy.start()
    out_rows = a_ref.shape[0] // n_row
    quarter = picks.shape[0] // 4
    hot = rows_hot(own_picks(picks, quarter, tok), tok)
    copies[0].wait()
    chosen = jnp.dot(hot, x_ref[...], preferred_element_type=F32)
    strips = [chosen[:, k : k + LANES] for k in range(0, chosen.shape[1], LANES)]
    block = jnp.concatenate(strips, axis=0).astype(BF)
    out_ref[:, out_rows:, :] = jnp.broadcast_to(block[None], (n_row,) + block.shape)
    each = step // out_rows
    for p in range(parts):
        copies[p + 1].wait()
        rows = a_ref[p * step : (p + 1) * step, :]
        part = lax.dot_general(rows, x_ref[...], LAST, preferred_element_type=F32)
        out_ref[p * each : (p + 1) * each, :out_rows, :] = part.astype(BF).reshape(
            each, out_rows, tok
        )


def pick_kernel(picks, g_ref, out_ref):
    tok = g_ref.shape[0]
    samp = picks.shape[0]
    plane = lax.axis_index("row") % 4
    first = lax.axis_index("col") * tok
    count = out_ref.shape[0] - samp
    ours = [64 * (i // 16) + 16 * plane + i % 16 for i in range(count)]
    hot = rows_hot(ours + [picks[i] - first for i in range(samp)], tok)
    out_ref[...] = jnp.dot(hot, g_ref[...], preferred_element_type=F32).astype(BF)


def right_kernel(b_ref, gy_ref, *refs):
    blocks, keep_ref, give_ref, held = refs[:-3], refs[-3], refs[-2], refs[-1]
    n_blk, unused, size, width = held.shape
    step = gy_ref.shape[0]
    spans = [slice(at, at + 2 * size) for at in (0, step)]
    rows = jnp.concatenate([block[span, :] for block in blocks for span in spans], axis=0)
    term = jnp.dot(rows, b_ref[...], preferred_element_type=F32)
    held[...] = term.reshape(held.shape)
    core = lax.axis_index("grp") % 2
    cut = n_blk * size
    keep_ref[:cut, :] = held[:, core].reshape(cut, width)
    give_ref[:cut, :] = held[:, 1 - core].reshape(cut, width).astype(BF)
    feat = width // 2
    samp = 2 * (give_ref.shape[0] - cut)
    begin = pl.multiple_of((lax.axis_index("row") % 4) * feat, LANES)
    own = gy_ref[gy_ref.shape[0] - samp :, pl.ds(begin, feat)]
    own = jnp.concatenate([own[: samp // 2], own[samp // 2 :]], axis=1)
    keep_ref[cut:, :] = own.astype(F32)
    give_ref[cut:, :] = own


def gather_kernel(got_ref, u_ref, x_ref):
    n_grp, x_rows, unused = x_ref.shape
    n_row, depth, tok = got_ref.shape
    out_rows = u_ref.shape[0]
    total = got_ref[0, :out_rows, :].astype(F32)
    for r in range(1, n_row):
        total = total + got_ref[r, :out_rows, :].astype(F32)
    u_ref[...] = total.astype(BF)
    per = n_row // n_grp
    feats = out_rows
    half = tok // 2
    other = jnp.where(lax.axis_index("grp") % 2 == 0, total[:, half:], total[:, :half])
    other = jnp.concatenate([other[: out_rows // 2], other[out_rows // 2 :]], axis=1).astype(BF)
    for g in range(n_grp):
        block = got_ref[g * per : (g + 1) * per, out_rows:, :].astype(F32)
        x_ref[g, :feats, :] = block.reshape(feats, tok).astype(BF)
        x_ref[g, feats:, :] = other


def second_kernel(picks, u_ref, x_ref, y_ref, tokens_ref, out_ref):
    n_col, depth, unused = out_ref.shape
    out_rows, tok = u_ref.shape
    feat = tokens_ref.shape[1]
    samp = picks.shape[0]
    tile = feat // n_col
    begin = lax.axis_index("col") * tok
    hot = rows_hot([picks[i] - begin for i in range(samp)], tok)
    chosen = jnp.dot(hot, tokens_ref[...], preferred_element_type=F32)
    own = y_ref[...].astype(F32)
    own = jnp.concatenate([own[:, :feat], own[:, feat:]], axis=0)
    empty = jnp.zeros((samp, LANES - 2 * tile), F32)
    half = tok // 2
    grp = lax.axis_index("grp")
    u_own = u_ref[...].astype(F32)
    u_own = jnp.where(grp % 2 == 0, u_own[:, :half], u_own[:, half:])
    u_pair = x_ref[grp ^ 1, out_rows:, :].astype(F32)
    u_pair = jnp.concatenate([u_pair[:, :half], u_pair[:, half:]], axis=0)
    u_block = jnp.concatenate([u_own, u_pair], axis=1).astype(BF)
    x_block = x_ref[:, :out_rows, :].reshape(x_ref.shape[0] * out_rows, LANES)
    for c in range(n_col):
        span = slice(c * tile, (c + 1) * tile)
        out_ref[c, :out_rows, :] = u_block
        out_ref[c, out_rows : depth - samp, :] = x_block
        side = jnp.concatenate([own[:, span], chosen[:, span], empty], axis=1)
        out_ref[c, depth - samp :, :] = side.astype(BF)


def final_kernel(got_ref, *refs):
    v_refs, own_ref, pair_ref, held = refs[:-3], refs[-3], refs[-2], refs[-1]
    n_col, spread, size, width = held.shape
    out_rows = own_ref.shape[0]
    row = lax.axis_index("row")
    for j, shift in enumerate(SHIFTS):
        plane = lax.rem(row - shift + spread, spread)
        for k in range(n_col):
            held[source_of(k), plane] = v_refs[j][k * size : (k + 1) * size, :]
    half = spread * size
    total = None
    for c in range(0, n_col, 4):
        blocks = [got_ref[c + i, :out_rows, :] for i in range(4)]
        own = jnp.concatenate([block[:, :half] for block in blocks], axis=1)
        pair = jnp.concatenate([block[:, half:] for block in blocks], axis=1)
        left = jnp.concatenate([own, pair], axis=0)
        right = held[c : c + 4].reshape(4 * half, width)
        term = jnp.dot(left, right, preferred_element_type=F32)
        total = term if total is None else total + term
    own_ref[...] = total[:out_rows]
    pair_ref[...] = total[out_rows:].astype(BF)


def factor_kernel(got_ref, *refs):
    blocks, act_ref, grad_ref = refs[:-2], refs[-2], refs[-1]
    n_col, depth, unused = got_ref.shape
    tile, width = act_ref.shape
    samp = blocks[0].shape[0] // 4
    quarter = samp // 4
    total = samp * n_col
    scale = 1.0 / total
    count = 4 * quarter * (width // LANES)
    span = got_ref[:, depth - samp - count : depth - samp, :].astype(F32)
    span = span.reshape(n_col, 4, count // 4, LANES)
    strips = []
    for t in range(width // LANES):
        strip = span[:, :, t * quarter : (t + 1) * quarter, :].reshape(total, LANES)
        strips.append(strip.astype(BF))
    right = jnp.concatenate(strips, axis=1)
    left = got_ref[:, depth - samp :, :].reshape(total, LANES)
    term = lax.dot_general(left, right, FIRST, preferred_element_type=F32)
    act_ref[...] = term[tile : 2 * tile] * scale
    sides = [got_ref[source_of(k), depth - samp :, :] for k in range(n_col)]
    left = jnp.concatenate(sides, axis=0)
    spans = [slice(at, at + samp) for at in (samp, 3 * samp)]
    right = jnp.concatenate([block[span, :] for block in blocks for span in spans], axis=0)
    term = lax.dot_general(left, right, FIRST, preferred_element_type=F32)
    grad_ref[...] = term[:tile] * scale


def body(tokens_in, cotangent, sample_rows, act_inverse, grad_inverse):
    n_row = lax.axis_size("row")
    n_col = lax.axis_size("col")
    n_grp = lax.axis_size("grp")
    tok, feat_row = tokens_in.shape
    feat_grp = cotangent.shape[1]
    width = grad_inverse.shape[1]
    samp = sample_rows.shape[0]
    quarter = samp // n_grp
    tile = feat_row // n_col
    out_rows = feat_grp // n_row
    strip = quarter * feat_row // LANES
    spread = 4
    size = tok // 2 // spread
    shape = jax.ShapeDtypeStruct

    picked = call(
        pick_kernel,
        (sample_rows, cotangent),
        [shape((2 * size + samp, feat_grp), BF)],
        2 * 64 * tok * feat_grp,
        limit=56,
    )[0]
    beside = lax.ppermute(picked, "col", [(i, (i + 4) % n_col) for i in range(n_col)])
    picked, x_in = lax.optimization_barrier((picked, tokens_in))
    payload = call(
        first_kernel,
        (sample_rows, x_in, act_inverse),
        [shape((n_row, out_rows + strip, tok), BF)],
        2 * feat_grp * feat_row * tok,
        [
            pltpu.VMEM(tokens_in.shape, BF),
            pltpu.VMEM(act_inverse.shape, BF),
            pltpu.SemaphoreType.DMA((5,)),
        ],
        pl.BlockSpec(memory_space=pl.ANY),
        limit=56,
    )[0]
    first = lax.all_to_all(payload, "row", 0, 0)

    def along_y(block, k):
        return lax.ppermute(
            block, "col", [(i, i - i % 4 + (i + k) % 4) for i in range(n_col)]
        )

    pair = jnp.concatenate([picked, beside], axis=0)
    pairs = [pair] + [along_y(pair, k) for k in range(1, 4)]
    half = n_col * size
    extra = samp // 2
    keep, give = call(
        right_kernel,
        (grad_inverse, picked, *pairs),
        [shape((half + extra, width), F32), shape((half + extra, width), BF)],
        4 * n_col * size * feat_grp * width,
        [pltpu.VMEM((n_col, 2, size, width), F32)],
    )
    first, unused = lax.optimization_barrier((first, give))

    owner = lax.axis_index("row") // 4
    grp = lax.axis_index("grp")
    taken = lax.ppermute(give, "grp", [(i, i ^ 1) for i in range(n_grp)]).astype(F32)
    own_y = jnp.where(grp % 2 == owner % 2, keep[half:], taken[half:])
    keep = jnp.concatenate([keep[:half] + taken[:half], own_y], axis=0)
    taken = lax.ppermute(keep.astype(BF), "grp", [(i, i ^ 2) for i in range(n_grp)]).astype(F32)
    own_y = jnp.where(grp // 2 == owner // 2, keep[half:], taken[half:]).astype(BF)
    right = (keep[:half] + taken[:half]).astype(BF)
    u_own, x_send = call(
        gather_kernel,
        (first,),
        [shape((out_rows, tok), BF), shape((n_grp, out_rows + out_rows // 2, LANES), BF)],
        1000000,
    )
    right, unused = lax.optimization_barrier((right, x_send))
    rights = [right] + [
        lax.ppermute(right, "row", [(i, (i + j) % n_row) for i in range(n_row)])
        for j in SHIFTS[1:]
    ]
    x_got = lax.all_to_all(x_send, "grp", 0, 0)
    send = call(
        second_kernel,
        (sample_rows, u_own, x_got, own_y, tokens_in),
        [shape((n_col, out_rows + strip * n_row + samp, LANES), BF)],
        2 * samp * tok * feat_row,
    )[0]
    got = lax.all_to_all(send, "col", 0, 0)

    term, send = call(
        final_kernel,
        (got, *rights),
        [shape((out_rows, width), F32), shape((out_rows, width), BF)],
        2 * out_rows * n_col * tok * width,
        [pltpu.VMEM((n_col, spread, size, width), BF)],
    )
    got, unused = lax.optimization_barrier((got, send))
    taken = lax.ppermute(send, "grp", [(i, i ^ 1) for i in range(n_grp)])
    precond = term + taken.astype(F32)
    act_cov, grad_cov = call(
        factor_kernel,
        (got, *pairs),
        [shape((tile, feat_grp), F32)] * 2,
        4 * LANES * samp * n_col * feat_grp,
    )
    return (precond, act_cov, grad_cov)


def solution(mesh):
    return jax.shard_map(
        body,
        mesh=mesh,
        in_specs=(P("col", "row"), P("col", "grp"), P("col"), P("grp", "row"), P("grp", "col")),
        out_specs=(P(("grp", "row"), "col"), P(("row", "col"), "grp"), P(("row", "col"), "grp")),
        check_vma=False,
    )
```

```python
import functools

import jax
import jax.numpy as jnp
from jax import lax
from jax.experimental import pallas as pl
from jax.experimental.pallas import tpu as pltpu
from jax.sharding import PartitionSpec as P

BF = jnp.bfloat16
F32 = jnp.float32
LANES = 128
FIRST = (((0,), (0,)), ((), ()))
LAST = (((1,), (1,)), ((), ()))
SMEM = pl.BlockSpec(memory_space=pltpu.SMEM)
VMEM = pl.BlockSpec(memory_space=pltpu.VMEM)
SHIFTS = (0, 2, 1, -1)


def call(kernel, inputs, outs, flops, scratch=(), place=VMEM, limit=16):
    moved = sum(x.size * x.dtype.itemsize for x in list(inputs) + list(outs))
    return pl.pallas_call(
        kernel,
        out_shape=outs,
        in_specs=[SMEM if x.dtype == jnp.int32 else place for x in inputs],
        out_specs=[VMEM] * len(outs),
        scratch_shapes=list(scratch),
        compiler_params=pltpu.CompilerParams(vmem_limit_bytes=limit * 1024 * 1024),
        cost_estimate=pl.CostEstimate(flops=flops, bytes_accessed=moved, transcendentals=0),
    )(*inputs)


def source_of(k):
    col = lax.axis_index("col")
    return 4 * ((col // 4) ^ (k % 2)) + lax.rem(col % 4 - k // 2 + 4, 4)


def own_picks(picks, count, tok):
    begin = lax.axis_index("grp") * count
    first = lax.axis_index("col") * tok
    return [picks[begin + i] - first for i in range(count)]


def rows_hot(targets, tok):
    shape = (len(targets), tok)
    sub = lax.broadcasted_iota(jnp.int32, shape, 0)
    lane = lax.broadcasted_iota(jnp.int32, shape, 1)
    want = jnp.zeros(shape, jnp.int32)
    for i, target in enumerate(targets):
        want = jnp.where(sub == i, target, want)
    return jnp.where(want == lane, 1.0, 0.0).astype(BF)


def first_kernel(picks, x_hbm, a_hbm, out_ref, x_ref, a_ref, sems):
    n_row, depth, tok = out_ref.shape
    parts = sems.shape[0] - 1
    step = a_ref.shape[0] // parts
    copies = [pltpu.make_async_copy(x_hbm, x_ref, sems.at[parts])]
    for p in range(parts):
        span = pl.ds(p * step, step)
        copies.append(pltpu.make_async_copy(a_hbm.at[span], a_ref.at[span], sems.at[p]))
    for copy in copies:
        copy.start()
    out_rows = a_ref.shape[0] // n_row
    quarter = picks.shape[0] // 4
    hot = rows_hot(own_picks(picks, quarter, tok), tok)
    copies[0].wait()
    chosen = jnp.dot(hot, x_ref[...], preferred_element_type=F32)
    strips = [chosen[:, k : k + LANES] for k in range(0, chosen.shape[1], LANES)]
    block = jnp.concatenate(strips, axis=0).astype(BF)
    out_ref[:, out_rows:, :] = jnp.broadcast_to(block[None], (n_row,) + block.shape)
    each = step // out_rows
    for p in range(parts):
        copies[p + 1].wait()
        rows = a_ref[p * step : (p + 1) * step, :]
        part = lax.dot_general(rows, x_ref[...], LAST, preferred_element_type=F32)
        out_ref[p * each : (p + 1) * each, :out_rows, :] = part.astype(BF).reshape(
            each, out_rows, tok
        )


def pick_kernel(picks, g_ref, out_ref):
    tok = g_ref.shape[0]
    samp = picks.shape[0]
    plane = lax.axis_index("row") % 4
    first = lax.axis_index("col") * tok
    count = out_ref.shape[0] - samp
    ours = [64 * (i // 16) + 16 * plane + i % 16 for i in range(count)]
    hot = rows_hot(ours + [picks[i] - first for i in range(samp)], tok)
    out_ref[...] = jnp.dot(hot, g_ref[...], preferred_element_type=F32).astype(BF)


def right_kernel(b_ref, gy_ref, *refs):
    blocks, keep_ref, give_ref, held = refs[:-3], refs[-3], refs[-2], refs[-1]
    n_blk, unused, size, width = held.shape
    step = gy_ref.shape[0]
    spans = [slice(at, at + 2 * size) for at in (0, step)]
    rows = jnp.concatenate([block[span, :] for block in blocks for span in spans], axis=0)
    term = jnp.dot(rows, b_ref[...], preferred_element_type=F32)
    held[...] = term.reshape(held.shape)
    core = lax.axis_index("grp") % 2
    cut = n_blk * size
    keep_ref[:cut, :] = held[:, core].reshape(cut, width)
    give_ref[:cut, :] = held[:, 1 - core].reshape(cut, width).astype(BF)
    feat = width // 2
    samp = 2 * (give_ref.shape[0] - cut)
    begin = pl.multiple_of((lax.axis_index("row") % 4) * feat, LANES)
    own = gy_ref[gy_ref.shape[0] - samp :, pl.ds(begin, feat)]
    own = jnp.concatenate([own[: samp // 2], own[samp // 2 :]], axis=1)
    keep_ref[cut:, :] = own.astype(F32)
    give_ref[cut:, :] = own


def gather_kernel(got_ref, u_ref, x_ref):
    n_grp, x_rows, unused = x_ref.shape
    n_row, depth, tok = got_ref.shape
    out_rows = u_ref.shape[0]
    total = got_ref[0, :out_rows, :].astype(F32)
    for r in range(1, n_row):
        total = total + got_ref[r, :out_rows, :].astype(F32)
    u_ref[...] = total.astype(BF)
    per = n_row // n_grp
    feats = out_rows
    half = tok // 2
    other = jnp.where(lax.axis_index("grp") % 2 == 0, total[:, half:], total[:, :half])
    other = jnp.concatenate([other[: out_rows // 2], other[out_rows // 2 :]], axis=1).astype(BF)
    for g in range(n_grp):
        block = got_ref[g * per : (g + 1) * per, out_rows:, :].astype(F32)
        x_ref[g, :feats, :] = block.reshape(feats, tok).astype(BF)
        x_ref[g, feats:, :] = other


def second_kernel(picks, u_ref, x_ref, y_ref, tokens_ref, out_ref):
    n_col, depth, unused = out_ref.shape
    out_rows, tok = u_ref.shape
    feat = tokens_ref.shape[1]
    samp = picks.shape[0]
    tile = feat // n_col
    begin = lax.axis_index("col") * tok
    hot = rows_hot([picks[i] - begin for i in range(samp)], tok)
    chosen = jnp.dot(hot, tokens_ref[...], preferred_element_type=F32)
    own = y_ref[...].astype(F32)
    own = jnp.concatenate([own[:, :feat], own[:, feat:]], axis=0)
    empty = jnp.zeros((samp, LANES - 2 * tile), F32)
    half = tok // 2
    grp = lax.axis_index("grp")
    u_own = u_ref[...].astype(F32)
    u_own = jnp.where(grp % 2 == 0, u_own[:, :half], u_own[:, half:])
    u_pair = x_ref[grp ^ 1, out_rows:, :].astype(F32)
    u_pair = jnp.concatenate([u_pair[:, :half], u_pair[:, half:]], axis=0)
    u_block = jnp.concatenate([u_own, u_pair], axis=1).astype(BF)
    x_block = x_ref[:, :out_rows, :].reshape(x_ref.shape[0] * out_rows, LANES)
    for c in range(n_col):
        span = slice(c * tile, (c + 1) * tile)
        out_ref[c, :out_rows, :] = u_block
        out_ref[c, out_rows : depth - samp, :] = x_block
        side = jnp.concatenate([own[:, span], chosen[:, span], empty], axis=1)
        out_ref[c, depth - samp :, :] = side.astype(BF)


def final_kernel(got_ref, *refs):
    v_refs, own_ref, pair_ref, held = refs[:-3], refs[-3], refs[-2], refs[-1]
    n_col, spread, size, width = held.shape
    out_rows = own_ref.shape[0]
    row = lax.axis_index("row")
    for j, shift in enumerate(SHIFTS):
        plane = lax.rem(row - shift + spread, spread)
        for k in range(n_col):
            held[source_of(k), plane] = v_refs[j][k * size : (k + 1) * size, :]
    half = spread * size
    total = None
    for c in range(0, n_col, 4):
        blocks = [got_ref[c + i, :out_rows, :] for i in range(4)]
        own = jnp.concatenate([block[:, :half] for block in blocks], axis=1)
        pair = jnp.concatenate([block[:, half:] for block in blocks], axis=1)
        left = jnp.concatenate([own, pair], axis=0)
        right = held[c : c + 4].reshape(4 * half, width)
        term = jnp.dot(left, right, preferred_element_type=F32)
        total = term if total is None else total + term
    own_ref[...] = total[:out_rows]
    pair_ref[...] = total[out_rows:].astype(BF)


def factor_kernel(got_ref, *refs):
    blocks, act_ref, grad_ref = refs[:-2], refs[-2], refs[-1]
    n_col, depth, unused = got_ref.shape
    tile, width = act_ref.shape
    samp = blocks[0].shape[0] // 4
    quarter = samp // 4
    total = samp * n_col
    scale = 1.0 / total
    count = 4 * quarter * (width // LANES)
    span = got_ref[:, depth - samp - count : depth - samp, :].astype(F32)
    span = span.reshape(n_col, 4, count // 4, LANES)
    strips = []
    for t in range(width // LANES):
        strip = span[:, :, t * quarter : (t + 1) * quarter, :].reshape(total, LANES)
        strips.append(strip.astype(BF))
    right = jnp.concatenate(strips, axis=1)
    left = got_ref[:, depth - samp :, :].reshape(total, LANES)
    term = lax.dot_general(left, right, FIRST, preferred_element_type=F32)
    act_ref[...] = term[tile : 2 * tile] * scale
    sides = [got_ref[source_of(k), depth - samp :, :] for k in range(n_col)]
    left = jnp.concatenate(sides, axis=0)
    spans = [slice(at, at + samp) for at in (samp, 3 * samp)]
    right = jnp.concatenate([block[span, :] for block in blocks for span in spans], axis=0)
    term = lax.dot_general(left, right, FIRST, preferred_element_type=F32)
    grad_ref[...] = term[:tile] * scale


def body(tokens_in, cotangent, sample_rows, act_inverse, grad_inverse):
    n_row = lax.axis_size("row")
    n_col = lax.axis_size("col")
    n_grp = lax.axis_size("grp")
    tok, feat_row = tokens_in.shape
    feat_grp = cotangent.shape[1]
    width = grad_inverse.shape[1]
    samp = sample_rows.shape[0]
    quarter = samp // n_grp
    tile = feat_row // n_col
    out_rows = feat_grp // n_row
    strip = quarter * feat_row // LANES
    spread = 4
    size = tok // 2 // spread
    shape = jax.ShapeDtypeStruct

    picked = call(
        pick_kernel,
        (sample_rows, cotangent),
        [shape((2 * size + samp, feat_grp), BF)],
        2 * 64 * tok * feat_grp,
        limit=56,
    )[0]
    beside = lax.ppermute(picked, "col", [(i, (i + 4) % n_col) for i in range(n_col)])
    picked, x_in = lax.optimization_barrier((picked, tokens_in))
    payload = call(
        first_kernel,
        (sample_rows, x_in, act_inverse),
        [shape((n_row, out_rows + strip, tok), BF)],
        2 * feat_grp * feat_row * tok,
        [
            pltpu.VMEM(tokens_in.shape, BF),
            pltpu.VMEM(act_inverse.shape, BF),
            pltpu.SemaphoreType.DMA((5,)),
        ],
        pl.BlockSpec(memory_space=pl.ANY),
        limit=56,
    )[0]
    first = lax.all_to_all(payload, "row", 0, 0)

    def along_y(block, k):
        return lax.ppermute(
            block, "col", [(i, i - i % 4 + (i + k) % 4) for i in range(n_col)]
        )

    pair = jnp.concatenate([picked, beside], axis=0)
    pairs = [pair] + [along_y(pair, k) for k in range(1, 4)]
    half = n_col * size
    extra = samp // 2
    keep, give = call(
        right_kernel,
        (grad_inverse, picked, *pairs),
        [shape((half + extra, width), F32), shape((half + extra, width), BF)],
        4 * n_col * size * feat_grp * width,
        [pltpu.VMEM((n_col, 2, size, width), F32)],
    )
    owner = lax.axis_index("row") // 4
    grp = lax.axis_index("grp")
    first, unused = lax.optimization_barrier((first, give))
    u_own, x_send = call(
        gather_kernel,
        (first,),
        [shape((out_rows, tok), BF), shape((n_grp, out_rows + out_rows // 2, LANES), BF)],
        1000000,
    )
    x_got = lax.all_to_all(x_send, "grp", 0, 0)
    taken = lax.ppermute(give, "grp", [(i, i ^ 1) for i in range(n_grp)])
    taken, unused = lax.optimization_barrier((taken, x_send))
    taken = taken.astype(F32)
    own_y = jnp.where(grp % 2 == owner % 2, keep[half:], taken[half:])
    keep = jnp.concatenate([keep[:half] + taken[:half], own_y], axis=0)
    taken = lax.ppermute(keep.astype(BF), "grp", [(i, i ^ 2) for i in range(n_grp)]).astype(F32)
    own_y = jnp.where(grp // 2 == owner // 2, keep[half:], taken[half:]).astype(BF)
    right = (keep[:half] + taken[:half]).astype(BF)
    send = call(
        second_kernel,
        (sample_rows, u_own, x_got, own_y, tokens_in),
        [shape((n_col, out_rows + strip * n_row + samp, LANES), BF)],
        2 * samp * tok * feat_row,
    )[0]
    got = lax.all_to_all(send, "col", 0, 0)
    right, unused = lax.optimization_barrier((right, send))
    rights = [right] + [
        lax.ppermute(right, "row", [(i, (i + j) % n_row) for i in range(n_row)])
        for j in SHIFTS[1:]
    ]
    term, send = call(
        final_kernel,
        (got, *rights),
        [shape((out_rows, width), F32), shape((out_rows, width), BF)],
        2 * out_rows * n_col * tok * width,
        [pltpu.VMEM((n_col, spread, size, width), BF)],
    )
    got, unused = lax.optimization_barrier((got, send))
    taken = lax.ppermute(send, "grp", [(i, i ^ 1) for i in range(n_grp)])
    precond = term + taken.astype(F32)
    act_cov, grad_cov = call(
        factor_kernel,
        (got, *pairs),
        [shape((tile, feat_grp), F32)] * 2,
        4 * LANES * samp * n_col * feat_grp,
    )
    return (precond, act_cov, grad_cov)


def solution(mesh):
    return jax.shard_map(
        body,
        mesh=mesh,
        in_specs=(P("col", "row"), P("col", "grp"), P("col"), P("grp", "row"), P("grp", "col")),
        out_specs=(P(("grp", "row"), "col"), P(("row", "col"), "grp"), P(("row", "col"), "grp")),
        check_vma=False,
    )
```

```python
import functools

import jax
import jax.numpy as jnp
from jax import lax
from jax.experimental import pallas as pl
from jax.experimental.pallas import tpu as pltpu
from jax.sharding import PartitionSpec as P

BF = jnp.bfloat16
F32 = jnp.float32
LANES = 128
FIRST = (((0,), (0,)), ((), ()))
LAST = (((1,), (1,)), ((), ()))
SMEM = pl.BlockSpec(memory_space=pltpu.SMEM)
VMEM = pl.BlockSpec(memory_space=pltpu.VMEM)
SHIFTS = (0, 2, 1, -1)


def call(kernel, inputs, outs, flops, scratch=(), place=VMEM, limit=16):
    moved = sum(x.size * x.dtype.itemsize for x in list(inputs) + list(outs))
    return pl.pallas_call(
        kernel,
        out_shape=outs,
        in_specs=[SMEM if x.dtype == jnp.int32 else place for x in inputs],
        out_specs=[VMEM] * len(outs),
        scratch_shapes=list(scratch),
        compiler_params=pltpu.CompilerParams(vmem_limit_bytes=limit * 1024 * 1024),
        cost_estimate=pl.CostEstimate(flops=flops, bytes_accessed=moved, transcendentals=0),
    )(*inputs)


def source_of(k):
    col = lax.axis_index("col")
    return 4 * ((col // 4) ^ (k % 2)) + lax.rem(col % 4 - k // 2 + 4, 4)


def own_picks(picks, count, tok):
    begin = lax.axis_index("grp") * count
    first = lax.axis_index("col") * tok
    return [picks[begin + i] - first for i in range(count)]


def rows_hot(targets, tok):
    shape = (len(targets), tok)
    sub = lax.broadcasted_iota(jnp.int32, shape, 0)
    lane = lax.broadcasted_iota(jnp.int32, shape, 1)
    want = jnp.zeros(shape, jnp.int32)
    for i, target in enumerate(targets):
        want = jnp.where(sub == i, target, want)
    return jnp.where(want == lane, 1.0, 0.0).astype(BF)


def pick_kernel(picks, g_ref, x_ref, rows_ref, samples_ref, block_ref):
    tok = g_ref.shape[0]
    samp = picks.shape[0]
    plane = lax.axis_index("row") % 4
    first = lax.axis_index("col") * tok
    count = rows_ref.shape[0]
    ours = [64 * (i // 16) + 16 * plane + i % 16 for i in range(count)]
    hot = rows_hot(ours + [picks[i] - first for i in range(samp)], tok)
    chosen = jnp.dot(hot, g_ref[...], preferred_element_type=F32).astype(BF)
    rows_ref[...] = chosen[:count]
    samples_ref[...] = chosen[count:]
    hot = rows_hot(own_picks(picks, samp // 4, tok), tok)
    chosen = jnp.dot(hot, x_ref[...], preferred_element_type=F32)
    strips = [chosen[:, k : k + LANES] for k in range(0, chosen.shape[1], LANES)]
    block_ref[...] = jnp.concatenate(strips, axis=0).astype(BF)


def first_kernel(x_hbm, a_hbm, out_ref, x_ref, a_ref, sems):
    n_row, out_rows, tok = out_ref.shape
    parts = sems.shape[0] - 1
    step = a_ref.shape[0] // parts
    copies = [pltpu.make_async_copy(x_hbm, x_ref, sems.at[parts])]
    for p in range(parts):
        span = pl.ds(p * step, step)
        copies.append(pltpu.make_async_copy(a_hbm.at[span], a_ref.at[span], sems.at[p]))
    for copy in copies:
        copy.start()
    copies[0].wait()
    each = step // out_rows
    for p in range(parts):
        copies[p + 1].wait()
        rows = a_ref[p * step : (p + 1) * step, :]
        part = lax.dot_general(rows, x_ref[...], LAST, preferred_element_type=F32)
        out_ref[p * each : (p + 1) * each] = part.astype(BF).reshape(each, out_rows, tok)


def right_kernel(b_ref, y_ref, g_ref, keep_ref, give_ref, held):
    n_blk, unused, size, width = held.shape
    rows = g_ref[...].reshape(n_blk * 2 * size, g_ref.shape[2])
    term = jnp.dot(rows, b_ref[...], preferred_element_type=F32)
    held[...] = term.reshape(held.shape)
    core = lax.axis_index("grp") % 2
    cut = n_blk * size
    keep_ref[:cut, :] = held[:, core].reshape(cut, width)
    give_ref[:cut, :] = held[:, 1 - core].reshape(cut, width).astype(BF)
    feat = width // 2
    samp = y_ref.shape[0]
    begin = pl.multiple_of((lax.axis_index("row") % 4) * feat, LANES)
    own = y_ref[:, pl.ds(begin, feat)]
    own = jnp.concatenate([own[: samp // 2], own[samp // 2 :]], axis=1)
    keep_ref[cut:, :] = own.astype(F32)
    give_ref[cut:, :] = own


def second_kernel(picks, got_ref, y_ref, tokens_ref, out_ref):
    n_col, depth, unused = out_ref.shape
    n_row, rows, tok = got_ref.shape
    feat = tokens_ref.shape[1]
    samp = picks.shape[0]
    tile = feat // n_col
    out_rows = rows - samp // 4 * feat // LANES
    total = got_ref[0, :out_rows, :].astype(F32)
    for r in range(1, n_row):
        total = total + got_ref[r, :out_rows, :].astype(F32)
    u_block = total.astype(BF)
    x_block = got_ref[:, out_rows:, :].astype(F32)
    x_block = x_block.reshape(depth - samp - out_rows, LANES).astype(BF)
    begin = lax.axis_index("col") * tok
    hot = rows_hot([picks[i] - begin for i in range(samp)], tok)
    chosen = jnp.dot(hot, tokens_ref[...], preferred_element_type=F32)
    own = y_ref[...].astype(F32)
    own = jnp.concatenate([own[:, :feat], own[:, feat:]], axis=0)
    empty = jnp.zeros((samp, LANES - 2 * tile), F32)
    for c in range(n_col):
        span = slice(c * tile, (c + 1) * tile)
        out_ref[c, :out_rows, :] = u_block
        out_ref[c, out_rows : depth - samp, :] = x_block
        side = jnp.concatenate([own[:, span], chosen[:, span], empty], axis=1)
        out_ref[c, depth - samp :, :] = side.astype(BF)


def final_kernel(got_ref, pair_ref, *refs):
    v_refs, out_ref, held = refs[:-2], refs[-2], refs[-1]
    n_col, unused, spread, size, width = held.shape
    out_rows = out_ref.shape[0]
    row = lax.axis_index("row")
    core = lax.axis_index("grp") % 2
    cut = n_col * size
    for j, shift in enumerate(SHIFTS):
        plane = lax.rem(row - shift + spread, spread)
        for k in range(n_col):
            span = slice(k * size, (k + 1) * size)
            held[k, core, plane] = v_refs[j][span, :]
            span = slice(j * cut + k * size, j * cut + (k + 1) * size)
            held[k, 1 - core, plane] = pair_ref[span, :]
    tokens = 2 * spread * size
    total = None
    for c in range(0, n_col, 2):
        left = jnp.concatenate([got_ref[c, :out_rows, :], got_ref[c + 1, :out_rows, :]], axis=1)
        right = held[c : c + 2].reshape(2 * tokens, width)
        term = jnp.dot(left, right, preferred_element_type=F32)
        total = term if total is None else total + term
    out_ref[...] = total


def factor_kernel(got_ref, *refs):
    blocks, act_ref, grad_ref = refs[:-2], refs[-2], refs[-1]
    n_col, depth, unused = got_ref.shape
    tile, width = act_ref.shape
    samp = blocks[0].shape[0] // 2
    quarter = samp // 4
    total = samp * n_col
    scale = 1.0 / total
    count = 4 * quarter * (width // LANES)
    span = got_ref[:, depth - samp - count : depth - samp, :].astype(F32)
    per = width // LANES // 4
    span = span.reshape(n_col, 4, 4, per * quarter, LANES)
    strips = []
    for t in range(width // LANES):
        at = t % per * quarter
        strip = span[:, t // per, :, at : at + quarter, :].reshape(total, LANES)
        strips.append(strip.astype(BF))
    right = jnp.concatenate(strips, axis=1)
    left = got_ref[:, depth - samp :, :].reshape(total, LANES)
    term = lax.dot_general(left, right, FIRST, preferred_element_type=F32)
    act_ref[...] = term[tile : 2 * tile] * scale
    sides = [got_ref[source_of(k), depth - samp :, :] for k in range(n_col)]
    left = jnp.concatenate(sides, axis=0)
    right = jnp.concatenate([block[...] for block in blocks], axis=0)
    term = lax.dot_general(left, right, FIRST, preferred_element_type=F32)
    grad_ref[...] = term[:tile] * scale


def body(tokens_in, cotangent, sample_rows, act_inverse, grad_inverse):
    n_row = lax.axis_size("row")
    n_col = lax.axis_size("col")
    n_grp = lax.axis_size("grp")
    tok, feat_row = tokens_in.shape
    feat_grp = cotangent.shape[1]
    width = grad_inverse.shape[1]
    samp = sample_rows.shape[0]
    quarter = samp // n_grp
    tile = feat_row // n_col
    out_rows = feat_grp // n_row
    strip = quarter * feat_row // LANES
    spread = 4
    size = tok // 2 // spread
    shape = jax.ShapeDtypeStruct

    rows, samples, block = call(
        pick_kernel,
        (sample_rows, cotangent, tokens_in),
        [
            shape((2 * size, feat_grp), BF),
            shape((samp, feat_grp), BF),
            shape((strip, LANES), BF),
        ],
        2 * 64 * tok * feat_grp,
        limit=56,
    )
    rows = lax.all_to_all(jnp.broadcast_to(rows, (n_col,) + rows.shape), "col", 0, 0)
    turn = [(g * n_row + r, n_grp * r + g) for g in range(n_grp) for r in range(n_row)]
    block = lax.ppermute(block, ("grp", "row"), turn)
    parts = call(
        first_kernel,
        (tokens_in, act_inverse),
        [shape((n_row, out_rows, tok), BF)],
        2 * feat_grp * feat_row * tok,
        [
            pltpu.VMEM(tokens_in.shape, BF),
            pltpu.VMEM(act_inverse.shape, BF),
            pltpu.SemaphoreType.DMA((5,)),
        ],
        pl.BlockSpec(memory_space=pl.ANY),
        limit=56,
    )[0]
    payload = jnp.concatenate(
        [parts, jnp.broadcast_to(block, (n_row,) + block.shape)], axis=1
    )
    first = lax.all_to_all(payload, "row", 0, 0)

    half = n_col * size
    keep, give = call(
        right_kernel,
        (grad_inverse, samples, rows),
        [shape((half + samp // 2, width), F32), shape((half + samp // 2, width), BF)],
        4 * n_col * size * feat_grp * width,
        [pltpu.VMEM((n_col, 2, size, width), F32)],
    )
    owner = lax.axis_index("row") // 4
    grp = lax.axis_index("grp")
    taken = lax.ppermute(give, "grp", [(i, i ^ 1) for i in range(n_grp)]).astype(F32)
    own_y = jnp.where(grp % 2 == owner % 2, keep[half:], taken[half:])
    keep = jnp.concatenate([keep[:half] + taken[:half], own_y], axis=0)
    taken = lax.ppermute(keep.astype(BF), "grp", [(i, i ^ 2) for i in range(n_grp)]).astype(F32)
    own_y = jnp.where(grp // 2 == owner // 2, keep[half:], taken[half:]).astype(BF)
    right = (keep[:half] + taken[:half]).astype(BF)
    rights = [right] + [
        lax.ppermute(right, "row", [(i, (i + j) % n_row) for i in range(n_row)])
        for j in SHIFTS[1:]
    ]
    other = lax.ppermute(
        jnp.concatenate(rights, axis=0), "grp", [(i, i ^ 1) for i in range(n_grp)]
    )

    send = call(
        second_kernel,
        (sample_rows, first, own_y, tokens_in),
        [shape((n_col, out_rows + strip * n_row + samp, LANES), BF)],
        2 * samp * tok * feat_row,
    )[0]
    got = lax.all_to_all(send, "col", 0, 0)

    unused, samples = lax.optimization_barrier((send, samples))
    beside = lax.ppermute(samples, "col", [(i, (i + 4) % n_col) for i in range(n_col)])
    samples = jnp.concatenate([samples, beside], axis=0)
    pairs = [samples] + [
        lax.ppermute(samples, "col", [(i, i - i % 4 + (i + k) % 4) for i in range(n_col)])
        for k in range(1, 4)
    ]

    precond = call(
        final_kernel,
        (got, other, *rights),
        [shape((out_rows, width), F32)],
        2 * out_rows * n_col * tok * width,
        [pltpu.VMEM((n_col, 2, spread, size, width), BF)],
    )[0]
    act_cov, grad_cov = call(
        factor_kernel,
        (got, *pairs),
        [shape((tile, feat_grp), F32)] * 2,
        4 * LANES * samp * n_col * feat_grp,
    )
    return (precond, act_cov, grad_cov)


def solution(mesh):
    return jax.shard_map(
        body,
        mesh=mesh,
        in_specs=(P("col", "row"), P("col", "grp"), P("col"), P("grp", "row"), P("grp", "col")),
        out_specs=(P(("grp", "row"), "col"), P(("row", "col"), "grp"), P(("row", "col"), "grp")),
        check_vma=False,
    )
```

```python
import functools

import jax
import jax.numpy as jnp
from jax import lax
from jax.experimental import pallas as pl
from jax.experimental.pallas import tpu as pltpu
from jax.sharding import PartitionSpec as P

BF = jnp.bfloat16
F32 = jnp.float32
LANES = 128
FIRST = (((0,), (0,)), ((), ()))
LAST = (((1,), (1,)), ((), ()))
SMEM = pl.BlockSpec(memory_space=pltpu.SMEM)
VMEM = pl.BlockSpec(memory_space=pltpu.VMEM)
PLANES = 2


def call(kernel, inputs, outs, flops, scratch=(), place=VMEM, limit=16):
    moved = sum(x.size * x.dtype.itemsize for x in list(inputs) + list(outs))
    return pl.pallas_call(
        kernel,
        out_shape=outs,
        in_specs=[SMEM if x.dtype == jnp.int32 else place for x in inputs],
        out_specs=[VMEM] * len(outs),
        scratch_shapes=list(scratch),
        compiler_params=pltpu.CompilerParams(vmem_limit_bytes=limit * 1024 * 1024),
        cost_estimate=pl.CostEstimate(flops=flops, bytes_accessed=moved, transcendentals=0),
    )(*inputs)


def source_of(k):
    col = lax.axis_index("col")
    return 4 * ((col // 4) ^ (k % 2)) + lax.rem(col % 4 - k // 2 + 4, 4)


def own_picks(picks, count, tok):
    begin = lax.axis_index("grp") * count
    first = lax.axis_index("col") * tok
    return [picks[begin + i] - first for i in range(count)]


def rows_hot(targets, tok):
    shape = (len(targets), tok)
    sub = lax.broadcasted_iota(jnp.int32, shape, 0)
    lane = lax.broadcasted_iota(jnp.int32, shape, 1)
    want = jnp.zeros(shape, jnp.int32)
    for i, target in enumerate(targets):
        want = jnp.where(sub == i, target, want)
    return jnp.where(want == lane, 1.0, 0.0).astype(BF)


def first_kernel(picks, x_hbm, a_hbm, out_ref, x_ref, a_ref, sems):
    n_row, depth, tok = out_ref.shape
    parts = sems.shape[0] - 1
    step = a_ref.shape[0] // parts
    copies = [pltpu.make_async_copy(x_hbm, x_ref, sems.at[parts])]
    for p in range(parts):
        span = pl.ds(p * step, step)
        copies.append(pltpu.make_async_copy(a_hbm.at[span], a_ref.at[span], sems.at[p]))
    for copy in copies:
        copy.start()
    out_rows = a_ref.shape[0] // n_row
    quarter = picks.shape[0] // 4
    hot = rows_hot(own_picks(picks, quarter, tok), tok)
    copies[0].wait()
    chosen = jnp.dot(hot, x_ref[...], preferred_element_type=F32)
    strips = [chosen[:, k : k + LANES] for k in range(0, chosen.shape[1], LANES)]
    block = jnp.concatenate(strips, axis=0).astype(BF)
    out_ref[:, out_rows:, :] = jnp.broadcast_to(block[None], (n_row,) + block.shape)
    each = step // out_rows
    for p in range(parts):
        copies[p + 1].wait()
        rows = a_ref[p * step : (p + 1) * step, :]
        part = lax.dot_general(rows, x_ref[...], LAST, preferred_element_type=F32)
        out_ref[p * each : (p + 1) * each, :out_rows, :] = part.astype(BF).reshape(
            each, out_rows, tok
        )


def pick_kernel(picks, g_ref, out_ref):
    tok = g_ref.shape[0]
    samp = picks.shape[0]
    plane = lax.axis_index("row") % PLANES
    first = lax.axis_index("col") * tok
    count = out_ref.shape[0] - samp
    size = count // 2
    ours = [tok // 2 * (i // size) + size * plane + i % size for i in range(count)]
    hot = rows_hot(ours + [picks[i] - first for i in range(samp)], tok)
    out_ref[...] = jnp.dot(hot, g_ref[...], preferred_element_type=F32).astype(BF)


def side_kernel(picks, x_ref, gy_ref, out_ref):
    n_col, depth, unused = out_ref.shape
    tok, feat = x_ref.shape
    samp = picks.shape[0]
    tile = feat // n_col
    quarter = samp // 4
    hot = rows_hot(own_picks(picks, quarter, tok), tok)
    chosen = jnp.dot(hot, x_ref[...], preferred_element_type=F32)
    begin = pl.multiple_of((lax.axis_index("row") % 4) * feat, LANES)
    own = gy_ref[gy_ref.shape[0] - samp :, pl.ds(begin, feat)].astype(F32)
    empty = jnp.zeros((samp - 3 * quarter, 16), F32)
    for c in range(n_col):
        at = c * tile
        top = own[:, at : at + 32]
        cuts = [chosen[:, at + k : at + k + 16] for k in range(0, tile, 16)]
        low = jnp.concatenate(
            [own[:, at + 32 : at + tile], jnp.concatenate(cuts + [empty], axis=0)], axis=1
        )
        block = jnp.concatenate([top, low], axis=0)
        block = jnp.concatenate([jnp.zeros((depth, LANES - 32), F32), block], axis=1)
        out_ref[c] = block.astype(BF)


def right_kernel(b_ref, *refs):
    blocks, keep_ref, give_ref, held = refs[:-3], refs[-3], refs[-2], refs[-1]
    n_blk, unused, size, width = held.shape
    rows = jnp.concatenate([block[...] for block in blocks], axis=0)
    term = jnp.dot(rows, b_ref[...], preferred_element_type=F32)
    held[...] = term.reshape(held.shape)
    core = lax.axis_index("grp") % 2
    keep_ref[...] = held[:, core].reshape(n_blk * size, width).astype(BF)
    give_ref[...] = held[:, 1 - core].reshape(n_blk * size, width).astype(BF)


def second_kernel(got_ref, side_ref, out_ref):
    n_grp, n_col, unused, unused = out_ref.shape
    n_row, depth, tok = got_ref.shape
    strip = depth - (depth // 32) * 32
    out_rows = depth - strip
    total = got_ref[0, :out_rows, :].astype(F32)
    for r in range(1, n_row):
        total = total + got_ref[r, :out_rows, :].astype(F32)
    total = jnp.concatenate([total, jnp.zeros((LANES - out_rows, tok), F32)], axis=0)
    turned = jnp.transpose(total).astype(BF)
    size = tok // 2
    per = n_row // n_grp
    x_rows = per * strip
    for g in range(n_grp):
        u_block = turned[(g % 2) * size : (g % 2 + 1) * size]
        x_block = got_ref[g * per : (g + 1) * per, out_rows:, :].astype(F32)
        x_block = x_block.reshape(x_rows, tok).astype(BF)
        for c in range(n_col):
            out_ref[g, c, :size, :] = u_block + side_ref[c]
            out_ref[g, c, size:, :] = x_block


def final_kernel(got_ref, *refs):
    v_refs, out_ref, held = refs[:-2], refs[-2], refs[-1]
    n_col, spread, size, width = held.shape
    n_grp, out_rows, unused = out_ref.shape
    row = lax.axis_index("row")
    for j in range(spread):
        for k in range(n_col):
            span = slice(k * size, (k + 1) * size)
            held[source_of(k), lax.rem(row + j, spread)] = v_refs[j][span, :]
    tokens = n_col * spread * size
    right = held[...].reshape(tokens, width)
    for g in range(n_grp):
        left = got_ref[g, :, : spread * size, :].reshape(tokens, LANES)
        term = lax.dot_general(left, right, FIRST, preferred_element_type=F32)
        out_ref[g] = term[:out_rows].astype(BF)


def factor_kernel(got_ref, *refs):
    blocks, act_ref, grad_ref = refs[:-2], refs[-2], refs[-1]
    n_grp, n_col, depth, unused = got_ref.shape
    tile, width = act_ref.shape
    samp = blocks[0].shape[0] // 2
    quarter = samp // n_grp
    total = samp * n_col
    scale = 1.0 / total
    begin = depth - quarter * (width // LANES)
    span = got_ref[:, :, begin:, :].astype(F32)
    strips = []
    for t in range(width // LANES):
        strip = span[:, :, t * quarter : (t + 1) * quarter, :].reshape(total, LANES)
        strips.append(strip.astype(BF))
    right = jnp.concatenate(strips, axis=1)
    lefts = got_ref[:, :, samp : 2 * samp, :].astype(F32)
    for k in range(tile // 16):
        left = lefts[:, :, k * quarter : (k + 1) * quarter, :].reshape(total, LANES).astype(BF)
        term = lax.dot_general(left, right, FIRST, preferred_element_type=F32)
        act_ref[16 * k : 16 * (k + 1), :] = term[LANES - 16 :] * scale
    owner = lax.axis_index("row") // 4
    sides = [got_ref[owner, source_of(k), : 2 * samp, :] for k in range(n_col)]
    right = jnp.concatenate([block[...] for block in blocks], axis=0)
    left = jnp.concatenate([side[:samp] for side in sides], axis=0)
    term = lax.dot_general(left, right, FIRST, preferred_element_type=F32)
    grad_ref[:32, :] = term[LANES - 32 :] * scale
    left = jnp.concatenate([side[samp:] for side in sides], axis=0)
    term = lax.dot_general(left, right, FIRST, preferred_element_type=F32)
    grad_ref[32:, :] = term[LANES - 32 : LANES - 16] * scale


def body(tokens_in, cotangent, sample_rows, act_inverse, grad_inverse):
    n_row = lax.axis_size("row")
    n_col = lax.axis_size("col")
    n_grp = lax.axis_size("grp")
    tok, feat_row = tokens_in.shape
    feat_grp = cotangent.shape[1]
    width = grad_inverse.shape[1]
    samp = sample_rows.shape[0]
    quarter = samp // n_grp
    tile = feat_row // n_col
    out_rows = feat_grp // n_row
    strip = quarter * feat_row // LANES
    spread = PLANES
    size = tok // 2 // spread
    shape = jax.ShapeDtypeStruct

    payload = call(
        first_kernel,
        (sample_rows, tokens_in, act_inverse),
        [shape((n_row, out_rows + strip, tok), BF)],
        2 * feat_grp * feat_row * tok,
        [
            pltpu.VMEM(tokens_in.shape, BF),
            pltpu.VMEM(act_inverse.shape, BF),
            pltpu.SemaphoreType.DMA((5,)),
        ],
        pl.BlockSpec(memory_space=pl.ANY),
        limit=56,
    )[0]
    first = lax.all_to_all(payload, "row", 0, 0)

    def along_y(block, k):
        return lax.ppermute(
            block, "col", [(i, i - i % 4 + (i + k) % 4) for i in range(n_col)]
        )

    picked = call(
        pick_kernel,
        (sample_rows, cotangent),
        [shape((2 * size + samp, feat_grp), BF)],
        2 * 64 * tok * feat_grp,
    )[0]
    beside = lax.ppermute(picked, "col", [(i, (i + 4) % n_col) for i in range(n_col)])
    cut = 2 * size
    pair = jnp.concatenate([picked[:cut], beside[:cut]], axis=0)
    pairs = [pair] + [along_y(pair, k) for k in range(1, 4)]
    keep, give = call(
        right_kernel,
        (grad_inverse, *pairs),
        [shape((n_col * size, width), BF)] * 2,
        4 * n_col * size * feat_grp * width,
        [pltpu.VMEM((n_col, 2, size, width), F32)],
    )
    first, unused = lax.optimization_barrier((first, (pairs[1], pairs[3])))
    taken = lax.ppermute(give, "grp", [(i, i ^ 1) for i in range(n_grp)])
    right = (keep.astype(F32) + taken.astype(F32)).astype(BF)
    rights = [right, lax.ppermute(right, "row", [(i, i ^ 1) for i in range(n_row)])]
    unused, picked_y, beside_y = lax.optimization_barrier((taken, picked[cut:], beside[cut:]))
    samples = jnp.concatenate([picked_y, beside_y], axis=0)
    samples = [samples] + [along_y(samples, k) for k in range(1, 4)]
    side = call(
        side_kernel,
        (sample_rows, tokens_in, picked),
        [shape((n_col, 2 * samp, LANES), BF)],
        2 * samp * tok * feat_row,
    )[0]
    send = call(
        second_kernel,
        (first, side),
        [shape((n_grp, n_col, size * spread + strip * n_row // n_grp, LANES), BF)],
        1000000,
    )[0]
    got = lax.all_to_all(send.reshape((n_grp * n_col,) + send.shape[2:]), ("grp", "col"), 0, 0)
    got = got.reshape(send.shape)

    rights, samples = lax.optimization_barrier((rights, samples))
    term = call(
        final_kernel,
        (got, *rights),
        [shape((n_grp, out_rows, width), BF)],
        2 * n_grp * LANES * n_col * spread * size * width,
        [pltpu.VMEM((n_col, spread, size, width), BF)],
    )[0]
    got, unused = lax.optimization_barrier((got, term))
    term = lax.all_to_all(term, "grp", 0, 0)
    precond = jnp.sum(term.astype(F32), axis=0)
    act_cov, grad_cov = call(
        factor_kernel,
        (got, *samples),
        [shape((tile, feat_grp), F32)] * 2,
        4 * LANES * samp * n_col * feat_grp,
    )
    return (precond, act_cov, grad_cov)


def solution(mesh):
    return jax.shard_map(
        body,
        mesh=mesh,
        in_specs=(P("col", "row"), P("col", "grp"), P("col"), P("grp", "row"), P("grp", "col")),
        out_specs=(P(("grp", "row"), "col"), P(("row", "col"), "grp"), P(("row", "col"), "grp")),
        check_vma=False,
    )
```

```python
import functools

import jax
import jax.numpy as jnp
from jax import lax
from jax.experimental import pallas as pl
from jax.experimental.pallas import tpu as pltpu
from jax.sharding import PartitionSpec as P

BF = jnp.bfloat16
F32 = jnp.float32
LANES = 128
FIRST = (((0,), (0,)), ((), ()))
LAST = (((1,), (1,)), ((), ()))
SMEM = pl.BlockSpec(memory_space=pltpu.SMEM)
VMEM = pl.BlockSpec(memory_space=pltpu.VMEM)
PLANES = 4
SHIFTS = (0, 2, 1, -1)


def call(kernel, inputs, outs, flops, scratch=(), places=None, limit=16):
    places = places or [SMEM if x.dtype == jnp.int32 else VMEM for x in inputs]
    moved = sum(x.size * x.dtype.itemsize for x in list(inputs) + list(outs))
    return pl.pallas_call(
        kernel,
        out_shape=outs,
        in_specs=places,
        out_specs=[VMEM] * len(outs),
        scratch_shapes=list(scratch),
        compiler_params=pltpu.CompilerParams(vmem_limit_bytes=limit * 1024 * 1024),
        cost_estimate=pl.CostEstimate(flops=flops, bytes_accessed=moved, transcendentals=0),
    )(*inputs)


def source_of(k):
    col = lax.axis_index("col")
    return 4 * ((col // 4) ^ (k % 2)) + lax.rem(col % 4 - k // 2 + 4, 4)


def own_picks(picks, count, tok):
    begin = lax.axis_index("grp") * count
    first = lax.axis_index("col") * tok
    return [picks[begin + i] - first for i in range(count)]


def rows_hot(targets, tok):
    shape = (len(targets), tok)
    sub = lax.broadcasted_iota(jnp.int32, shape, 0)
    lane = lax.broadcasted_iota(jnp.int32, shape, 1)
    want = jnp.zeros(shape, jnp.int32)
    for i, target in enumerate(targets):
        want = jnp.where(sub == i, target, want)
    return jnp.where(want == lane, 1.0, 0.0).astype(BF)


def first_kernel(picks, x_hbm, a_hbm, out_ref, x_ref, a_ref, sems):
    n_row, depth, tok = out_ref.shape
    parts = sems.shape[0] - 1
    step = a_ref.shape[0] // parts
    copies = [pltpu.make_async_copy(x_hbm, x_ref, sems.at[parts])]
    for p in range(parts):
        span = pl.ds(p * step, step)
        copies.append(pltpu.make_async_copy(a_hbm.at[span], a_ref.at[span], sems.at[p]))
    for copy in copies:
        copy.start()
    out_rows = a_ref.shape[0] // n_row
    quarter = picks.shape[0] // 4
    hot = rows_hot(own_picks(picks, quarter, tok), tok)
    copies[0].wait()
    chosen = jnp.dot(hot, x_ref[...], preferred_element_type=F32)
    strips = [chosen[:, k : k + LANES] for k in range(0, chosen.shape[1], LANES)]
    block = jnp.concatenate(strips, axis=0).astype(BF)
    out_ref[:, out_rows:, :] = jnp.broadcast_to(block[None], (n_row,) + block.shape)
    each = step // out_rows
    for p in range(parts):
        copies[p + 1].wait()
        rows = a_ref[p * step : (p + 1) * step, :]
        part = lax.dot_general(rows, x_ref[...], LAST, preferred_element_type=F32)
        out_ref[p * each : (p + 1) * each, :out_rows, :] = part.astype(BF).reshape(
            each, out_rows, tok
        )


def pick_kernel(picks, g_ref, out_ref):
    tok = g_ref.shape[0]
    samp = picks.shape[0]
    plane = lax.axis_index("row") % PLANES
    first = lax.axis_index("col") * tok
    count = out_ref.shape[0] - samp
    size = count // 2
    ours = [tok // 2 * (i // size) + size * plane + i % size for i in range(count)]
    hot = rows_hot(ours + [picks[i] - first for i in range(samp)], tok)
    out_ref[...] = jnp.dot(hot, g_ref[...], preferred_element_type=F32).astype(BF)


def side_kernel(picks, x_ref, gy_ref, out_ref):
    n_col, depth, unused = out_ref.shape
    tok, feat = x_ref.shape
    samp = picks.shape[0]
    tile = feat // n_col
    quarter = samp // 4
    hot = rows_hot(own_picks(picks, quarter, tok), tok)
    chosen = jnp.dot(hot, x_ref[...], preferred_element_type=F32)
    begin = pl.multiple_of((lax.axis_index("row") % 4) * feat, LANES)
    own = gy_ref[gy_ref.shape[0] - samp :, pl.ds(begin, feat)].astype(F32)
    empty = jnp.zeros((samp - 3 * quarter, 16), F32)
    for c in range(n_col):
        at = c * tile
        top = own[:, at : at + 32]
        cuts = [chosen[:, at + k : at + k + 16] for k in range(0, tile, 16)]
        low = jnp.concatenate(
            [own[:, at + 32 : at + tile], jnp.concatenate(cuts + [empty], axis=0)], axis=1
        )
        block = jnp.concatenate([top, low], axis=0)
        block = jnp.concatenate([jnp.zeros((depth, LANES - 32), F32), block], axis=1)
        out_ref[c] = block.astype(BF)


def rows_of(block, begin, count):
    step = block.shape[0] // 2
    begin = begin if step > count else 0
    return [block[at : at + count, :] for at in (begin, step + begin)]


def right_kernel(b_hbm, *refs):
    blocks, keep_ref, give_ref, held, b_ref, sems = refs[:-5], *refs[-5:]
    n_blk, unused, size, width = held.shape
    parts = sems.shape[0]
    step = b_ref.shape[0] // parts
    spans = [pl.ds(p * step, step) for p in range(parts)]
    copies = [
        pltpu.make_async_copy(b_hbm.at[span], b_ref.at[span], sems.at[p])
        for p, span in enumerate(spans)
    ]
    for copy in copies:
        copy.start()
    rows = [piece for block in blocks for piece in rows_of(block, 0, 2 * size)]
    rows = jnp.concatenate(rows, axis=0)
    term = None
    for p in range(parts):
        copies[p].wait()
        left = rows[:, p * step : (p + 1) * step]
        part = jnp.dot(left, b_ref[spans[p], :], preferred_element_type=F32)
        term = part if term is None else term + part
    held[...] = term.reshape(held.shape)
    core = lax.axis_index("grp") % 2
    keep_ref[...] = held[:, core].reshape(n_blk * size, width).astype(BF)
    give_ref[...] = held[:, 1 - core].reshape(n_blk * size, width).astype(BF)


def second_kernel(got_ref, side_ref, out_ref):
    n_grp, n_col, unused, unused = out_ref.shape
    n_row, depth, tok = got_ref.shape
    strip = depth - (depth // 32) * 32
    out_rows = depth - strip
    total = got_ref[0, :out_rows, :].astype(F32)
    for r in range(1, n_row):
        total = total + got_ref[r, :out_rows, :].astype(F32)
    total = jnp.concatenate([total, jnp.zeros((LANES - out_rows, tok), F32)], axis=0)
    turned = jnp.transpose(total).astype(BF)
    size = tok // 2
    per = n_row // n_grp
    x_rows = per * strip
    for g in range(n_grp):
        u_block = turned[(g % 2) * size : (g % 2 + 1) * size]
        x_block = got_ref[g * per : (g + 1) * per, out_rows:, :].astype(F32)
        x_block = x_block.reshape(x_rows, tok).astype(BF)
        for c in range(n_col):
            out_ref[g, c, :size, :] = u_block + side_ref[c]
            out_ref[g, c, size:, :] = x_block


def final_kernel(got_ref, *refs):
    v_refs, out_ref, held = refs[:-2], refs[-2], refs[-1]
    n_col, spread, size, width = held.shape
    n_grp, out_rows, unused = out_ref.shape
    row = lax.axis_index("row")
    for j, shift in enumerate(SHIFTS):
        plane = lax.rem(row - shift + spread, spread)
        for k in range(n_col):
            held[source_of(k), plane] = v_refs[j][k * size : (k + 1) * size, :]
    tokens = n_col * spread * size
    right = held[...].reshape(tokens, width)
    for g in range(n_grp):
        left = got_ref[g, :, : spread * size, :].reshape(tokens, LANES)
        term = lax.dot_general(left, right, FIRST, preferred_element_type=F32)
        out_ref[g] = term[:out_rows].astype(BF)


def factor_kernel(got_ref, *refs):
    blocks, act_ref, grad_ref = refs[:-2], refs[-2], refs[-1]
    n_grp, n_col, depth, unused = got_ref.shape
    tile, width = act_ref.shape
    samp = blocks[0].shape[0] // 4
    quarter = samp // n_grp
    total = samp * n_col
    scale = 1.0 / total
    begin = depth - quarter * (width // LANES)
    span = got_ref[:, :, begin:, :].astype(F32)
    strips = []
    for t in range(width // LANES):
        strip = span[:, :, t * quarter : (t + 1) * quarter, :].reshape(total, LANES)
        strips.append(strip.astype(BF))
    right = jnp.concatenate(strips, axis=1)
    lefts = got_ref[:, :, samp : 2 * samp, :].astype(F32)
    for k in range(tile // 16):
        left = lefts[:, :, k * quarter : (k + 1) * quarter, :].reshape(total, LANES).astype(BF)
        term = lax.dot_general(left, right, FIRST, preferred_element_type=F32)
        act_ref[16 * k : 16 * (k + 1), :] = term[LANES - 16 :] * scale
    owner = lax.axis_index("row") // 4
    sides = [got_ref[owner, source_of(k), : 2 * samp, :] for k in range(n_col)]
    rights = [piece for block in blocks for piece in rows_of(block, samp, samp)]
    right = jnp.concatenate(rights, axis=0)
    left = jnp.concatenate([side[:samp] for side in sides], axis=0)
    term = lax.dot_general(left, right, FIRST, preferred_element_type=F32)
    grad_ref[:32, :] = term[LANES - 32 :] * scale
    left = jnp.concatenate([side[samp:] for side in sides], axis=0)
    term = lax.dot_general(left, right, FIRST, preferred_element_type=F32)
    grad_ref[32:, :] = term[LANES - 32 : LANES - 16] * scale


def body(tokens_in, cotangent, sample_rows, act_inverse, grad_inverse):
    n_row = lax.axis_size("row")
    n_col = lax.axis_size("col")
    n_grp = lax.axis_size("grp")
    tok, feat_row = tokens_in.shape
    feat_grp = cotangent.shape[1]
    width = grad_inverse.shape[1]
    samp = sample_rows.shape[0]
    quarter = samp // n_grp
    tile = feat_row // n_col
    out_rows = feat_grp // n_row
    strip = quarter * feat_row // LANES
    spread = PLANES
    size = tok // 2 // spread
    shape = jax.ShapeDtypeStruct

    payload = call(
        first_kernel,
        (sample_rows, tokens_in, act_inverse),
        [shape((n_row, out_rows + strip, tok), BF)],
        2 * feat_grp * feat_row * tok,
        [
            pltpu.VMEM(tokens_in.shape, BF),
            pltpu.VMEM(act_inverse.shape, BF),
            pltpu.SemaphoreType.DMA((5,)),
        ],
        [SMEM] + [pl.BlockSpec(memory_space=pl.ANY)] * 2,
        limit=56,
    )[0]
    first = lax.all_to_all(payload, "row", 0, 0)

    def along_y(block, k):
        return lax.ppermute(
            block, "col", [(i, i - i % 4 + (i + k) % 4) for i in range(n_col)]
        )

    picked = call(
        pick_kernel,
        (sample_rows, cotangent),
        [shape((2 * size + samp, feat_grp), BF)],
        2 * 64 * tok * feat_grp,
    )[0]
    beside = lax.ppermute(picked, "col", [(i, (i + 4) % n_col) for i in range(n_col)])
    cut = 2 * size
    pair = jnp.concatenate([picked, beside], axis=0)
    rows = jnp.concatenate([picked[:cut], beside[:cut]], axis=0)
    near = {k: along_y(pair, k) for k in (1, 3)}
    pairs = [pair, near[1], along_y(rows, 2), near[3]]
    keep, give = call(
        right_kernel,
        (grad_inverse, *pairs),
        [shape((n_col * size, width), BF)] * 2,
        4 * n_col * size * feat_grp * width,
        [
            pltpu.VMEM((n_col, 2, size, width), F32),
            pltpu.VMEM(grad_inverse.shape, BF),
            pltpu.SemaphoreType.DMA((4,)),
        ],
        places=[pl.BlockSpec(memory_space=pl.ANY)] + [VMEM] * 4,
    )
    first, unused = lax.optimization_barrier((first, give))
    taken = lax.ppermute(give, "grp", [(i, i ^ 1) for i in range(n_grp)])
    right = (keep.astype(F32) + taken.astype(F32)).astype(BF)
    rights = [right] + [
        lax.ppermute(right, "row", [(i, (i + j) % n_row) for i in range(n_row)])
        for j in SHIFTS[1:]
    ]
    side = call(
        side_kernel,
        (sample_rows, tokens_in, picked),
        [shape((n_col, 2 * samp, LANES), BF)],
        2 * samp * tok * feat_row,
    )[0]
    send = call(
        second_kernel,
        (first, side),
        [shape((n_grp, n_col, size * spread + strip * n_row // n_grp, LANES), BF)],
        1000000,
    )[0]
    got = lax.all_to_all(send.reshape((n_grp * n_col,) + send.shape[2:]), ("grp", "col"), 0, 0)
    got = got.reshape(send.shape)

    term = call(
        final_kernel,
        (got, *rights),
        [shape((n_grp, out_rows, width), BF)],
        2 * n_grp * LANES * n_col * spread * size * width,
        [pltpu.VMEM((n_col, spread, size, width), BF)],
    )[0]
    got, picked, beside, unused = lax.optimization_barrier((got, picked, beside, term))
    term = lax.all_to_all(term, "grp", 0, 0)
    far = along_y(jnp.concatenate([picked[cut:], beside[cut:]], axis=0), 2)
    precond = jnp.sum(term.astype(F32), axis=0)
    act_cov, grad_cov = call(
        factor_kernel,
        (got, pair, near[1], far, near[3]),
        [shape((tile, feat_grp), F32)] * 2,
        4 * LANES * samp * n_col * feat_grp,
    )
    return (precond, act_cov, grad_cov)


def solution(mesh):
    return jax.shard_map(
        body,
        mesh=mesh,
        in_specs=(P("col", "row"), P("col", "grp"), P("col"), P("grp", "row"), P("grp", "col")),
        out_specs=(P(("grp", "row"), "col"), P(("row", "col"), "grp"), P(("row", "col"), "grp")),
        check_vma=False,
    )
```

```python
import functools

import jax
import jax.numpy as jnp
from jax import lax
from jax.experimental import pallas as pl
from jax.experimental.pallas import tpu as pltpu
from jax.sharding import PartitionSpec as P

BF = jnp.bfloat16
F32 = jnp.float32
LANES = 128
FIRST = (((0,), (0,)), ((), ()))
LAST = (((1,), (1,)), ((), ()))
SMEM = pl.BlockSpec(memory_space=pltpu.SMEM)
VMEM = pl.BlockSpec(memory_space=pltpu.VMEM)
PLANES = 4
SHIFTS = (0, 2, 1, -1)


def call(kernel, inputs, outs, flops, scratch=(), places=None, limit=16):
    places = places or [SMEM if x.dtype == jnp.int32 else VMEM for x in inputs]
    moved = sum(x.size * x.dtype.itemsize for x in list(inputs) + list(outs))
    return pl.pallas_call(
        kernel,
        out_shape=outs,
        in_specs=places,
        out_specs=[VMEM] * len(outs),
        scratch_shapes=list(scratch),
        compiler_params=pltpu.CompilerParams(vmem_limit_bytes=limit * 1024 * 1024),
        cost_estimate=pl.CostEstimate(flops=flops, bytes_accessed=moved, transcendentals=0),
    )(*inputs)


def source_of(k):
    col = lax.axis_index("col")
    return 4 * ((col // 4) ^ (k % 2)) + lax.rem(col % 4 - k // 2 + 4, 4)


def own_picks(picks, count, tok):
    begin = lax.axis_index("grp") * count
    first = lax.axis_index("col") * tok
    return [picks[begin + i] - first for i in range(count)]


def rows_hot(targets, tok):
    shape = (len(targets), tok)
    sub = lax.broadcasted_iota(jnp.int32, shape, 0)
    lane = lax.broadcasted_iota(jnp.int32, shape, 1)
    want = jnp.zeros(shape, jnp.int32)
    for i, target in enumerate(targets):
        want = jnp.where(sub == i, target, want)
    return jnp.where(want == lane, 1.0, 0.0).astype(BF)


def first_kernel(picks, x_hbm, a_hbm, out_ref, x_ref, a_ref, sems):
    n_row, depth, tok = out_ref.shape
    parts = sems.shape[0] - 1
    step = a_ref.shape[0] // parts
    copies = [pltpu.make_async_copy(x_hbm, x_ref, sems.at[parts])]
    for p in range(parts):
        span = pl.ds(p * step, step)
        copies.append(pltpu.make_async_copy(a_hbm.at[span], a_ref.at[span], sems.at[p]))
    for copy in copies:
        copy.start()
    out_rows = a_ref.shape[0] // n_row
    quarter = picks.shape[0] // 4
    hot = rows_hot(own_picks(picks, quarter, tok), tok)
    copies[0].wait()
    chosen = jnp.dot(hot, x_ref[...], preferred_element_type=F32)
    strips = [chosen[:, k : k + LANES] for k in range(0, chosen.shape[1], LANES)]
    block = jnp.concatenate(strips, axis=0).astype(BF)
    out_ref[:, out_rows:, :] = jnp.broadcast_to(block[None], (n_row,) + block.shape)
    each = step // out_rows
    for p in range(parts):
        copies[p + 1].wait()
        rows = a_ref[p * step : (p + 1) * step, :]
        part = lax.dot_general(rows, x_ref[...], LAST, preferred_element_type=F32)
        out_ref[p * each : (p + 1) * each, :out_rows, :] = part.astype(BF).reshape(
            each, out_rows, tok
        )


def pick_kernel(picks, g_ref, out_ref):
    tok = g_ref.shape[0]
    samp = picks.shape[0]
    plane = lax.axis_index("row") % PLANES
    first = lax.axis_index("col") * tok
    count = out_ref.shape[0] - samp
    size = count // 2
    ours = [tok // 2 * (i // size) + size * plane + i % size for i in range(count)]
    hot = rows_hot(ours + [picks[i] - first for i in range(samp)], tok)
    out_ref[...] = jnp.dot(hot, g_ref[...], preferred_element_type=F32).astype(BF)


def side_kernel(picks, x_ref, gy_ref, out_ref):
    n_col, depth, unused = out_ref.shape
    tok, feat = x_ref.shape
    samp = picks.shape[0]
    tile = feat // n_col
    quarter = samp // 4
    hot = rows_hot(own_picks(picks, quarter, tok), tok)
    chosen = jnp.dot(hot, x_ref[...], preferred_element_type=F32)
    begin = pl.multiple_of((lax.axis_index("row") % 4) * feat, LANES)
    own = gy_ref[gy_ref.shape[0] - samp :, pl.ds(begin, feat)].astype(F32)
    empty = jnp.zeros((samp - 3 * quarter, 16), F32)
    for c in range(n_col):
        at = c * tile
        top = own[:, at : at + 32]
        cuts = [chosen[:, at + k : at + k + 16] for k in range(0, tile, 16)]
        low = jnp.concatenate(
            [own[:, at + 32 : at + tile], jnp.concatenate(cuts + [empty], axis=0)], axis=1
        )
        block = jnp.concatenate([top, low], axis=0)
        block = jnp.concatenate([jnp.zeros((depth, LANES - 32), F32), block], axis=1)
        out_ref[c] = block.astype(BF)


def rows_of(block, begin, count):
    step = block.shape[0] // 2
    begin = begin if step > count else 0
    return [block[at : at + count, :] for at in (begin, step + begin)]


def right_kernel(b_hbm, *refs):
    blocks, keep_ref, give_ref, held, b_ref, sems = refs[:-5], *refs[-5:]
    n_blk, unused, size, width = held.shape
    parts = sems.shape[0]
    step = b_ref.shape[0] // parts
    spans = [pl.ds(p * step, step) for p in range(parts)]
    copies = [
        pltpu.make_async_copy(b_hbm.at[span], b_ref.at[span], sems.at[p])
        for p, span in enumerate(spans)
    ]
    for copy in copies:
        copy.start()
    rows = [piece for block in blocks for piece in rows_of(block, 0, 2 * size)]
    rows = jnp.concatenate(rows, axis=0)
    term = None
    for p in range(parts):
        copies[p].wait()
        left = rows[:, p * step : (p + 1) * step]
        part = jnp.dot(left, b_ref[spans[p], :], preferred_element_type=F32)
        term = part if term is None else term + part
    held[...] = term.reshape(held.shape)
    core = lax.axis_index("grp") % 2
    keep_ref[...] = held[:, core].reshape(n_blk * size, width).astype(BF)
    give_ref[...] = held[:, 1 - core].reshape(n_blk * size, width).astype(BF)


def second_kernel(got_ref, side_ref, out_ref):
    n_grp, n_col, unused, unused = out_ref.shape
    n_row, depth, tok = got_ref.shape
    strip = depth - (depth // 32) * 32
    out_rows = depth - strip
    total = got_ref[0, :out_rows, :].astype(F32)
    for r in range(1, n_row):
        total = total + got_ref[r, :out_rows, :].astype(F32)
    total = jnp.concatenate([total, jnp.zeros((LANES - out_rows, tok), F32)], axis=0)
    turned = jnp.transpose(total).astype(BF)
    size = tok // 2
    per = n_row // n_grp
    x_rows = per * strip
    for g in range(n_grp):
        u_block = turned[(g % 2) * size : (g % 2 + 1) * size]
        x_block = got_ref[g * per : (g + 1) * per, out_rows:, :].astype(F32)
        x_block = x_block.reshape(x_rows, tok).astype(BF)
        for c in range(n_col):
            out_ref[g, c, :size, :] = u_block + side_ref[c]
            out_ref[g, c, size:, :] = x_block


def final_kernel(got_ref, *refs):
    v_refs, own_ref, pair_ref, held = refs[:-3], refs[-3], refs[-2], refs[-1]
    n_col, spread, size, width = held.shape
    row = lax.axis_index("row")
    for j, shift in enumerate(SHIFTS):
        plane = lax.rem(row - shift + spread, spread)
        for k in range(n_col):
            held[source_of(k), plane] = v_refs[j][k * size : (k + 1) * size, :]
    tokens = n_col * spread * size
    right = held[...].reshape(tokens, width)
    grp = lax.axis_index("grp")
    for source, ref in ((grp, own_ref), (grp ^ 1, pair_ref)):
        left = got_ref[source, :, : spread * size, :].reshape(tokens, LANES)
        term = lax.dot_general(left, right, FIRST, preferred_element_type=F32)
        ref[...] = term[: ref.shape[0]].astype(ref.dtype)


def factor_kernel(got_ref, *refs):
    blocks, act_ref, grad_ref = refs[:-2], refs[-2], refs[-1]
    n_grp, n_col, depth, unused = got_ref.shape
    tile, width = act_ref.shape
    samp = blocks[0].shape[0] // 4
    quarter = samp // n_grp
    total = samp * n_col
    scale = 1.0 / total
    begin = depth - quarter * (width // LANES)
    span = got_ref[:, :, begin:, :].astype(F32)
    strips = []
    for t in range(width // LANES):
        strip = span[:, :, t * quarter : (t + 1) * quarter, :].reshape(total, LANES)
        strips.append(strip.astype(BF))
    right = jnp.concatenate(strips, axis=1)
    lefts = got_ref[:, :, samp : 2 * samp, :].astype(F32)
    for k in range(tile // 16):
        left = lefts[:, :, k * quarter : (k + 1) * quarter, :].reshape(total, LANES).astype(BF)
        term = lax.dot_general(left, right, FIRST, preferred_element_type=F32)
        act_ref[16 * k : 16 * (k + 1), :] = term[LANES - 16 :] * scale
    owner = lax.axis_index("row") // 4
    sides = [got_ref[owner, source_of(k), : 2 * samp, :] for k in range(n_col)]
    rights = [piece for block in blocks for piece in rows_of(block, samp, samp)]
    right = jnp.concatenate(rights, axis=0)
    left = jnp.concatenate([side[:samp] for side in sides], axis=0)
    term = lax.dot_general(left, right, FIRST, preferred_element_type=F32)
    grad_ref[:32, :] = term[LANES - 32 :] * scale
    left = jnp.concatenate([side[samp:] for side in sides], axis=0)
    term = lax.dot_general(left, right, FIRST, preferred_element_type=F32)
    grad_ref[32:, :] = term[LANES - 32 : LANES - 16] * scale


def body(tokens_in, cotangent, sample_rows, act_inverse, grad_inverse):
    n_row = lax.axis_size("row")
    n_col = lax.axis_size("col")
    n_grp = lax.axis_size("grp")
    tok, feat_row = tokens_in.shape
    feat_grp = cotangent.shape[1]
    width = grad_inverse.shape[1]
    samp = sample_rows.shape[0]
    quarter = samp // n_grp
    tile = feat_row // n_col
    out_rows = feat_grp // n_row
    strip = quarter * feat_row // LANES
    spread = PLANES
    size = tok // 2 // spread
    shape = jax.ShapeDtypeStruct

    payload = call(
        first_kernel,
        (sample_rows, tokens_in, act_inverse),
        [shape((n_row, out_rows + strip, tok), BF)],
        2 * feat_grp * feat_row * tok,
        [
            pltpu.VMEM(tokens_in.shape, BF),
            pltpu.VMEM(act_inverse.shape, BF),
            pltpu.SemaphoreType.DMA((5,)),
        ],
        [SMEM] + [pl.BlockSpec(memory_space=pl.ANY)] * 2,
        limit=56,
    )[0]
    first = lax.all_to_all(payload, "row", 0, 0)

    def along_y(block, k):
        return lax.ppermute(
            block, "col", [(i, i - i % 4 + (i + k) % 4) for i in range(n_col)]
        )

    picked = call(
        pick_kernel,
        (sample_rows, cotangent),
        [shape((2 * size + samp, feat_grp), BF)],
        2 * 64 * tok * feat_grp,
    )[0]
    beside = lax.ppermute(picked, "col", [(i, (i + 4) % n_col) for i in range(n_col)])
    cut = 2 * size
    pair = jnp.concatenate([picked, beside], axis=0)
    rows = jnp.concatenate([picked[:cut], beside[:cut]], axis=0)
    near = {k: along_y(pair, k) for k in (1, 3)}
    pairs = [pair, near[1], along_y(rows, 2), near[3]]
    keep, give = call(
        right_kernel,
        (grad_inverse, *pairs),
        [shape((n_col * size, width), BF)] * 2,
        4 * n_col * size * feat_grp * width,
        [
            pltpu.VMEM((n_col, 2, size, width), F32),
            pltpu.VMEM(grad_inverse.shape, BF),
            pltpu.SemaphoreType.DMA((4,)),
        ],
        places=[pl.BlockSpec(memory_space=pl.ANY)] + [VMEM] * 4,
    )
    taken = lax.ppermute(give, "grp", [(i, i ^ 1) for i in range(n_grp)])
    some = keep.astype(F32) + taken.astype(F32)
    give = some.astype(BF)
    first, give = lax.optimization_barrier((first, give))
    taken = lax.ppermute(give, "grp", [(i, i ^ 2) for i in range(n_grp)])
    right = (some + taken.astype(F32)).astype(BF)
    rights = [right] + [
        lax.ppermute(right, "row", [(i, (i + j) % n_row) for i in range(n_row)])
        for j in SHIFTS[1:]
    ]
    unused, picked_y, beside_y = lax.optimization_barrier((right, picked[cut:], beside[cut:]))
    far = along_y(jnp.concatenate([picked_y, beside_y], axis=0), 2)
    side = call(
        side_kernel,
        (sample_rows, tokens_in, picked),
        [shape((n_col, 2 * samp, LANES), BF)],
        2 * samp * tok * feat_row,
    )[0]
    send = call(
        second_kernel,
        (first, side),
        [shape((n_grp, n_col, size * spread + strip * n_row // n_grp, LANES), BF)],
        1000000,
    )[0]
    got = lax.all_to_all(send.reshape((n_grp * n_col,) + send.shape[2:]), ("grp", "col"), 0, 0)
    got = got.reshape(send.shape)

    rights, far = lax.optimization_barrier((rights, far))
    term, give = call(
        final_kernel,
        (got, *rights),
        [shape((out_rows, width), F32), shape((out_rows, width), BF)],
        4 * LANES * n_col * spread * size * width,
        [pltpu.VMEM((n_col, spread, size, width), BF)],
    )
    taken = lax.ppermute(give, "grp", [(i, i ^ 1) for i in range(n_grp)])
    precond = term + taken.astype(F32)
    got, unused = lax.optimization_barrier((got, give))
    act_cov, grad_cov = call(
        factor_kernel,
        (got, pair, near[1], far, near[3]),
        [shape((tile, feat_grp), F32)] * 2,
        4 * LANES * samp * n_col * feat_grp,
    )
    return (precond, act_cov, grad_cov)


def solution(mesh):
    return jax.shard_map(
        body,
        mesh=mesh,
        in_specs=(P("col", "row"), P("col", "grp"), P("col"), P("grp", "row"), P("grp", "col")),
        out_specs=(P(("grp", "row"), "col"), P(("row", "col"), "grp"), P(("row", "col"), "grp")),
        check_vma=False,
    )
```

```python
import functools

import jax
import jax.numpy as jnp
from jax import lax
from jax.experimental import pallas as pl
from jax.experimental.pallas import tpu as pltpu
from jax.sharding import PartitionSpec as P

BF = jnp.bfloat16
F32 = jnp.float32
LANES = 128
FIRST = (((0,), (0,)), ((), ()))
LAST = (((1,), (1,)), ((), ()))
SMEM = pl.BlockSpec(memory_space=pltpu.SMEM)
VMEM = pl.BlockSpec(memory_space=pltpu.VMEM)
PLANES = 4
SHIFTS = (0, 2, 1, -1)


def call(kernel, inputs, outs, flops, scratch=(), places=None, limit=16):
    places = places or [SMEM if x.dtype == jnp.int32 else VMEM for x in inputs]
    moved = sum(x.size * x.dtype.itemsize for x in list(inputs) + list(outs))
    return pl.pallas_call(
        kernel,
        out_shape=outs,
        in_specs=places,
        out_specs=[VMEM] * len(outs),
        scratch_shapes=list(scratch),
        compiler_params=pltpu.CompilerParams(vmem_limit_bytes=limit * 1024 * 1024),
        cost_estimate=pl.CostEstimate(flops=flops, bytes_accessed=moved, transcendentals=0),
    )(*inputs)


def source_of(k):
    col = lax.axis_index("col")
    return 4 * ((col // 4) ^ (k % 2)) + lax.rem(col % 4 - k // 2 + 4, 4)


def own_picks(picks, count, tok):
    begin = lax.axis_index("grp") * count
    first = lax.axis_index("col") * tok
    return [picks[begin + i] - first for i in range(count)]


def rows_hot(targets, tok):
    shape = (len(targets), tok)
    sub = lax.broadcasted_iota(jnp.int32, shape, 0)
    lane = lax.broadcasted_iota(jnp.int32, shape, 1)
    want = jnp.zeros(shape, jnp.int32)
    for i, target in enumerate(targets):
        want = jnp.where(sub == i, target, want)
    return jnp.where(want == lane, 1.0, 0.0).astype(BF)


def first_kernel(picks, x_hbm, a_hbm, out_ref, x_ref, a_ref, sems):
    n_row, depth, tok = out_ref.shape
    parts = sems.shape[0] - 1
    step = a_ref.shape[0] // parts
    copies = [pltpu.make_async_copy(x_hbm, x_ref, sems.at[parts])]
    for p in range(parts):
        span = pl.ds(p * step, step)
        copies.append(pltpu.make_async_copy(a_hbm.at[span], a_ref.at[span], sems.at[p]))
    for copy in copies:
        copy.start()
    out_rows = a_ref.shape[0] // n_row
    quarter = picks.shape[0] // 4
    hot = rows_hot(own_picks(picks, quarter, tok), tok)
    copies[0].wait()
    chosen = jnp.dot(hot, x_ref[...], preferred_element_type=F32)
    strips = [chosen[:, k : k + LANES] for k in range(0, chosen.shape[1], LANES)]
    block = jnp.concatenate(strips, axis=0).astype(BF)
    out_ref[:, out_rows:, :] = jnp.broadcast_to(block[None], (n_row,) + block.shape)
    each = step // out_rows
    for p in range(parts):
        copies[p + 1].wait()
        rows = a_ref[p * step : (p + 1) * step, :]
        part = lax.dot_general(rows, x_ref[...], LAST, preferred_element_type=F32)
        out_ref[p * each : (p + 1) * each, :out_rows, :] = part.astype(BF).reshape(
            each, out_rows, tok
        )


def pick_kernel(picks, g_ref, out_ref):
    tok = g_ref.shape[0]
    samp = picks.shape[0]
    plane = lax.axis_index("row") % PLANES
    first = lax.axis_index("col") * tok
    count = out_ref.shape[0] - samp
    size = count // 2
    ours = [tok // 2 * (i // size) + size * plane + i % size for i in range(count)]
    hot = rows_hot(ours + [picks[i] - first for i in range(samp)], tok)
    out_ref[...] = jnp.dot(hot, g_ref[...], preferred_element_type=F32).astype(BF)


def side_kernel(picks, x_ref, gy_ref, out_ref):
    n_col, depth, unused = out_ref.shape
    tok, feat = x_ref.shape
    samp = picks.shape[0]
    tile = feat // n_col
    quarter = samp // 4
    hot = rows_hot(own_picks(picks, quarter, tok), tok)
    chosen = jnp.dot(hot, x_ref[...], preferred_element_type=F32)
    begin = pl.multiple_of((lax.axis_index("row") % 4) * feat, LANES)
    own = gy_ref[gy_ref.shape[0] - samp :, pl.ds(begin, feat)].astype(F32)
    empty = jnp.zeros((samp - 3 * quarter, 16), F32)
    for c in range(n_col):
        at = c * tile
        top = own[:, at : at + 32]
        cuts = [chosen[:, at + k : at + k + 16] for k in range(0, tile, 16)]
        low = jnp.concatenate(
            [own[:, at + 32 : at + tile], jnp.concatenate(cuts + [empty], axis=0)], axis=1
        )
        block = jnp.concatenate([top, low], axis=0)
        block = jnp.concatenate([jnp.zeros((depth, LANES - 32), F32), block], axis=1)
        out_ref[c] = block.astype(BF)


def rows_of(block, begin, count):
    step = block.shape[0] // 2
    begin = begin if step > count else 0
    return [block[at : at + count, :] for at in (begin, step + begin)]


def right_kernel(b_ref, *refs):
    blocks, keep_ref, give_ref, held = refs[:-3], refs[-3], refs[-2], refs[-1]
    n_blk, unused, size, width = held.shape
    rows = [piece for block in blocks for piece in rows_of(block, 0, 2 * size)]
    rows = jnp.concatenate(rows, axis=0)
    term = jnp.dot(rows, b_ref[...], preferred_element_type=F32)
    held[...] = term.reshape(held.shape)
    core = lax.axis_index("grp") % 2
    keep_ref[...] = held[:, core].reshape(n_blk * size, width).astype(BF)
    give_ref[...] = held[:, 1 - core].reshape(n_blk * size, width).astype(BF)


def second_kernel(got_ref, side_ref, out_ref):
    n_grp, n_col, unused, unused = out_ref.shape
    n_row, depth, tok = got_ref.shape
    strip = depth - (depth // 32) * 32
    out_rows = depth - strip
    total = got_ref[0, :out_rows, :].astype(F32)
    for r in range(1, n_row):
        total = total + got_ref[r, :out_rows, :].astype(F32)
    total = jnp.concatenate([total, jnp.zeros((LANES - out_rows, tok), F32)], axis=0)
    turned = jnp.transpose(total).astype(BF)
    size = tok // 2
    per = n_row // n_grp
    x_rows = per * strip
    for g in range(n_grp):
        u_block = turned[(g % 2) * size : (g % 2 + 1) * size]
        x_block = got_ref[g * per : (g + 1) * per, out_rows:, :].astype(F32)
        x_block = x_block.reshape(x_rows, tok).astype(BF)
        for c in range(n_col):
            out_ref[g, c, :size, :] = u_block + side_ref[c]
            out_ref[g, c, size:, :] = x_block


def final_kernel(got_ref, *refs):
    v_refs, own_ref, pair_ref, held = refs[:-3], refs[-3], refs[-2], refs[-1]
    n_col, spread, size, width = held.shape
    row = lax.axis_index("row")
    for j, shift in enumerate(SHIFTS):
        plane = lax.rem(row - shift + spread, spread)
        for k in range(n_col):
            held[source_of(k), plane] = v_refs[j][k * size : (k + 1) * size, :]
    tokens = n_col * spread * size
    right = held[...].reshape(tokens, width)
    grp = lax.axis_index("grp")
    for source, ref in ((grp, own_ref), (grp ^ 1, pair_ref)):
        left = got_ref[source, :, : spread * size, :].reshape(tokens, LANES)
        term = lax.dot_general(left, right, FIRST, preferred_element_type=F32)
        ref[...] = term[: ref.shape[0]].astype(ref.dtype)


def factor_kernel(got_ref, *refs):
    blocks, act_ref, grad_ref = refs[:-2], refs[-2], refs[-1]
    n_grp, n_col, depth, unused = got_ref.shape
    tile, width = act_ref.shape
    samp = blocks[0].shape[0] // 4
    quarter = samp // n_grp
    total = samp * n_col
    scale = 1.0 / total
    begin = depth - quarter * (width // LANES)
    span = got_ref[:, :, begin:, :].astype(F32)
    strips = []
    for t in range(width // LANES):
        strip = span[:, :, t * quarter : (t + 1) * quarter, :].reshape(total, LANES)
        strips.append(strip.astype(BF))
    right = jnp.concatenate(strips, axis=1)
    lefts = got_ref[:, :, samp : 2 * samp, :].astype(F32)
    for k in range(tile // 16):
        left = lefts[:, :, k * quarter : (k + 1) * quarter, :].reshape(total, LANES).astype(BF)
        term = lax.dot_general(left, right, FIRST, preferred_element_type=F32)
        act_ref[16 * k : 16 * (k + 1), :] = term[LANES - 16 :] * scale
    owner = lax.axis_index("row") // 4
    sides = [got_ref[owner, source_of(k), : 2 * samp, :] for k in range(n_col)]
    rights = [piece for block in blocks for piece in rows_of(block, samp, samp)]
    right = jnp.concatenate(rights, axis=0)
    left = jnp.concatenate([side[:samp] for side in sides], axis=0)
    term = lax.dot_general(left, right, FIRST, preferred_element_type=F32)
    grad_ref[:32, :] = term[LANES - 32 :] * scale
    left = jnp.concatenate([side[samp:] for side in sides], axis=0)
    term = lax.dot_general(left, right, FIRST, preferred_element_type=F32)
    grad_ref[32:, :] = term[LANES - 32 : LANES - 16] * scale


def body(tokens_in, cotangent, sample_rows, act_inverse, grad_inverse):
    n_row = lax.axis_size("row")
    n_col = lax.axis_size("col")
    n_grp = lax.axis_size("grp")
    tok, feat_row = tokens_in.shape
    feat_grp = cotangent.shape[1]
    width = grad_inverse.shape[1]
    samp = sample_rows.shape[0]
    quarter = samp // n_grp
    tile = feat_row // n_col
    out_rows = feat_grp // n_row
    strip = quarter * feat_row // LANES
    spread = PLANES
    size = tok // 2 // spread
    shape = jax.ShapeDtypeStruct

    payload = call(
        first_kernel,
        (sample_rows, tokens_in, act_inverse),
        [shape((n_row, out_rows + strip, tok), BF)],
        2 * feat_grp * feat_row * tok,
        [
            pltpu.VMEM(tokens_in.shape, BF),
            pltpu.VMEM(act_inverse.shape, BF),
            pltpu.SemaphoreType.DMA((5,)),
        ],
        [SMEM] + [pl.BlockSpec(memory_space=pl.ANY)] * 2,
        limit=56,
    )[0]
    first = lax.all_to_all(payload, "row", 0, 0)

    def along_y(block, k):
        return lax.ppermute(
            block, "col", [(i, i - i % 4 + (i + k) % 4) for i in range(n_col)]
        )

    picked = call(
        pick_kernel,
        (sample_rows, cotangent),
        [shape((2 * size + samp, feat_grp), BF)],
        2 * 64 * tok * feat_grp,
    )[0]
    beside = lax.ppermute(picked, "col", [(i, (i + 4) % n_col) for i in range(n_col)])
    cut = 2 * size
    pair = jnp.concatenate([picked, beside], axis=0)
    rows = jnp.concatenate([picked[:cut], beside[:cut]], axis=0)
    near = {k: along_y(pair, k) for k in (1, 3)}
    pairs = [pair, near[1], along_y(rows, 2), near[3]]
    keep, give = call(
        right_kernel,
        (grad_inverse, *pairs),
        [shape((n_col * size, width), BF)] * 2,
        4 * n_col * size * feat_grp * width,
        [pltpu.VMEM((n_col, 2, size, width), F32)],
    )
    taken = lax.ppermute(give, "grp", [(i, i ^ 1) for i in range(n_grp)])
    some = keep.astype(F32) + taken.astype(F32)
    give = some.astype(BF)
    first, give = lax.optimization_barrier((first, give))
    taken = lax.ppermute(give, "grp", [(i, i ^ 2) for i in range(n_grp)])
    right = (some + taken.astype(F32)).astype(BF)
    side = call(
        side_kernel,
        (sample_rows, tokens_in, picked),
        [shape((n_col, 2 * samp, LANES), BF)],
        2 * samp * tok * feat_row,
    )[0]
    send = call(
        second_kernel,
        (first, side),
        [shape((n_grp, n_col, size * spread + strip * n_row // n_grp, LANES), BF)],
        1000000,
    )[0]
    send, right = lax.optimization_barrier((send, right))
    got = lax.all_to_all(send.reshape((n_grp * n_col,) + send.shape[2:]), ("grp", "col"), 0, 0)
    got = got.reshape(send.shape)
    rights = [right] + [
        lax.ppermute(right, "row", [(i, (i + j) % n_row) for i in range(n_row)])
        for j in SHIFTS[1:]
    ]
    unused, picked_y, beside_y = lax.optimization_barrier((right, picked[cut:], beside[cut:]))
    far = along_y(jnp.concatenate([picked_y, beside_y], axis=0), 2)

    rights, far = lax.optimization_barrier((rights, far))
    term, give = call(
        final_kernel,
        (got, *rights),
        [shape((out_rows, width), F32), shape((out_rows, width), BF)],
        4 * LANES * n_col * spread * size * width,
        [pltpu.VMEM((n_col, spread, size, width), BF)],
    )
    taken = lax.ppermute(give, "grp", [(i, i ^ 1) for i in range(n_grp)])
    precond = term + taken.astype(F32)
    got, unused = lax.optimization_barrier((got, give))
    act_cov, grad_cov = call(
        factor_kernel,
        (got, pair, near[1], far, near[3]),
        [shape((tile, feat_grp), F32)] * 2,
        4 * LANES * samp * n_col * feat_grp,
    )
    return (precond, act_cov, grad_cov)


def solution(mesh):
    return jax.shard_map(
        body,
        mesh=mesh,
        in_specs=(P("col", "row"), P("col", "grp"), P("col"), P("grp", "row"), P("grp", "col")),
        out_specs=(P(("grp", "row"), "col"), P(("row", "col"), "grp"), P(("row", "col"), "grp")),
        check_vma=False,
    )
```

```python
import functools

import jax
import jax.numpy as jnp
from jax import lax
from jax.experimental import pallas as pl
from jax.experimental.pallas import tpu as pltpu
from jax.sharding import PartitionSpec as P

BF = jnp.bfloat16
F32 = jnp.float32
LANES = 128
FIRST = (((0,), (0,)), ((), ()))
LAST = (((1,), (1,)), ((), ()))
SMEM = pl.BlockSpec(memory_space=pltpu.SMEM)
VMEM = pl.BlockSpec(memory_space=pltpu.VMEM)
PLANES = 4
SHIFTS = (0, 2, 1, -1)


def call(kernel, inputs, outs, flops, scratch=(), places=None, limit=16):
    places = places or [SMEM if x.dtype == jnp.int32 else VMEM for x in inputs]
    moved = sum(x.size * x.dtype.itemsize for x in list(inputs) + list(outs))
    return pl.pallas_call(
        kernel,
        out_shape=outs,
        in_specs=places,
        out_specs=[VMEM] * len(outs),
        scratch_shapes=list(scratch),
        compiler_params=pltpu.CompilerParams(vmem_limit_bytes=limit * 1024 * 1024),
        cost_estimate=pl.CostEstimate(flops=flops, bytes_accessed=moved, transcendentals=0),
    )(*inputs)


def source_of(k):
    col = lax.axis_index("col")
    return 4 * ((col // 4) ^ (k % 2)) + lax.rem(col % 4 - k // 2 + 4, 4)


def own_picks(picks, count, tok):
    begin = lax.axis_index("grp") * count
    first = lax.axis_index("col") * tok
    return [picks[begin + i] - first for i in range(count)]


def rows_hot(targets, tok):
    shape = (len(targets), tok)
    sub = lax.broadcasted_iota(jnp.int32, shape, 0)
    lane = lax.broadcasted_iota(jnp.int32, shape, 1)
    want = jnp.zeros(shape, jnp.int32)
    for i, target in enumerate(targets):
        want = jnp.where(sub == i, target, want)
    return jnp.where(want == lane, 1.0, 0.0).astype(BF)


def first_kernel(picks, x_hbm, a_hbm, out_ref, x_ref, a_ref, sems):
    n_row, depth, tok = out_ref.shape
    parts = sems.shape[0] - 1
    step = a_ref.shape[0] // parts
    copies = [pltpu.make_async_copy(x_hbm, x_ref, sems.at[parts])]
    for p in range(parts):
        span = pl.ds(p * step, step)
        copies.append(pltpu.make_async_copy(a_hbm.at[span], a_ref.at[span], sems.at[p]))
    for copy in copies:
        copy.start()
    out_rows = a_ref.shape[0] // n_row
    quarter = picks.shape[0] // 4
    hot = rows_hot(own_picks(picks, quarter, tok), tok)
    copies[0].wait()
    chosen = jnp.dot(hot, x_ref[...], preferred_element_type=F32)
    strips = [chosen[:, k : k + LANES] for k in range(0, chosen.shape[1], LANES)]
    block = jnp.concatenate(strips, axis=0).astype(BF)
    out_ref[:, out_rows:, :] = jnp.broadcast_to(block[None], (n_row,) + block.shape)
    each = step // out_rows
    for p in range(parts):
        copies[p + 1].wait()
        rows = a_ref[p * step : (p + 1) * step, :]
        part = lax.dot_general(rows, x_ref[...], LAST, preferred_element_type=F32)
        out_ref[p * each : (p + 1) * each, :out_rows, :] = part.astype(BF).reshape(
            each, out_rows, tok
        )


def pick_kernel(picks, g_ref, out_ref):
    tok = g_ref.shape[0]
    samp = picks.shape[0]
    plane = lax.axis_index("row") % PLANES
    first = lax.axis_index("col") * tok
    count = out_ref.shape[0] - samp
    size = count // 2
    ours = [tok // 2 * (i // size) + size * plane + i % size for i in range(count)]
    hot = rows_hot(ours + [picks[i] - first for i in range(samp)], tok)
    out_ref[...] = jnp.dot(hot, g_ref[...], preferred_element_type=F32).astype(BF)


def side_kernel(picks, x_ref, gy_ref, out_ref):
    n_col, depth, unused = out_ref.shape
    tok, feat = x_ref.shape
    samp = picks.shape[0]
    tile = feat // n_col
    quarter = samp // 4
    hot = rows_hot(own_picks(picks, quarter, tok), tok)
    chosen = jnp.dot(hot, x_ref[...], preferred_element_type=F32)
    begin = pl.multiple_of((lax.axis_index("row") % 4) * feat, LANES)
    own = gy_ref[gy_ref.shape[0] - samp :, pl.ds(begin, feat)].astype(F32)
    empty = jnp.zeros((samp - 3 * quarter, 16), F32)
    for c in range(n_col):
        at = c * tile
        top = own[:, at : at + 32]
        cuts = [chosen[:, at + k : at + k + 16] for k in range(0, tile, 16)]
        low = jnp.concatenate(
            [own[:, at + 32 : at + tile], jnp.concatenate(cuts + [empty], axis=0)], axis=1
        )
        block = jnp.concatenate([top, low], axis=0)
        block = jnp.concatenate([jnp.zeros((depth, LANES - 32), F32), block], axis=1)
        out_ref[c] = block.astype(BF)


def right_kernel(b_hbm, *refs):
    blocks, keep_ref, give_ref, held, b_ref, sems = refs[:-5], *refs[-5:]
    n_blk, unused, size, width = held.shape
    parts = sems.shape[0]
    step = b_ref.shape[0] // parts
    spans = [pl.ds(p * step, step) for p in range(parts)]
    copies = [
        pltpu.make_async_copy(b_hbm.at[span], b_ref.at[span], sems.at[p])
        for p, span in enumerate(spans)
    ]
    for copy in copies:
        copy.start()
    rows = jnp.concatenate([block[: 4 * size, :] for block in blocks], axis=0)
    term = None
    for p in range(parts):
        copies[p].wait()
        left = rows[:, p * step : (p + 1) * step]
        part = jnp.dot(left, b_ref[spans[p], :], preferred_element_type=F32)
        term = part if term is None else term + part
    held[...] = term.reshape(held.shape)
    core = lax.axis_index("grp") % 2
    keep_ref[...] = held[:, core].reshape(n_blk * size, width).astype(BF)
    give_ref[...] = held[:, 1 - core].reshape(n_blk * size, width).astype(BF)


def second_kernel(got_ref, side_ref, out_ref):
    n_grp, n_col, unused, unused = out_ref.shape
    n_row, depth, tok = got_ref.shape
    strip = depth - (depth // 32) * 32
    out_rows = depth - strip
    total = got_ref[0, :out_rows, :].astype(F32)
    for r in range(1, n_row):
        total = total + got_ref[r, :out_rows, :].astype(F32)
    total = jnp.concatenate([total, jnp.zeros((LANES - out_rows, tok), F32)], axis=0)
    turned = jnp.transpose(total).astype(BF)
    size = tok // 2
    per = n_row // n_grp
    x_rows = per * strip
    for g in range(n_grp):
        u_block = turned[(g % 2) * size : (g % 2 + 1) * size]
        x_block = got_ref[g * per : (g + 1) * per, out_rows:, :].astype(F32)
        x_block = x_block.reshape(x_rows, tok).astype(BF)
        for c in range(n_col):
            out_ref[g, c, :size, :] = u_block + side_ref[c]
            out_ref[g, c, size:, :] = x_block


def final_kernel(got_ref, *refs):
    v_refs, own_ref, pair_ref, held = refs[:-3], refs[-3], refs[-2], refs[-1]
    n_col, spread, size, width = held.shape
    row = lax.axis_index("row")
    for j, shift in enumerate(SHIFTS):
        plane = lax.rem(row - shift + spread, spread)
        for k in range(n_col):
            held[source_of(k), plane] = v_refs[j][k * size : (k + 1) * size, :]
    tokens = n_col * spread * size
    right = held[...].reshape(tokens, width)
    grp = lax.axis_index("grp")
    for source, ref in ((grp, own_ref), (grp ^ 1, pair_ref)):
        left = got_ref[source, :, : spread * size, :].reshape(tokens, LANES)
        term = lax.dot_general(left, right, FIRST, preferred_element_type=F32)
        ref[...] = term[: ref.shape[0]].astype(ref.dtype)


def factor_kernel(got_ref, *refs):
    blocks, act_ref, grad_ref = refs[:-2], refs[-2], refs[-1]
    n_grp, n_col, depth, unused = got_ref.shape
    tile, width = act_ref.shape
    samp = blocks[0].shape[0] // 4
    quarter = samp // n_grp
    total = samp * n_col
    scale = 1.0 / total
    begin = depth - quarter * (width // LANES)
    span = got_ref[:, :, begin:, :].astype(F32)
    strips = []
    for t in range(width // LANES):
        strip = span[:, :, t * quarter : (t + 1) * quarter, :].reshape(total, LANES)
        strips.append(strip.astype(BF))
    right = jnp.concatenate(strips, axis=1)
    lefts = got_ref[:, :, samp : 2 * samp, :].astype(F32)
    for k in range(tile // 16):
        left = lefts[:, :, k * quarter : (k + 1) * quarter, :].reshape(total, LANES).astype(BF)
        term = lax.dot_general(left, right, FIRST, preferred_element_type=F32)
        act_ref[16 * k : 16 * (k + 1), :] = term[LANES - 16 :] * scale
    owner = lax.axis_index("row") // 4
    sides = [got_ref[owner, source_of(k), : 2 * samp, :] for k in range(n_col)]
    rights = [block[block.shape[0] - 2 * samp :, :] for block in blocks]
    right = jnp.concatenate(rights, axis=0)
    left = jnp.concatenate([side[:samp] for side in sides], axis=0)
    term = lax.dot_general(left, right, FIRST, preferred_element_type=F32)
    grad_ref[:32, :] = term[LANES - 32 :] * scale
    left = jnp.concatenate([side[samp:] for side in sides], axis=0)
    term = lax.dot_general(left, right, FIRST, preferred_element_type=F32)
    grad_ref[32:, :] = term[LANES - 32 : LANES - 16] * scale


def body(tokens_in, cotangent, sample_rows, act_inverse, grad_inverse):
    n_row = lax.axis_size("row")
    n_col = lax.axis_size("col")
    n_grp = lax.axis_size("grp")
    tok, feat_row = tokens_in.shape
    feat_grp = cotangent.shape[1]
    width = grad_inverse.shape[1]
    samp = sample_rows.shape[0]
    quarter = samp // n_grp
    tile = feat_row // n_col
    out_rows = feat_grp // n_row
    strip = quarter * feat_row // LANES
    spread = PLANES
    size = tok // 2 // spread
    shape = jax.ShapeDtypeStruct

    payload = call(
        first_kernel,
        (sample_rows, tokens_in, act_inverse),
        [shape((n_row, out_rows + strip, tok), BF)],
        2 * feat_grp * feat_row * tok,
        [
            pltpu.VMEM(tokens_in.shape, BF),
            pltpu.VMEM(act_inverse.shape, BF),
            pltpu.SemaphoreType.DMA((5,)),
        ],
        [SMEM] + [pl.BlockSpec(memory_space=pl.ANY)] * 2,
        limit=56,
    )[0]
    first = lax.all_to_all(payload, "row", 0, 0)

    def along_y(block, k):
        return lax.ppermute(
            block, "col", [(i, i - i % 4 + (i + k) % 4) for i in range(n_col)]
        )

    picked = call(
        pick_kernel,
        (sample_rows, cotangent),
        [shape((2 * size + samp, feat_grp), BF)],
        2 * 64 * tok * feat_grp,
        limit=56,
    )[0]
    beside = lax.ppermute(picked, "col", [(i, (i + 4) % n_col) for i in range(n_col)])
    cut = 2 * size
    kinds = (picked[:cut], beside[:cut], picked[cut:], beside[cut:])
    pair = jnp.concatenate(kinds, axis=0)
    near = {k: along_y(pair, k) for k in (1, 3)}
    far_rows = along_y(near[1][: 2 * cut], 1)
    far_samples = along_y(near[3][2 * cut :], 3)
    pairs = [pair, near[1], far_rows, near[3]]
    keep, give = call(
        right_kernel,
        (grad_inverse, *pairs),
        [shape((n_col * size, width), BF)] * 2,
        4 * n_col * size * feat_grp * width,
        [
            pltpu.VMEM((n_col, 2, size, width), F32),
            pltpu.VMEM(grad_inverse.shape, BF),
            pltpu.SemaphoreType.DMA((4,)),
        ],
        places=[pl.BlockSpec(memory_space=pl.ANY)] + [VMEM] * 4,
    )
    taken = lax.ppermute(give, "grp", [(i, i ^ 1) for i in range(n_grp)])
    some = keep.astype(F32) + taken.astype(F32)
    give = some.astype(BF)
    first, give, far_samples = lax.optimization_barrier((first, give, far_samples))
    taken = lax.ppermute(give, "grp", [(i, i ^ 2) for i in range(n_grp)])
    right = (some + taken.astype(F32)).astype(BF)
    side = call(
        side_kernel,
        (sample_rows, tokens_in, picked),
        [shape((n_col, 2 * samp, LANES), BF)],
        2 * samp * tok * feat_row,
    )[0]
    send = call(
        second_kernel,
        (first, side),
        [shape((n_grp, n_col, size * spread + strip * n_row // n_grp, LANES), BF)],
        1000000,
    )[0]
    send, right = lax.optimization_barrier((send, right))
    got = lax.all_to_all(send.reshape((n_grp * n_col,) + send.shape[2:]), ("grp", "col"), 0, 0)
    got = got.reshape(send.shape)
    rights = [right] + [
        lax.ppermute(right, "row", [(i, (i + j) % n_row) for i in range(n_row)])
        for j in SHIFTS[1:]
    ]
    term, give = call(
        final_kernel,
        (got, *rights),
        [shape((out_rows, width), F32), shape((out_rows, width), BF)],
        4 * LANES * n_col * spread * size * width,
        [pltpu.VMEM((n_col, spread, size, width), BF)],
    )
    taken = lax.ppermute(give, "grp", [(i, i ^ 1) for i in range(n_grp)])
    precond = term + taken.astype(F32)
    got, unused = lax.optimization_barrier((got, give))
    act_cov, grad_cov = call(
        factor_kernel,
        (got, pair, near[1], far_samples, near[3]),
        [shape((tile, feat_grp), F32)] * 2,
        4 * LANES * samp * n_col * feat_grp,
    )
    return (precond, act_cov, grad_cov)


def solution(mesh):
    return jax.shard_map(
        body,
        mesh=mesh,
        in_specs=(P("col", "row"), P("col", "grp"), P("col"), P("grp", "row"), P("grp", "col")),
        out_specs=(P(("grp", "row"), "col"), P(("row", "col"), "grp"), P(("row", "col"), "grp")),
        check_vma=False,
    )
```

```python
import functools

import jax
import jax.numpy as jnp
from jax import lax
from jax.experimental import pallas as pl
from jax.experimental.pallas import tpu as pltpu
from jax.sharding import PartitionSpec as P

BF = jnp.bfloat16
F32 = jnp.float32
LANES = 128
FIRST = (((0,), (0,)), ((), ()))
LAST = (((1,), (1,)), ((), ()))
SMEM = pl.BlockSpec(memory_space=pltpu.SMEM)
VMEM = pl.BlockSpec(memory_space=pltpu.VMEM)
HBM = pl.BlockSpec(memory_space=pltpu.HBM)
PLANES = 4
SHIFTS = (0, 2, 1, -1)


def call(kernel, inputs, outs, flops, scratch=(), places=None, limit=16):
    places = places or [SMEM if x.dtype == jnp.int32 else VMEM for x in inputs]
    moved = sum(x.size * x.dtype.itemsize for x in list(inputs) + list(outs))
    return pl.pallas_call(
        kernel,
        out_shape=outs,
        in_specs=places,
        out_specs=[VMEM] * len(outs),
        scratch_shapes=list(scratch),
        compiler_params=pltpu.CompilerParams(vmem_limit_bytes=limit * 1024 * 1024),
        cost_estimate=pl.CostEstimate(flops=flops, bytes_accessed=moved, transcendentals=0),
    )(*inputs)


def source_of(k):
    col = lax.axis_index("col")
    return 4 * ((col // 4) ^ (k % 2)) + lax.rem(col % 4 - k // 2 + 4, 4)


def own_picks(picks, count, tok):
    begin = lax.axis_index("grp") * count
    first = lax.axis_index("col") * tok
    return [picks[begin + i] - first for i in range(count)]


def rows_hot(targets, tok):
    shape = (len(targets), tok)
    sub = lax.broadcasted_iota(jnp.int32, shape, 0)
    lane = lax.broadcasted_iota(jnp.int32, shape, 1)
    want = jnp.zeros(shape, jnp.int32)
    for i, target in enumerate(targets):
        want = jnp.where(sub == i, target, want)
    return jnp.where(want == lane, 1.0, 0.0).astype(BF)


def first_kernel(picks, x_hbm, a_hbm, out_ref, x_ref, a_ref, sems):
    n_row, depth, tok = out_ref.shape
    parts = sems.shape[0] - 1
    step = a_ref.shape[0] // parts
    copies = [pltpu.make_async_copy(x_hbm, x_ref, sems.at[parts])]
    for p in range(parts):
        span = pl.ds(p * step, step)
        copies.append(pltpu.make_async_copy(a_hbm.at[span], a_ref.at[span], sems.at[p]))
    for copy in copies:
        copy.start()
    out_rows = a_ref.shape[0] // n_row
    quarter = picks.shape[0] // 4
    hot = rows_hot(own_picks(picks, quarter, tok), tok)
    copies[0].wait()
    chosen = jnp.dot(hot, x_ref[...], preferred_element_type=F32)
    strips = [chosen[:, k : k + LANES] for k in range(0, chosen.shape[1], LANES)]
    block = jnp.concatenate(strips, axis=0).astype(BF)
    out_ref[:, out_rows:, :] = jnp.broadcast_to(block[None], (n_row,) + block.shape)
    each = step // out_rows
    for p in range(parts):
        copies[p + 1].wait()
        rows = a_ref[p * step : (p + 1) * step, :]
        part = lax.dot_general(rows, x_ref[...], LAST, preferred_element_type=F32)
        out_ref[p * each : (p + 1) * each, :out_rows, :] = part.astype(BF).reshape(
            each, out_rows, tok
        )


def pick_kernel(picks, g_ref, out_ref):
    tok = g_ref.shape[0]
    samp = picks.shape[0]
    plane = lax.axis_index("row") % PLANES
    first = lax.axis_index("col") * tok
    count = out_ref.shape[0] - samp
    size = count // 2
    ours = [tok // 2 * (i // size) + size * plane + i % size for i in range(count)]
    hot = rows_hot(ours + [picks[i] - first for i in range(samp)], tok)
    out_ref[...] = jnp.dot(hot, g_ref[...], preferred_element_type=F32).astype(BF)


def side_kernel(picks, x_ref, gy_ref, out_ref):
    n_col, depth, unused = out_ref.shape
    tok, feat = x_ref.shape
    samp = picks.shape[0]
    tile = feat // n_col
    quarter = samp // 4
    hot = rows_hot(own_picks(picks, quarter, tok), tok)
    chosen = jnp.dot(hot, x_ref[...], preferred_element_type=F32)
    begin = pl.multiple_of((lax.axis_index("row") % 4) * feat, LANES)
    own = gy_ref[gy_ref.shape[0] - samp :, pl.ds(begin, feat)].astype(F32)
    empty = jnp.zeros((samp - 3 * quarter, 16), F32)
    for c in range(n_col):
        at = c * tile
        top = own[:, at : at + 32]
        cuts = [chosen[:, at + k : at + k + 16] for k in range(0, tile, 16)]
        low = jnp.concatenate(
            [own[:, at + 32 : at + tile], jnp.concatenate(cuts + [empty], axis=0)], axis=1
        )
        block = jnp.concatenate([top, low], axis=0)
        block = jnp.concatenate([jnp.zeros((depth, LANES - 32), F32), block], axis=1)
        out_ref[c] = block.astype(BF)


def right_kernel(b_hbm, *refs):
    blocks, keep_ref, give_ref, held, b_ref, sems = refs[:-5], *refs[-5:]
    n_blk, unused, size, width = held.shape
    parts = sems.shape[0]
    step = b_ref.shape[0] // parts
    spans = [pl.ds(p * step, step) for p in range(parts)]
    copies = [
        pltpu.make_async_copy(b_hbm.at[span], b_ref.at[span], sems.at[p])
        for p, span in enumerate(spans)
    ]
    for copy in copies:
        copy.start()
    rows = jnp.concatenate([block[: 4 * size, :] for block in blocks], axis=0)
    term = None
    for p in range(parts):
        copies[p].wait()
        left = rows[:, p * step : (p + 1) * step]
        part = jnp.dot(left, b_ref[spans[p], :], preferred_element_type=F32)
        term = part if term is None else term + part
    held[...] = term.reshape(held.shape)
    core = lax.axis_index("grp") % 2
    keep_ref[...] = held[:, core].reshape(n_blk * size, width).astype(BF)
    give_ref[...] = held[:, 1 - core].reshape(n_blk * size, width).astype(BF)


def second_kernel(got_ref, side_ref, out_ref):
    n_grp, n_col, unused, unused = out_ref.shape
    n_row, depth, tok = got_ref.shape
    strip = depth - (depth // 32) * 32
    out_rows = depth - strip
    total = got_ref[0, :out_rows, :].astype(F32)
    for r in range(1, n_row):
        total = total + got_ref[r, :out_rows, :].astype(F32)
    total = jnp.concatenate([total, jnp.zeros((LANES - out_rows, tok), F32)], axis=0)
    turned = jnp.transpose(total).astype(BF)
    size = tok // 2
    per = n_row // n_grp
    x_rows = per * strip
    for g in range(n_grp):
        u_block = turned[(g % 2) * size : (g % 2 + 1) * size]
        x_block = got_ref[g * per : (g + 1) * per, out_rows:, :].astype(F32)
        x_block = x_block.reshape(x_rows, tok).astype(BF)
        for c in range(n_col):
            out_ref[g, c, :size, :] = u_block + side_ref[c]
            out_ref[g, c, size:, :] = x_block


def final_kernel(got_ref, *refs):
    v_refs, own_ref, pair_ref, held = refs[:-3], refs[-3], refs[-2], refs[-1]
    n_col, spread, size, width = held.shape
    row = lax.axis_index("row")
    for j, shift in enumerate(SHIFTS):
        plane = lax.rem(row - shift + spread, spread)
        for k in range(n_col):
            held[source_of(k), plane] = v_refs[j][k * size : (k + 1) * size, :]
    tokens = n_col * spread * size
    right = held[...].reshape(tokens, width)
    grp = lax.axis_index("grp")
    for source, ref in ((grp, own_ref), (grp ^ 1, pair_ref)):
        left = got_ref[source, :, : spread * size, :].reshape(tokens, LANES)
        term = lax.dot_general(left, right, FIRST, preferred_element_type=F32)
        ref[...] = term[: ref.shape[0]].astype(ref.dtype)


def factor_kernel(got_ref, *refs):
    blocks, act_ref, grad_ref = refs[:-2], refs[-2], refs[-1]
    n_grp, n_col, depth, unused = got_ref.shape
    tile, width = act_ref.shape
    samp = blocks[0].shape[0] // 4
    quarter = samp // n_grp
    total = samp * n_col
    scale = 1.0 / total
    begin = depth - quarter * (width // LANES)
    span = got_ref[:, :, begin:, :].astype(F32)
    strips = []
    for t in range(width // LANES):
        strip = span[:, :, t * quarter : (t + 1) * quarter, :].reshape(total, LANES)
        strips.append(strip.astype(BF))
    right = jnp.concatenate(strips, axis=1)
    lefts = got_ref[:, :, samp : 2 * samp, :].astype(F32)
    for k in range(tile // 16):
        left = lefts[:, :, k * quarter : (k + 1) * quarter, :].reshape(total, LANES).astype(BF)
        term = lax.dot_general(left, right, FIRST, preferred_element_type=F32)
        act_ref[16 * k : 16 * (k + 1), :] = term[LANES - 16 :] * scale
    owner = lax.axis_index("row") // 4
    sides = [got_ref[owner, source_of(k), : 2 * samp, :] for k in range(n_col)]
    rights = [block[block.shape[0] - 2 * samp :, :] for block in blocks]
    right = jnp.concatenate(rights, axis=0)
    left = jnp.concatenate([side[:samp] for side in sides], axis=0)
    term = lax.dot_general(left, right, FIRST, preferred_element_type=F32)
    grad_ref[:32, :] = term[LANES - 32 :] * scale
    left = jnp.concatenate([side[samp:] for side in sides], axis=0)
    term = lax.dot_general(left, right, FIRST, preferred_element_type=F32)
    grad_ref[32:, :] = term[LANES - 32 : LANES - 16] * scale


def body(tokens_in, cotangent, sample_rows, act_inverse, grad_inverse):
    n_row = lax.axis_size("row")
    n_col = lax.axis_size("col")
    n_grp = lax.axis_size("grp")
    tok, feat_row = tokens_in.shape
    feat_grp = cotangent.shape[1]
    width = grad_inverse.shape[1]
    samp = sample_rows.shape[0]
    quarter = samp // n_grp
    tile = feat_row // n_col
    out_rows = feat_grp // n_row
    strip = quarter * feat_row // LANES
    spread = PLANES
    size = tok // 2 // spread
    shape = jax.ShapeDtypeStruct

    payload = call(
        first_kernel,
        (sample_rows, tokens_in, act_inverse),
        [shape((n_row, out_rows + strip, tok), BF)],
        2 * feat_grp * feat_row * tok,
        [
            pltpu.VMEM(tokens_in.shape, BF),
            pltpu.VMEM(act_inverse.shape, BF),
            pltpu.SemaphoreType.DMA((5,)),
        ],
        [SMEM] + [HBM] * 2,
    )[0]
    payload, cot = lax.optimization_barrier((payload, cotangent))
    first = lax.all_to_all(payload, "row", 0, 0)

    def along_y(block, k):
        return lax.ppermute(
            block, "col", [(i, i - i % 4 + (i + k) % 4) for i in range(n_col)]
        )

    picked = call(
        pick_kernel,
        (sample_rows, cot),
        [shape((2 * size + samp, feat_grp), BF)],
        2 * 64 * tok * feat_grp,
    )[0]
    beside = lax.ppermute(picked, "col", [(i, (i + 4) % n_col) for i in range(n_col)])
    cut = 2 * size
    kinds = (picked[:cut], beside[:cut], picked[cut:], beside[cut:])
    pair = jnp.concatenate(kinds, axis=0)
    near = {k: along_y(pair, k) for k in (1, 3)}
    far_rows = along_y(near[1][: 2 * cut], 1)
    far_samples = along_y(near[3][2 * cut :], 3)
    pairs = [pair, near[1], far_rows, near[3]]
    keep, give = call(
        right_kernel,
        (grad_inverse, *pairs),
        [shape((n_col * size, width), BF)] * 2,
        4 * n_col * size * feat_grp * width,
        [
            pltpu.VMEM((n_col, 2, size, width), F32),
            pltpu.VMEM(grad_inverse.shape, BF),
            pltpu.SemaphoreType.DMA((4,)),
        ],
        places=[HBM] + [VMEM] * 4,
    )
    taken = lax.ppermute(give, "grp", [(i, i ^ 1) for i in range(n_grp)])
    some = keep.astype(F32) + taken.astype(F32)
    give = some.astype(BF)
    first, far_samples, unused = lax.optimization_barrier((first, far_samples, give))
    taken = lax.ppermute(give, "grp", [(i, i ^ 2) for i in range(n_grp)])
    right = (some + taken.astype(F32)).astype(BF)
    side = call(
        side_kernel,
        (sample_rows, tokens_in, picked),
        [shape((n_col, 2 * samp, LANES), BF)],
        2 * samp * tok * feat_row,
    )[0]
    send = call(
        second_kernel,
        (first, side),
        [shape((n_grp, n_col, size * spread + strip * n_row // n_grp, LANES), BF)],
        1000000,
    )[0]
    send, right = lax.optimization_barrier((send, right))
    got = lax.all_to_all(send.reshape((n_grp * n_col,) + send.shape[2:]), ("grp", "col"), 0, 0)
    got = got.reshape(send.shape)
    rights = [right] + [
        lax.ppermute(right, "row", [(i, (i + j) % n_row) for i in range(n_row)])
        for j in SHIFTS[1:]
    ]
    term, give = call(
        final_kernel,
        (got, *rights),
        [shape((out_rows, width), F32), shape((out_rows, width), BF)],
        4 * LANES * n_col * spread * size * width,
        [pltpu.VMEM((n_col, spread, size, width), BF)],
    )
    taken = lax.ppermute(give, "grp", [(i, i ^ 1) for i in range(n_grp)])
    precond = term + taken.astype(F32)
    got, unused = lax.optimization_barrier((got, give))
    act_cov, grad_cov = call(
        factor_kernel,
        (got, pair, near[1], far_samples, near[3]),
        [shape((tile, feat_grp), F32)] * 2,
        4 * LANES * samp * n_col * feat_grp,
    )
    return (precond, act_cov, grad_cov)


def solution(mesh):
    return jax.shard_map(
        body,
        mesh=mesh,
        in_specs=(P("col", "row"), P("col", "grp"), P("col"), P("grp", "row"), P("grp", "col")),
        out_specs=(P(("grp", "row"), "col"), P(("row", "col"), "grp"), P(("row", "col"), "grp")),
        check_vma=False,
    )
```

```python
import functools

import jax
import jax.numpy as jnp
from jax import lax
from jax.experimental import pallas as pl
from jax.experimental.pallas import tpu as pltpu
from jax.sharding import PartitionSpec as P

BF = jnp.bfloat16
F32 = jnp.float32
LANES = 128
FIRST = (((0,), (0,)), ((), ()))
LAST = (((1,), (1,)), ((), ()))
SMEM = pl.BlockSpec(memory_space=pltpu.SMEM)
VMEM = pl.BlockSpec(memory_space=pltpu.VMEM)
PLANES = 4
SHIFTS = (0, 2, 1, -1)


def call(kernel, inputs, outs, flops, scratch=(), places=None, limit=16):
    places = places or [SMEM if x.dtype == jnp.int32 else VMEM for x in inputs]
    moved = sum(x.size * x.dtype.itemsize for x in list(inputs) + list(outs))
    return pl.pallas_call(
        kernel,
        out_shape=outs,
        in_specs=places,
        out_specs=[VMEM] * len(outs),
        scratch_shapes=list(scratch),
        compiler_params=pltpu.CompilerParams(vmem_limit_bytes=limit * 1024 * 1024),
        cost_estimate=pl.CostEstimate(flops=flops, bytes_accessed=moved, transcendentals=0),
    )(*inputs)


def source_of(k):
    col = lax.axis_index("col")
    return 4 * ((col // 4) ^ (k % 2)) + lax.rem(col % 4 - k // 2 + 4, 4)


def own_picks(picks, count, tok):
    begin = lax.axis_index("grp") * count
    first = lax.axis_index("col") * tok
    return [picks[begin + i] - first for i in range(count)]


def rows_hot(targets, tok):
    shape = (len(targets), tok)
    sub = lax.broadcasted_iota(jnp.int32, shape, 0)
    lane = lax.broadcasted_iota(jnp.int32, shape, 1)
    want = jnp.zeros(shape, jnp.int32)
    for i, target in enumerate(targets):
        want = jnp.where(sub == i, target, want)
    return jnp.where(want == lane, 1.0, 0.0).astype(BF)


def first_kernel(picks, x_hbm, a_hbm, out_ref, x_ref, a_ref, sems):
    n_row, depth, tok = out_ref.shape
    parts = sems.shape[0] - 1
    step = a_ref.shape[0] // parts
    copies = [pltpu.make_async_copy(x_hbm, x_ref, sems.at[parts])]
    for p in range(parts):
        span = pl.ds(p * step, step)
        copies.append(pltpu.make_async_copy(a_hbm.at[span], a_ref.at[span], sems.at[p]))
    for copy in copies:
        copy.start()
    out_rows = a_ref.shape[0] // n_row
    quarter = picks.shape[0] // 4
    hot = rows_hot(own_picks(picks, quarter, tok), tok)
    copies[0].wait()
    chosen = jnp.dot(hot, x_ref[...], preferred_element_type=F32)
    strips = [chosen[:, k : k + LANES] for k in range(0, chosen.shape[1], LANES)]
    block = jnp.concatenate(strips, axis=0).astype(BF)
    out_ref[:, out_rows:, :] = jnp.broadcast_to(block[None], (n_row,) + block.shape)
    each = step // out_rows
    for p in range(parts):
        copies[p + 1].wait()
        rows = a_ref[p * step : (p + 1) * step, :]
        part = lax.dot_general(rows, x_ref[...], LAST, preferred_element_type=F32)
        out_ref[p * each : (p + 1) * each, :out_rows, :] = part.astype(BF).reshape(
            each, out_rows, tok
        )


def pick_kernel(picks, g_ref, out_ref):
    tok = g_ref.shape[0]
    samp = picks.shape[0]
    plane = lax.axis_index("row") % PLANES
    first = lax.axis_index("col") * tok
    count = out_ref.shape[0] - samp
    size = count // 2
    ours = [tok // 2 * (i // size) + size * plane + i % size for i in range(count)]
    hot = rows_hot(ours + [picks[i] - first for i in range(samp)], tok)
    out_ref[...] = jnp.dot(hot, g_ref[...], preferred_element_type=F32).astype(BF)


def side_kernel(picks, x_ref, gy_ref, out_ref):
    n_col, depth, unused = out_ref.shape
    tok, feat = x_ref.shape
    samp = picks.shape[0]
    tile = feat // n_col
    quarter = samp // 4
    hot = rows_hot(own_picks(picks, quarter, tok), tok)
    chosen = jnp.dot(hot, x_ref[...], preferred_element_type=F32)
    begin = pl.multiple_of((lax.axis_index("row") % 4) * feat, LANES)
    own = gy_ref[gy_ref.shape[0] - samp :, pl.ds(begin, feat)].astype(F32)
    empty = jnp.zeros((samp - 3 * quarter, 16), F32)
    for c in range(n_col):
        at = c * tile
        top = own[:, at : at + 32]
        cuts = [chosen[:, at + k : at + k + 16] for k in range(0, tile, 16)]
        low = jnp.concatenate(
            [own[:, at + 32 : at + tile], jnp.concatenate(cuts + [empty], axis=0)], axis=1
        )
        block = jnp.concatenate([top, low], axis=0)
        block = jnp.concatenate([jnp.zeros((depth, LANES - 32), F32), block], axis=1)
        out_ref[c] = block.astype(BF)


def rows_of(block, begin, count):
    step = block.shape[0] // 2
    begin = begin if step > count else 0
    return [block[at : at + count, :] for at in (begin, step + begin)]


def right_kernel(b_hbm, *refs):
    blocks, keep_ref, give_ref, held, b_ref, sems = refs[:-5], *refs[-5:]
    n_blk, unused, size, width = held.shape
    parts = sems.shape[0]
    step = b_ref.shape[0] // parts
    spans = [pl.ds(p * step, step) for p in range(parts)]
    copies = [
        pltpu.make_async_copy(b_hbm.at[span], b_ref.at[span], sems.at[p])
        for p, span in enumerate(spans)
    ]
    for copy in copies:
        copy.start()
    rows = [piece for block in blocks for piece in rows_of(block, 0, 2 * size)]
    rows = jnp.concatenate(rows, axis=0)
    term = None
    for p in range(parts):
        copies[p].wait()
        left = rows[:, p * step : (p + 1) * step]
        part = jnp.dot(left, b_ref[spans[p], :], preferred_element_type=F32)
        term = part if term is None else term + part
    held[...] = term.reshape(held.shape)
    core = lax.axis_index("grp") % 2
    keep_ref[...] = held[:, core].reshape(n_blk * size, width).astype(BF)
    give_ref[...] = held[:, 1 - core].reshape(n_blk * size, width).astype(BF)


def second_kernel(got_ref, side_ref, out_ref):
    n_grp, n_col, unused, unused = out_ref.shape
    n_row, depth, tok = got_ref.shape
    strip = depth - (depth // 32) * 32
    out_rows = depth - strip
    total = got_ref[0, :out_rows, :].astype(F32)
    for r in range(1, n_row):
        total = total + got_ref[r, :out_rows, :].astype(F32)
    total = jnp.concatenate([total, jnp.zeros((LANES - out_rows, tok), F32)], axis=0)
    turned = jnp.transpose(total).astype(BF)
    size = tok // 2
    per = n_row // n_grp
    x_rows = per * strip
    for g in range(n_grp):
        u_block = turned[(g % 2) * size : (g % 2 + 1) * size]
        x_block = got_ref[g * per : (g + 1) * per, out_rows:, :].astype(F32)
        x_block = x_block.reshape(x_rows, tok).astype(BF)
        for c in range(n_col):
            out_ref[g, c, :size, :] = u_block + side_ref[c]
            out_ref[g, c, size:, :] = x_block


def final_kernel(got_ref, *refs):
    v_refs, own_ref, pair_ref, held = refs[:-3], refs[-3], refs[-2], refs[-1]
    n_col, spread, size, width = held.shape
    row = lax.axis_index("row")
    for j, shift in enumerate(SHIFTS):
        plane = lax.rem(row - shift + spread, spread)
        for k in range(n_col):
            held[source_of(k), plane] = v_refs[j][k * size : (k + 1) * size, :]
    tokens = n_col * spread * size
    right = held[...].reshape(tokens, width)
    grp = lax.axis_index("grp")
    for source, ref in ((grp, own_ref), (grp ^ 1, pair_ref)):
        left = got_ref[source, :, : spread * size, :].reshape(tokens, LANES)
        term = lax.dot_general(left, right, FIRST, preferred_element_type=F32)
        ref[...] = term[: ref.shape[0]].astype(ref.dtype)


def factor_kernel(got_ref, *refs):
    blocks, act_ref, grad_ref = refs[:-2], refs[-2], refs[-1]
    n_grp, n_col, depth, unused = got_ref.shape
    tile, width = act_ref.shape
    samp = blocks[0].shape[0] // 4
    quarter = samp // n_grp
    total = samp * n_col
    scale = 1.0 / total
    begin = depth - quarter * (width // LANES)
    span = got_ref[:, :, begin:, :].astype(F32)
    strips = []
    for t in range(width // LANES):
        strip = span[:, :, t * quarter : (t + 1) * quarter, :].reshape(total, LANES)
        strips.append(strip.astype(BF))
    right = jnp.concatenate(strips, axis=1)
    lefts = got_ref[:, :, samp : 2 * samp, :].astype(F32)
    for k in range(tile // 16):
        left = lefts[:, :, k * quarter : (k + 1) * quarter, :].reshape(total, LANES).astype(BF)
        term = lax.dot_general(left, right, FIRST, preferred_element_type=F32)
        act_ref[16 * k : 16 * (k + 1), :] = term[LANES - 16 :] * scale
    owner = lax.axis_index("row") // 4
    sides = [got_ref[owner, source_of(k), : 2 * samp, :] for k in range(n_col)]
    rights = [piece for block in blocks for piece in rows_of(block, samp, samp)]
    right = jnp.concatenate(rights, axis=0)
    left = jnp.concatenate([side[:samp] for side in sides], axis=0)
    term = lax.dot_general(left, right, FIRST, preferred_element_type=F32)
    grad_ref[:32, :] = term[LANES - 32 :] * scale
    left = jnp.concatenate([side[samp:] for side in sides], axis=0)
    term = lax.dot_general(left, right, FIRST, preferred_element_type=F32)
    grad_ref[32:, :] = term[LANES - 32 : LANES - 16] * scale


def body(tokens_in, cotangent, sample_rows, act_inverse, grad_inverse):
    n_row = lax.axis_size("row")
    n_col = lax.axis_size("col")
    n_grp = lax.axis_size("grp")
    tok, feat_row = tokens_in.shape
    feat_grp = cotangent.shape[1]
    width = grad_inverse.shape[1]
    samp = sample_rows.shape[0]
    quarter = samp // n_grp
    tile = feat_row // n_col
    out_rows = feat_grp // n_row
    strip = quarter * feat_row // LANES
    spread = PLANES
    size = tok // 2 // spread
    shape = jax.ShapeDtypeStruct

    payload = call(
        first_kernel,
        (sample_rows, tokens_in, act_inverse),
        [shape((n_row, out_rows + strip, tok), BF)],
        2 * feat_grp * feat_row * tok,
        [
            pltpu.VMEM(tokens_in.shape, BF),
            pltpu.VMEM(act_inverse.shape, BF),
            pltpu.SemaphoreType.DMA((5,)),
        ],
        [SMEM] + [pl.BlockSpec(memory_space=pl.ANY)] * 2,
        limit=56,
    )[0]
    payload, cot = lax.optimization_barrier((payload, cotangent))
    first = lax.all_to_all(payload, "row", 0, 0)

    def along_y(block, k):
        return lax.ppermute(
            block, "col", [(i, i - i % 4 + (i + k) % 4) for i in range(n_col)]
        )

    picked = call(
        pick_kernel,
        (sample_rows, cot),
        [shape((2 * size + samp, feat_grp), BF)],
        2 * 64 * tok * feat_grp,
    )[0]
    beside = lax.ppermute(picked, "col", [(i, (i + 4) % n_col) for i in range(n_col)])
    cut = 2 * size
    pair = jnp.concatenate([picked, beside], axis=0)
    rows = jnp.concatenate([picked[:cut], beside[:cut]], axis=0)
    near = {k: along_y(pair, k) for k in (1, 3)}
    pairs = [pair, near[1], along_y(rows, 2), near[3]]
    keep, give = call(
        right_kernel,
        (grad_inverse, *pairs),
        [shape((n_col * size, width), BF)] * 2,
        4 * n_col * size * feat_grp * width,
        [
            pltpu.VMEM((n_col, 2, size, width), F32),
            pltpu.VMEM(grad_inverse.shape, BF),
            pltpu.SemaphoreType.DMA((4,)),
        ],
        places=[pl.BlockSpec(memory_space=pl.ANY)] + [VMEM] * 4,
    )
    taken = lax.ppermute(give, "grp", [(i, i ^ 1) for i in range(n_grp)])
    some = keep.astype(F32) + taken.astype(F32)
    give = some.astype(BF)
    first, give = lax.optimization_barrier((first, give))
    taken = lax.ppermute(give, "grp", [(i, i ^ 2) for i in range(n_grp)])
    right = (some + taken.astype(F32)).astype(BF)
    side = call(
        side_kernel,
        (sample_rows, tokens_in, picked),
        [shape((n_col, 2 * samp, LANES), BF)],
        2 * samp * tok * feat_row,
    )[0]
    send = call(
        second_kernel,
        (first, side),
        [shape((n_grp, n_col, size * spread + strip * n_row // n_grp, LANES), BF)],
        1000000,
    )[0]
    send, picked_y, beside_y = lax.optimization_barrier((send, picked[cut:], beside[cut:]))
    far = along_y(jnp.concatenate([picked_y, beside_y], axis=0), 2)
    send, right = lax.optimization_barrier((send, right))
    got = lax.all_to_all(send.reshape((n_grp * n_col,) + send.shape[2:]), ("grp", "col"), 0, 0)
    got = got.reshape(send.shape)
    right, far = lax.optimization_barrier((right, far))
    rights = [right] + [
        lax.ppermute(right, "row", [(i, (i + j) % n_row) for i in range(n_row)])
        for j in SHIFTS[1:]
    ]

    term, give = call(
        final_kernel,
        (got, *rights),
        [shape((out_rows, width), F32), shape((out_rows, width), BF)],
        4 * LANES * n_col * spread * size * width,
        [pltpu.VMEM((n_col, spread, size, width), BF)],
    )
    taken = lax.ppermute(give, "grp", [(i, i ^ 1) for i in range(n_grp)])
    precond = term + taken.astype(F32)
    got, unused = lax.optimization_barrier((got, give))
    act_cov, grad_cov = call(
        factor_kernel,
        (got, pair, near[1], far, near[3]),
        [shape((tile, feat_grp), F32)] * 2,
        4 * LANES * samp * n_col * feat_grp,
    )
    return (precond, act_cov, grad_cov)


def solution(mesh):
    return jax.shard_map(
        body,
        mesh=mesh,
        in_specs=(P("col", "row"), P("col", "grp"), P("col"), P("grp", "row"), P("grp", "col")),
        out_specs=(P(("grp", "row"), "col"), P(("row", "col"), "grp"), P(("row", "col"), "grp")),
        check_vma=False,
    )
```

```python
import functools

import jax
import jax.numpy as jnp
from jax import lax
from jax.experimental import pallas as pl
from jax.experimental.pallas import tpu as pltpu
from jax.sharding import PartitionSpec as P

BF = jnp.bfloat16
F32 = jnp.float32
LANES = 128
FIRST = (((0,), (0,)), ((), ()))
LAST = (((1,), (1,)), ((), ()))
SMEM = pl.BlockSpec(memory_space=pltpu.SMEM)
VMEM = pl.BlockSpec(memory_space=pltpu.VMEM)
PLANES = 4
SHIFTS = (0, 2, 1, -1)


def call(kernel, inputs, outs, flops, scratch=(), places=None, limit=16):
    places = places or [SMEM if x.dtype == jnp.int32 else VMEM for x in inputs]
    moved = sum(x.size * x.dtype.itemsize for x in list(inputs) + list(outs))
    return pl.pallas_call(
        kernel,
        out_shape=outs,
        in_specs=places,
        out_specs=[VMEM] * len(outs),
        scratch_shapes=list(scratch),
        compiler_params=pltpu.CompilerParams(vmem_limit_bytes=limit * 1024 * 1024),
        cost_estimate=pl.CostEstimate(flops=flops, bytes_accessed=moved, transcendentals=0),
    )(*inputs)


def source_of(k):
    col = lax.axis_index("col")
    return 4 * ((col // 4) ^ (k % 2)) + lax.rem(col % 4 - k // 2 + 4, 4)


def own_picks(picks, count, tok):
    begin = lax.axis_index("grp") * count
    first = lax.axis_index("col") * tok
    return [picks[begin + i] - first for i in range(count)]


def rows_hot(targets, tok):
    shape = (len(targets), tok)
    sub = lax.broadcasted_iota(jnp.int32, shape, 0)
    lane = lax.broadcasted_iota(jnp.int32, shape, 1)
    want = jnp.zeros(shape, jnp.int32)
    for i, target in enumerate(targets):
        want = jnp.where(sub == i, target, want)
    return jnp.where(want == lane, 1.0, 0.0).astype(BF)


def first_kernel(picks, x_hbm, a_hbm, out_ref, x_ref, a_ref, sems):
    n_row, depth, tok = out_ref.shape
    parts = sems.shape[0] - 1
    step = a_ref.shape[0] // parts
    copies = [pltpu.make_async_copy(x_hbm, x_ref, sems.at[parts])]
    for p in range(parts):
        span = pl.ds(p * step, step)
        copies.append(pltpu.make_async_copy(a_hbm.at[span], a_ref.at[span], sems.at[p]))
    for copy in copies:
        copy.start()
    out_rows = a_ref.shape[0] // n_row
    quarter = picks.shape[0] // 4
    hot = rows_hot(own_picks(picks, quarter, tok), tok)
    copies[0].wait()
    chosen = jnp.dot(hot, x_ref[...], preferred_element_type=F32)
    strips = [chosen[:, k : k + LANES] for k in range(0, chosen.shape[1], LANES)]
    block = jnp.concatenate(strips, axis=0).astype(BF)
    out_ref[:, out_rows:, :] = jnp.broadcast_to(block[None], (n_row,) + block.shape)
    each = step // out_rows
    for p in range(parts):
        copies[p + 1].wait()
        rows = a_ref[p * step : (p + 1) * step, :]
        part = lax.dot_general(rows, x_ref[...], LAST, preferred_element_type=F32)
        out_ref[p * each : (p + 1) * each, :out_rows, :] = part.astype(BF).reshape(
            each, out_rows, tok
        )


def pick_kernel(picks, g_ref, out_ref):
    tok = g_ref.shape[0]
    samp = picks.shape[0]
    plane = lax.axis_index("row") % PLANES
    first = lax.axis_index("col") * tok
    count = out_ref.shape[0] - samp
    size = count // 2
    ours = [tok // 2 * (i // size) + size * plane + i % size for i in range(count)]
    hot = rows_hot(ours + [picks[i] - first for i in range(samp)], tok)
    out_ref[...] = jnp.dot(hot, g_ref[...], preferred_element_type=F32).astype(BF)


def side_kernel(picks, x_ref, gy_ref, out_ref):
    n_col, depth, unused = out_ref.shape
    tok, feat = x_ref.shape
    samp = picks.shape[0]
    tile = feat // n_col
    quarter = samp // 4
    hot = rows_hot(own_picks(picks, quarter, tok), tok)
    chosen = jnp.dot(hot, x_ref[...], preferred_element_type=F32)
    begin = pl.multiple_of((lax.axis_index("row") % 4) * feat, LANES)
    own = gy_ref[gy_ref.shape[0] - samp :, pl.ds(begin, feat)].astype(F32)
    empty = jnp.zeros((samp - 3 * quarter, 16), F32)
    for c in range(n_col):
        at = c * tile
        top = own[:, at : at + 32]
        cuts = [chosen[:, at + k : at + k + 16] for k in range(0, tile, 16)]
        low = jnp.concatenate(
            [own[:, at + 32 : at + tile], jnp.concatenate(cuts + [empty], axis=0)], axis=1
        )
        block = jnp.concatenate([top, low], axis=0)
        block = jnp.concatenate([jnp.zeros((depth, LANES - 32), F32), block], axis=1)
        out_ref[c] = block.astype(BF)


def right_kernel(b_hbm, *refs):
    blocks, keep_ref, give_ref, held, b_ref, sems = refs[:-5], *refs[-5:]
    n_blk, unused, size, width = held.shape
    parts = sems.shape[0]
    step = b_ref.shape[0] // parts
    spans = [pl.ds(p * step, step) for p in range(parts)]
    copies = [
        pltpu.make_async_copy(b_hbm.at[span], b_ref.at[span], sems.at[p])
        for p, span in enumerate(spans)
    ]
    for copy in copies:
        copy.start()
    rows = jnp.concatenate([block[: 4 * size, :] for block in blocks], axis=0)
    term = None
    for p in range(parts):
        copies[p].wait()
        left = rows[:, p * step : (p + 1) * step]
        part = jnp.dot(left, b_ref[spans[p], :], preferred_element_type=F32)
        term = part if term is None else term + part
    held[...] = term.reshape(held.shape)
    core = lax.axis_index("grp") % 2
    keep_ref[...] = held[:, core].reshape(n_blk * size, width).astype(BF)
    give_ref[...] = held[:, 1 - core].reshape(n_blk * size, width).astype(BF)


def second_kernel(got_ref, side_ref, out_ref):
    n_grp, n_col, unused, unused = out_ref.shape
    n_row, depth, tok = got_ref.shape
    strip = depth - (depth // 32) * 32
    out_rows = depth - strip
    total = got_ref[0, :out_rows, :].astype(F32)
    for r in range(1, n_row):
        total = total + got_ref[r, :out_rows, :].astype(F32)
    total = jnp.concatenate([total, jnp.zeros((LANES - out_rows, tok), F32)], axis=0)
    turned = jnp.transpose(total).astype(BF)
    size = tok // 2
    per = n_row // n_grp
    x_rows = per * strip
    for g in range(n_grp):
        u_block = turned[(g % 2) * size : (g % 2 + 1) * size]
        x_block = got_ref[g * per : (g + 1) * per, out_rows:, :].astype(F32)
        x_block = x_block.reshape(x_rows, tok).astype(BF)
        for c in range(n_col):
            out_ref[g, c, :size, :] = u_block + side_ref[c]
            out_ref[g, c, size:, :] = x_block


def final_kernel(got_ref, *refs):
    v_refs, out_ref, held = refs[:-2], refs[-2], refs[-1]
    n_col, spread, size, width = held.shape
    n_grp, out_rows, unused = out_ref.shape
    row = lax.axis_index("row")
    for j, shift in enumerate(SHIFTS):
        plane = lax.rem(row - shift + spread, spread)
        for k in range(n_col):
            held[source_of(k), plane] = v_refs[j][k * size : (k + 1) * size, :]
    tokens = n_col * spread * size
    right = held[...].reshape(tokens, width)
    for g in range(n_grp):
        left = got_ref[g, :, : spread * size, :].reshape(tokens, LANES)
        term = lax.dot_general(left, right, FIRST, preferred_element_type=F32)
        out_ref[g] = term[:out_rows].astype(BF)


def factor_kernel(got_ref, *refs):
    blocks, act_ref, grad_ref = refs[:-2], refs[-2], refs[-1]
    n_grp, n_col, depth, unused = got_ref.shape
    tile, width = act_ref.shape
    samp = blocks[0].shape[0] // 4
    quarter = samp // n_grp
    total = samp * n_col
    scale = 1.0 / total
    begin = depth - quarter * (width // LANES)
    span = got_ref[:, :, begin:, :].astype(F32)
    strips = []
    for t in range(width // LANES):
        strip = span[:, :, t * quarter : (t + 1) * quarter, :].reshape(total, LANES)
        strips.append(strip.astype(BF))
    right = jnp.concatenate(strips, axis=1)
    lefts = got_ref[:, :, samp : 2 * samp, :].astype(F32)
    for k in range(tile // 16):
        left = lefts[:, :, k * quarter : (k + 1) * quarter, :].reshape(total, LANES).astype(BF)
        term = lax.dot_general(left, right, FIRST, preferred_element_type=F32)
        act_ref[16 * k : 16 * (k + 1), :] = term[LANES - 16 :] * scale
    owner = lax.axis_index("row") // 4
    sides = [got_ref[owner, source_of(k), : 2 * samp, :] for k in range(n_col)]
    rights = [block[block.shape[0] - 2 * samp :, :] for block in blocks]
    right = jnp.concatenate(rights, axis=0)
    left = jnp.concatenate([side[:samp] for side in sides], axis=0)
    term = lax.dot_general(left, right, FIRST, preferred_element_type=F32)
    grad_ref[:32, :] = term[LANES - 32 :] * scale
    left = jnp.concatenate([side[samp:] for side in sides], axis=0)
    term = lax.dot_general(left, right, FIRST, preferred_element_type=F32)
    grad_ref[32:, :] = term[LANES - 32 : LANES - 16] * scale


def body(tokens_in, cotangent, sample_rows, act_inverse, grad_inverse):
    n_row = lax.axis_size("row")
    n_col = lax.axis_size("col")
    n_grp = lax.axis_size("grp")
    tok, feat_row = tokens_in.shape
    feat_grp = cotangent.shape[1]
    width = grad_inverse.shape[1]
    samp = sample_rows.shape[0]
    quarter = samp // n_grp
    tile = feat_row // n_col
    out_rows = feat_grp // n_row
    strip = quarter * feat_row // LANES
    spread = PLANES
    size = tok // 2 // spread
    shape = jax.ShapeDtypeStruct

    payload = call(
        first_kernel,
        (sample_rows, tokens_in, act_inverse),
        [shape((n_row, out_rows + strip, tok), BF)],
        2 * feat_grp * feat_row * tok,
        [
            pltpu.VMEM(tokens_in.shape, BF),
            pltpu.VMEM(act_inverse.shape, BF),
            pltpu.SemaphoreType.DMA((5,)),
        ],
        [SMEM] + [pl.BlockSpec(memory_space=pl.ANY)] * 2,
        limit=56,
    )[0]
    first = lax.all_to_all(payload, "row", 0, 0)

    def along_y(block, k):
        return lax.ppermute(
            block, "col", [(i, i - i % 4 + (i + k) % 4) for i in range(n_col)]
        )

    picked = call(
        pick_kernel,
        (sample_rows, cotangent),
        [shape((2 * size + samp, feat_grp), BF)],
        2 * 64 * tok * feat_grp,
    )[0]
    beside = lax.ppermute(picked, "col", [(i, (i + 4) % n_col) for i in range(n_col)])
    cut = 2 * size
    rows = jnp.concatenate([picked[:cut], beside[:cut]], axis=0)
    samples = jnp.concatenate([picked[cut:], beside[cut:]], axis=0)
    pair = jnp.concatenate([rows, samples], axis=0)
    after = along_y(pair, 3)
    before = along_y(rows, 1)
    pairs = [pair, before, along_y(rows, 2), after]
    keep, give = call(
        right_kernel,
        (grad_inverse, *pairs),
        [shape((n_col * size, width), BF)] * 2,
        4 * n_col * size * feat_grp * width,
        [
            pltpu.VMEM((n_col, 2, size, width), F32),
            pltpu.VMEM(grad_inverse.shape, BF),
            pltpu.SemaphoreType.DMA((4,)),
        ],
        places=[pl.BlockSpec(memory_space=pl.ANY)] + [VMEM] * 4,
    )
    before, samples = lax.optimization_barrier((before, samples))
    nearby = along_y(samples, 1)
    taken = lax.ppermute(give, "grp", [(i, i ^ 1) for i in range(n_grp)])
    right = (keep.astype(F32) + taken.astype(F32)).astype(BF)
    first, unused = lax.optimization_barrier((first, (right, nearby)))
    rights = [right] + [
        lax.ppermute(right, "row", [(i, (i + j) % n_row) for i in range(n_row)])
        for j in SHIFTS[1:]
    ]
    side = call(
        side_kernel,
        (sample_rows, tokens_in, picked),
        [shape((n_col, 2 * samp, LANES), BF)],
        2 * samp * tok * feat_row,
    )[0]
    send = call(
        second_kernel,
        (first, side),
        [shape((n_grp, n_col, size * spread + strip * n_row // n_grp, LANES), BF)],
        1000000,
    )[0]
    got = lax.all_to_all(send.reshape((n_grp * n_col,) + send.shape[2:]), ("grp", "col"), 0, 0)
    got = got.reshape(send.shape)

    term = call(
        final_kernel,
        (got, *rights),
        [shape((n_grp, out_rows, width), BF)],
        2 * n_grp * LANES * n_col * spread * size * width,
        [pltpu.VMEM((n_col, spread, size, width), BF)],
    )[0]
    got, beyond, unused = lax.optimization_barrier((got, after[2 * cut :], term))
    term = lax.all_to_all(term, "grp", 0, 0)
    far = along_y(beyond, 3)
    precond = jnp.sum(term.astype(F32), axis=0)
    act_cov, grad_cov = call(
        factor_kernel,
        (got, pair, nearby, far, after),
        [shape((tile, feat_grp), F32)] * 2,
        4 * LANES * samp * n_col * feat_grp,
    )
    return (precond, act_cov, grad_cov)


def solution(mesh):
    return jax.shard_map(
        body,
        mesh=mesh,
        in_specs=(P("col", "row"), P("col", "grp"), P("col"), P("grp", "row"), P("grp", "col")),
        out_specs=(P(("grp", "row"), "col"), P(("row", "col"), "grp"), P(("row", "col"), "grp")),
        check_vma=False,
    )
```

```python
import functools

import jax
import jax.numpy as jnp
from jax import lax
from jax.experimental import pallas as pl
from jax.experimental.pallas import tpu as pltpu
from jax.sharding import PartitionSpec as P

BF = jnp.bfloat16
F32 = jnp.float32
LANES = 128
FIRST = (((0,), (0,)), ((), ()))
LAST = (((1,), (1,)), ((), ()))
SMEM = pl.BlockSpec(memory_space=pltpu.SMEM)
VMEM = pl.BlockSpec(memory_space=pltpu.VMEM)
PLANES = 4
SHIFTS = (0, 2, 1, -1)


def call(kernel, inputs, outs, flops, scratch=(), places=None, limit=16):
    places = places or [SMEM if x.dtype == jnp.int32 else VMEM for x in inputs]
    moved = sum(x.size * x.dtype.itemsize for x in list(inputs) + list(outs))
    return pl.pallas_call(
        kernel,
        out_shape=outs,
        in_specs=places,
        out_specs=[VMEM] * len(outs),
        scratch_shapes=list(scratch),
        compiler_params=pltpu.CompilerParams(vmem_limit_bytes=limit * 1024 * 1024),
        cost_estimate=pl.CostEstimate(flops=flops, bytes_accessed=moved, transcendentals=0),
    )(*inputs)


def source_of(k):
    col = lax.axis_index("col")
    return 4 * ((col // 4) ^ (k % 2)) + lax.rem(col % 4 - k // 2 + 4, 4)


def own_picks(picks, count, tok):
    begin = lax.axis_index("grp") * count
    first = lax.axis_index("col") * tok
    return [picks[begin + i] - first for i in range(count)]


def rows_hot(targets, tok):
    shape = (len(targets), tok)
    sub = lax.broadcasted_iota(jnp.int32, shape, 0)
    lane = lax.broadcasted_iota(jnp.int32, shape, 1)
    want = jnp.zeros(shape, jnp.int32)
    for i, target in enumerate(targets):
        want = jnp.where(sub == i, target, want)
    return jnp.where(want == lane, 1.0, 0.0).astype(BF)


def first_kernel(picks, x_hbm, a_hbm, out_ref, x_ref, a_ref, sems):
    n_row, depth, tok = out_ref.shape
    parts = sems.shape[0] - 1
    step = a_ref.shape[0] // parts
    copies = [pltpu.make_async_copy(x_hbm, x_ref, sems.at[parts])]
    for p in range(parts):
        span = pl.ds(p * step, step)
        copies.append(pltpu.make_async_copy(a_hbm.at[span], a_ref.at[span], sems.at[p]))
    for copy in copies:
        copy.start()
    out_rows = a_ref.shape[0] // n_row
    quarter = picks.shape[0] // 4
    hot = rows_hot(own_picks(picks, quarter, tok), tok)
    copies[0].wait()
    chosen = jnp.dot(hot, x_ref[...], preferred_element_type=F32)
    strips = [chosen[:, k : k + LANES] for k in range(0, chosen.shape[1], LANES)]
    block = jnp.concatenate(strips, axis=0).astype(BF)
    out_ref[:, out_rows:, :] = jnp.broadcast_to(block[None], (n_row,) + block.shape)
    each = step // out_rows
    for p in range(parts):
        copies[p + 1].wait()
        rows = a_ref[p * step : (p + 1) * step, :]
        part = lax.dot_general(rows, x_ref[...], LAST, preferred_element_type=F32)
        out_ref[p * each : (p + 1) * each, :out_rows, :] = part.astype(BF).reshape(
            each, out_rows, tok
        )


def pick_kernel(picks, g_ref, out_ref):
    tok = g_ref.shape[0]
    samp = picks.shape[0]
    plane = lax.axis_index("row") % PLANES
    first = lax.axis_index("col") * tok
    count = out_ref.shape[0] - samp
    size = count // 2
    ours = [tok // 2 * (i // size) + size * plane + i % size for i in range(count)]
    hot = rows_hot(ours + [picks[i] - first for i in range(samp)], tok)
    out_ref[...] = jnp.dot(hot, g_ref[...], preferred_element_type=F32).astype(BF)


def side_kernel(picks, x_ref, gy_ref, out_ref):
    n_col, depth, unused = out_ref.shape
    tok, feat = x_ref.shape
    samp = picks.shape[0]
    tile = feat // n_col
    quarter = samp // 4
    hot = rows_hot(own_picks(picks, quarter, tok), tok)
    chosen = jnp.dot(hot, x_ref[...], preferred_element_type=F32)
    begin = pl.multiple_of((lax.axis_index("row") % 4) * feat, LANES)
    own = gy_ref[gy_ref.shape[0] - samp :, pl.ds(begin, feat)].astype(F32)
    empty = jnp.zeros((samp - 3 * quarter, 16), F32)
    for c in range(n_col):
        at = c * tile
        top = own[:, at : at + 32]
        cuts = [chosen[:, at + k : at + k + 16] for k in range(0, tile, 16)]
        low = jnp.concatenate(
            [own[:, at + 32 : at + tile], jnp.concatenate(cuts + [empty], axis=0)], axis=1
        )
        block = jnp.concatenate([top, low], axis=0)
        block = jnp.concatenate([jnp.zeros((depth, LANES - 32), F32), block], axis=1)
        out_ref[c] = block.astype(BF)


def right_kernel(b_hbm, *refs):
    blocks, keep_ref, give_ref, held, b_ref, sems = refs[:-5], *refs[-5:]
    n_blk, unused, size, width = held.shape
    parts = sems.shape[0]
    step = b_ref.shape[0] // parts
    spans = [pl.ds(p * step, step) for p in range(parts)]
    copies = [
        pltpu.make_async_copy(b_hbm.at[span], b_ref.at[span], sems.at[p])
        for p, span in enumerate(spans)
    ]
    for copy in copies:
        copy.start()
    rows = jnp.concatenate([block[: 4 * size, :] for block in blocks], axis=0)
    term = None
    for p in range(parts):
        copies[p].wait()
        left = rows[:, p * step : (p + 1) * step]
        part = jnp.dot(left, b_ref[spans[p], :], preferred_element_type=F32)
        term = part if term is None else term + part
    held[...] = term.reshape(held.shape)
    core = lax.axis_index("grp") % 2
    keep_ref[...] = held[:, core].reshape(n_blk * size, width).astype(BF)
    give_ref[...] = held[:, 1 - core].reshape(n_blk * size, width).astype(BF)


def second_kernel(got_ref, side_ref, out_ref):
    n_grp, n_col, unused, unused = out_ref.shape
    n_row, depth, tok = got_ref.shape
    strip = depth - (depth // 32) * 32
    out_rows = depth - strip
    total = got_ref[0, :out_rows, :].astype(F32)
    for r in range(1, n_row):
        total = total + got_ref[r, :out_rows, :].astype(F32)
    total = jnp.concatenate([total, jnp.zeros((LANES - out_rows, tok), F32)], axis=0)
    turned = jnp.transpose(total).astype(BF)
    size = tok // 2
    per = n_row // n_grp
    x_rows = per * strip
    for g in range(n_grp):
        u_block = turned[(g % 2) * size : (g % 2 + 1) * size]
        x_block = got_ref[g * per : (g + 1) * per, out_rows:, :].astype(F32)
        x_block = x_block.reshape(x_rows, tok).astype(BF)
        for c in range(n_col):
            out_ref[g, c, :size, :] = u_block + side_ref[c]
            out_ref[g, c, size:, :] = x_block


def final_kernel(got_ref, *refs):
    v_refs, own_ref, pair_ref, held = refs[:-3], refs[-3], refs[-2], refs[-1]
    n_col, spread, size, width = held.shape
    row = lax.axis_index("row")
    for j, shift in enumerate(SHIFTS):
        plane = lax.rem(row - shift + spread, spread)
        for k in range(n_col):
            held[source_of(k), plane] = v_refs[j][k * size : (k + 1) * size, :]
    tokens = n_col * spread * size
    right = held[...].reshape(tokens, width)
    grp = lax.axis_index("grp")
    for source, ref in ((grp, own_ref), (grp ^ 1, pair_ref)):
        left = got_ref[source, :, : spread * size, :].reshape(tokens, LANES)
        term = lax.dot_general(left, right, FIRST, preferred_element_type=F32)
        ref[...] = term[: ref.shape[0]].astype(ref.dtype)


def factor_kernel(got_ref, *refs):
    blocks, act_ref, grad_ref = refs[:-2], refs[-2], refs[-1]
    n_grp, n_col, depth, unused = got_ref.shape
    tile, width = act_ref.shape
    samp = blocks[0].shape[0] // 4
    quarter = samp // n_grp
    total = samp * n_col
    scale = 1.0 / total
    begin = depth - quarter * (width // LANES)
    span = got_ref[:, :, begin:, :].astype(F32)
    strips = []
    for t in range(width // LANES):
        strip = span[:, :, t * quarter : (t + 1) * quarter, :].reshape(total, LANES)
        strips.append(strip.astype(BF))
    right = jnp.concatenate(strips, axis=1)
    lefts = got_ref[:, :, samp : 2 * samp, :].astype(F32)
    for k in range(tile // 16):
        left = lefts[:, :, k * quarter : (k + 1) * quarter, :].reshape(total, LANES).astype(BF)
        term = lax.dot_general(left, right, FIRST, preferred_element_type=F32)
        act_ref[16 * k : 16 * (k + 1), :] = term[LANES - 16 :] * scale
    owner = lax.axis_index("row") // 4
    sides = [got_ref[owner, source_of(k), : 2 * samp, :] for k in range(n_col)]
    rights = [block[block.shape[0] - 2 * samp :, :] for block in blocks]
    right = jnp.concatenate(rights, axis=0)
    left = jnp.concatenate([side[:samp] for side in sides], axis=0)
    term = lax.dot_general(left, right, FIRST, preferred_element_type=F32)
    grad_ref[:32, :] = term[LANES - 32 :] * scale
    left = jnp.concatenate([side[samp:] for side in sides], axis=0)
    term = lax.dot_general(left, right, FIRST, preferred_element_type=F32)
    grad_ref[32:, :] = term[LANES - 32 : LANES - 16] * scale


def body(tokens_in, cotangent, sample_rows, act_inverse, grad_inverse):
    n_row = lax.axis_size("row")
    n_col = lax.axis_size("col")
    n_grp = lax.axis_size("grp")
    tok, feat_row = tokens_in.shape
    feat_grp = cotangent.shape[1]
    width = grad_inverse.shape[1]
    samp = sample_rows.shape[0]
    quarter = samp // n_grp
    tile = feat_row // n_col
    out_rows = feat_grp // n_row
    strip = quarter * feat_row // LANES
    spread = PLANES
    size = tok // 2 // spread
    shape = jax.ShapeDtypeStruct

    payload = call(
        first_kernel,
        (sample_rows, tokens_in, act_inverse),
        [shape((n_row, out_rows + strip, tok), BF)],
        2 * feat_grp * feat_row * tok,
        [
            pltpu.VMEM(tokens_in.shape, BF),
            pltpu.VMEM(act_inverse.shape, BF),
            pltpu.SemaphoreType.DMA((5,)),
        ],
        [SMEM] + [pl.BlockSpec(memory_space=pl.ANY)] * 2,
        limit=56,
    )[0]
    first = lax.all_to_all(payload, "row", 0, 0)

    def along_y(block, k):
        return lax.ppermute(
            block, "col", [(i, i - i % 4 + (i + k) % 4) for i in range(n_col)]
        )

    picked = call(
        pick_kernel,
        (sample_rows, cotangent),
        [shape((2 * size + samp, feat_grp), BF)],
        2 * 64 * tok * feat_grp,
    )[0]
    beside = lax.ppermute(picked, "col", [(i, (i + 4) % n_col) for i in range(n_col)])
    cut = 2 * size
    rows = jnp.concatenate([picked[:cut], beside[:cut]], axis=0)
    samples = jnp.concatenate([picked[cut:], beside[cut:]], axis=0)
    pair = jnp.concatenate([rows, samples], axis=0)
    after = along_y(pair, 3)
    before = along_y(pair, 1)
    pairs = [pair, before, along_y(rows, 2), after]
    keep, give = call(
        right_kernel,
        (grad_inverse, *pairs),
        [shape((n_col * size, width), BF)] * 2,
        4 * n_col * size * feat_grp * width,
        [
            pltpu.VMEM((n_col, 2, size, width), F32),
            pltpu.VMEM(grad_inverse.shape, BF),
            pltpu.SemaphoreType.DMA((4,)),
        ],
        places=[pl.BlockSpec(memory_space=pl.ANY)] + [VMEM] * 4,
    )
    taken = lax.ppermute(give, "grp", [(i, i ^ 1) for i in range(n_grp)])
    some = keep.astype(F32) + taken.astype(F32)
    give = some.astype(BF)
    first, give = lax.optimization_barrier((first, give))
    taken = lax.ppermute(give, "grp", [(i, i ^ 2) for i in range(n_grp)])
    right = (some + taken.astype(F32)).astype(BF)
    side = call(
        side_kernel,
        (sample_rows, tokens_in, picked),
        [shape((n_col, 2 * samp, LANES), BF)],
        2 * samp * tok * feat_row,
    )[0]
    send = call(
        second_kernel,
        (first, side),
        [shape((n_grp, n_col, size * spread + strip * n_row // n_grp, LANES), BF)],
        1000000,
    )[0]
    send, right = lax.optimization_barrier((send, right))
    got = lax.all_to_all(send.reshape((n_grp * n_col,) + send.shape[2:]), ("grp", "col"), 0, 0)
    got = got.reshape(send.shape)
    rights = [right] + [
        lax.ppermute(right, "row", [(i, (i + j) % n_row) for i in range(n_row)])
        for j in SHIFTS[1:]
    ]
    unused, beyond = lax.optimization_barrier((rights[1], after[2 * cut :]))
    far = along_y(beyond, 3)

    rights, far = lax.optimization_barrier((rights, far))
    term, give = call(
        final_kernel,
        (got, *rights),
        [shape((out_rows, width), F32), shape((out_rows, width), BF)],
        4 * LANES * n_col * spread * size * width,
        [pltpu.VMEM((n_col, spread, size, width), BF)],
    )
    taken = lax.ppermute(give, "grp", [(i, i ^ 1) for i in range(n_grp)])
    precond = term + taken.astype(F32)
    got, unused = lax.optimization_barrier((got, give))
    act_cov, grad_cov = call(
        factor_kernel,
        (got, pair, before, far, after),
        [shape((tile, feat_grp), F32)] * 2,
        4 * LANES * samp * n_col * feat_grp,
    )
    return (precond, act_cov, grad_cov)


def solution(mesh):
    return jax.shard_map(
        body,
        mesh=mesh,
        in_specs=(P("col", "row"), P("col", "grp"), P("col"), P("grp", "row"), P("grp", "col")),
        out_specs=(P(("grp", "row"), "col"), P(("row", "col"), "grp"), P(("row", "col"), "grp")),
        check_vma=False,
    )
```

```python
import functools

import jax
import jax.numpy as jnp
from jax import lax
from jax.experimental import pallas as pl
from jax.experimental.pallas import tpu as pltpu
from jax.sharding import PartitionSpec as P

BF = jnp.bfloat16
F32 = jnp.float32
LANES = 128
FIRST = (((0,), (0,)), ((), ()))
LAST = (((1,), (1,)), ((), ()))
SMEM = pl.BlockSpec(memory_space=pltpu.SMEM)
VMEM = pl.BlockSpec(memory_space=pltpu.VMEM)
PLANES = 4
SHIFTS = (0, 2, 1, -1)


def call(kernel, inputs, outs, flops, scratch=(), places=None, limit=16):
    places = places or [SMEM if x.dtype == jnp.int32 else VMEM for x in inputs]
    moved = sum(x.size * x.dtype.itemsize for x in list(inputs) + list(outs))
    return pl.pallas_call(
        kernel,
        out_shape=outs,
        in_specs=places,
        out_specs=[VMEM] * len(outs),
        scratch_shapes=list(scratch),
        compiler_params=pltpu.CompilerParams(vmem_limit_bytes=limit * 1024 * 1024),
        cost_estimate=pl.CostEstimate(flops=flops, bytes_accessed=moved, transcendentals=0),
    )(*inputs)


def source_of(k):
    col = lax.axis_index("col")
    return 4 * ((col // 4) ^ (k % 2)) + lax.rem(col % 4 - k // 2 + 4, 4)


def own_picks(picks, count, tok):
    begin = lax.axis_index("grp") * count
    first = lax.axis_index("col") * tok
    return [picks[begin + i] - first for i in range(count)]


def rows_hot(targets, tok):
    shape = (len(targets), tok)
    sub = lax.broadcasted_iota(jnp.int32, shape, 0)
    lane = lax.broadcasted_iota(jnp.int32, shape, 1)
    want = jnp.zeros(shape, jnp.int32)
    for i, target in enumerate(targets):
        want = jnp.where(sub == i, target, want)
    return jnp.where(want == lane, 1.0, 0.0).astype(BF)


def first_kernel(picks, x_hbm, a_hbm, out_ref, x_ref, a_ref, sems):
    n_row, depth, tok = out_ref.shape
    parts = sems.shape[0] - 1
    step = a_ref.shape[0] // parts
    copies = [pltpu.make_async_copy(x_hbm, x_ref, sems.at[parts])]
    for p in range(parts):
        span = pl.ds(p * step, step)
        copies.append(pltpu.make_async_copy(a_hbm.at[span], a_ref.at[span], sems.at[p]))
    for copy in copies:
        copy.start()
    out_rows = a_ref.shape[0] // n_row
    quarter = picks.shape[0] // 4
    hot = rows_hot(own_picks(picks, quarter, tok), tok)
    copies[0].wait()
    chosen = jnp.dot(hot, x_ref[...], preferred_element_type=F32)
    strips = [chosen[:, k : k + LANES] for k in range(0, chosen.shape[1], LANES)]
    block = jnp.concatenate(strips, axis=0).astype(BF)
    out_ref[:, out_rows:, :] = jnp.broadcast_to(block[None], (n_row,) + block.shape)
    each = step // out_rows
    for p in range(parts):
        copies[p + 1].wait()
        rows = a_ref[p * step : (p + 1) * step, :]
        part = lax.dot_general(rows, x_ref[...], LAST, preferred_element_type=F32)
        out_ref[p * each : (p + 1) * each, :out_rows, :] = part.astype(BF).reshape(
            each, out_rows, tok
        )


def pick_kernel(picks, g_ref, out_ref):
    tok = g_ref.shape[0]
    samp = picks.shape[0]
    plane = lax.axis_index("row") % PLANES
    first = lax.axis_index("col") * tok
    count = out_ref.shape[0] - samp
    size = count // 2
    ours = [tok // 2 * (i // size) + size * plane + i % size for i in range(count)]
    hot = rows_hot(ours + [picks[i] - first for i in range(samp)], tok)
    out_ref[...] = jnp.dot(hot, g_ref[...], preferred_element_type=F32).astype(BF)


def side_kernel(picks, x_ref, gy_ref, out_ref):
    n_col, depth, unused = out_ref.shape
    tok, feat = x_ref.shape
    samp = picks.shape[0]
    tile = feat // n_col
    quarter = samp // 4
    hot = rows_hot(own_picks(picks, quarter, tok), tok)
    chosen = jnp.dot(hot, x_ref[...], preferred_element_type=F32)
    begin = pl.multiple_of((lax.axis_index("row") % 4) * feat, LANES)
    own = gy_ref[gy_ref.shape[0] - samp :, pl.ds(begin, feat)].astype(F32)
    empty = jnp.zeros((samp - 3 * quarter, 16), F32)
    for c in range(n_col):
        at = c * tile
        top = own[:, at : at + 32]
        cuts = [chosen[:, at + k : at + k + 16] for k in range(0, tile, 16)]
        low = jnp.concatenate(
            [own[:, at + 32 : at + tile], jnp.concatenate(cuts + [empty], axis=0)], axis=1
        )
        block = jnp.concatenate([top, low], axis=0)
        block = jnp.concatenate([jnp.zeros((depth, LANES - 32), F32), block], axis=1)
        out_ref[c] = block.astype(BF)


def right_kernel(b_hbm, *refs):
    blocks, keep_ref, give_ref, held, b_ref, sems = refs[:-5], *refs[-5:]
    n_blk, unused, size, width = held.shape
    parts = sems.shape[0]
    step = b_ref.shape[0] // parts
    spans = [pl.ds(p * step, step) for p in range(parts)]
    copies = [
        pltpu.make_async_copy(b_hbm.at[span], b_ref.at[span], sems.at[p])
        for p, span in enumerate(spans)
    ]
    for copy in copies:
        copy.start()
    rows = jnp.concatenate([block[: 4 * size, :] for block in blocks], axis=0)
    term = None
    for p in range(parts):
        copies[p].wait()
        left = rows[:, p * step : (p + 1) * step]
        part = jnp.dot(left, b_ref[spans[p], :], preferred_element_type=F32)
        term = part if term is None else term + part
    held[...] = term.reshape(held.shape)
    core = lax.axis_index("grp") % 2
    keep_ref[...] = held[:, core].reshape(n_blk * size, width).astype(BF)
    give_ref[...] = held[:, 1 - core].reshape(n_blk * size, width).astype(BF)


def second_kernel(got_ref, side_ref, out_ref):
    n_grp, n_col, unused, unused = out_ref.shape
    n_row, depth, tok = got_ref.shape
    strip = depth - (depth // 32) * 32
    out_rows = depth - strip
    total = got_ref[0, :out_rows, :].astype(F32)
    for r in range(1, n_row):
        total = total + got_ref[r, :out_rows, :].astype(F32)
    total = jnp.concatenate([total, jnp.zeros((LANES - out_rows, tok), F32)], axis=0)
    turned = jnp.transpose(total).astype(BF)
    size = tok // 2
    per = n_row // n_grp
    x_rows = per * strip
    for g in range(n_grp):
        u_block = turned[(g % 2) * size : (g % 2 + 1) * size]
        x_block = got_ref[g * per : (g + 1) * per, out_rows:, :].astype(F32)
        x_block = x_block.reshape(x_rows, tok).astype(BF)
        for c in range(n_col):
            out_ref[g, c, :size, :] = u_block + side_ref[c]
            out_ref[g, c, size:, :] = x_block


def final_kernel(got_ref, *refs):
    v_refs, own_ref, pair_ref, held = refs[:-3], refs[-3], refs[-2], refs[-1]
    n_col, spread, size, width = held.shape
    row = lax.axis_index("row")
    for j, shift in enumerate(SHIFTS):
        plane = lax.rem(row - shift + spread, spread)
        for k in range(n_col):
            held[source_of(k), plane] = v_refs[j][k * size : (k + 1) * size, :]
    tokens = n_col * spread * size
    right = held[...].reshape(tokens, width)
    grp = lax.axis_index("grp")
    for source, ref in ((grp, own_ref), (grp ^ 1, pair_ref)):
        left = got_ref[source, :, : spread * size, :].reshape(tokens, LANES)
        term = lax.dot_general(left, right, FIRST, preferred_element_type=F32)
        ref[...] = term[: ref.shape[0]].astype(ref.dtype)


def factor_kernel(got_ref, *refs):
    blocks, act_ref, grad_ref = refs[:-2], refs[-2], refs[-1]
    n_grp, n_col, depth, unused = got_ref.shape
    tile, width = act_ref.shape
    samp = blocks[0].shape[0] // 4
    quarter = samp // n_grp
    total = samp * n_col
    scale = 1.0 / total
    begin = depth - quarter * (width // LANES)
    span = got_ref[:, :, begin:, :].astype(F32)
    strips = []
    for t in range(width // LANES):
        strip = span[:, :, t * quarter : (t + 1) * quarter, :].reshape(total, LANES)
        strips.append(strip.astype(BF))
    right = jnp.concatenate(strips, axis=1)
    lefts = got_ref[:, :, samp : 2 * samp, :].astype(F32)
    for k in range(tile // 16):
        left = lefts[:, :, k * quarter : (k + 1) * quarter, :].reshape(total, LANES).astype(BF)
        term = lax.dot_general(left, right, FIRST, preferred_element_type=F32)
        act_ref[16 * k : 16 * (k + 1), :] = term[LANES - 16 :] * scale
    owner = lax.axis_index("row") // 4
    sides = [got_ref[owner, source_of(k), : 2 * samp, :] for k in range(n_col)]
    rights = [block[block.shape[0] - 2 * samp :, :] for block in blocks]
    right = jnp.concatenate(rights, axis=0)
    left = jnp.concatenate([side[:samp] for side in sides], axis=0)
    term = lax.dot_general(left, right, FIRST, preferred_element_type=F32)
    grad_ref[:32, :] = term[LANES - 32 :] * scale
    left = jnp.concatenate([side[samp:] for side in sides], axis=0)
    term = lax.dot_general(left, right, FIRST, preferred_element_type=F32)
    grad_ref[32:, :] = term[LANES - 32 : LANES - 16] * scale


def body(tokens_in, cotangent, sample_rows, act_inverse, grad_inverse):
    n_row = lax.axis_size("row")
    n_col = lax.axis_size("col")
    n_grp = lax.axis_size("grp")
    tok, feat_row = tokens_in.shape
    feat_grp = cotangent.shape[1]
    width = grad_inverse.shape[1]
    samp = sample_rows.shape[0]
    quarter = samp // n_grp
    tile = feat_row // n_col
    out_rows = feat_grp // n_row
    strip = quarter * feat_row // LANES
    spread = PLANES
    size = tok // 2 // spread
    shape = jax.ShapeDtypeStruct

    def along_y(block, k):
        return lax.ppermute(
            block, "col", [(i, i - i % 4 + (i + k) % 4) for i in range(n_col)]
        )

    picked = call(
        pick_kernel,
        (sample_rows, cotangent),
        [shape((2 * size + samp, feat_grp), BF)],
        2 * 64 * tok * feat_grp,
    )[0]
    beside = lax.ppermute(picked, "col", [(i, (i + 4) % n_col) for i in range(n_col)])
    picked, x_in = lax.optimization_barrier((picked, tokens_in))
    payload = call(
        first_kernel,
        (sample_rows, x_in, act_inverse),
        [shape((n_row, out_rows + strip, tok), BF)],
        2 * feat_grp * feat_row * tok,
        [
            pltpu.VMEM(tokens_in.shape, BF),
            pltpu.VMEM(act_inverse.shape, BF),
            pltpu.SemaphoreType.DMA((5,)),
        ],
        [SMEM] + [pl.BlockSpec(memory_space=pl.ANY)] * 2,
        limit=56,
    )[0]
    first = lax.all_to_all(payload, "row", 0, 0)

    cut = 2 * size
    rows = jnp.concatenate([picked[:cut], beside[:cut]], axis=0)
    samples = jnp.concatenate([picked[cut:], beside[cut:]], axis=0)
    pair = jnp.concatenate([rows, samples], axis=0)
    after = along_y(pair, 3)
    before = along_y(pair, 1)
    pairs = [pair, before, along_y(rows, 2), after]
    keep, give = call(
        right_kernel,
        (grad_inverse, *pairs),
        [shape((n_col * size, width), BF)] * 2,
        4 * n_col * size * feat_grp * width,
        [
            pltpu.VMEM((n_col, 2, size, width), F32),
            pltpu.VMEM(grad_inverse.shape, BF),
            pltpu.SemaphoreType.DMA((4,)),
        ],
        places=[pl.BlockSpec(memory_space=pl.ANY)] + [VMEM] * 4,
    )
    taken = lax.ppermute(give, "grp", [(i, i ^ 1) for i in range(n_grp)])
    some = keep.astype(F32) + taken.astype(F32)
    give = some.astype(BF)
    first, give = lax.optimization_barrier((first, give))
    taken = lax.ppermute(give, "grp", [(i, i ^ 2) for i in range(n_grp)])
    right = (some + taken.astype(F32)).astype(BF)
    side = call(
        side_kernel,
        (sample_rows, tokens_in, picked),
        [shape((n_col, 2 * samp, LANES), BF)],
        2 * samp * tok * feat_row,
    )[0]
    send = call(
        second_kernel,
        (first, side),
        [shape((n_grp, n_col, size * spread + strip * n_row // n_grp, LANES), BF)],
        1000000,
    )[0]
    send, right = lax.optimization_barrier((send, right))
    got = lax.all_to_all(send.reshape((n_grp * n_col,) + send.shape[2:]), ("grp", "col"), 0, 0)
    got = got.reshape(send.shape)
    rights = [right] + [
        lax.ppermute(right, "row", [(i, (i + j) % n_row) for i in range(n_row)])
        for j in SHIFTS[1:]
    ]
    unused, beyond = lax.optimization_barrier((rights[1], after[2 * cut :]))
    far = along_y(beyond, 3)

    rights, far = lax.optimization_barrier((rights, far))
    term, give = call(
        final_kernel,
        (got, *rights),
        [shape((out_rows, width), F32), shape((out_rows, width), BF)],
        4 * LANES * n_col * spread * size * width,
        [pltpu.VMEM((n_col, spread, size, width), BF)],
    )
    taken = lax.ppermute(give, "grp", [(i, i ^ 1) for i in range(n_grp)])
    precond = term + taken.astype(F32)
    got, unused = lax.optimization_barrier((got, give))
    act_cov, grad_cov = call(
        factor_kernel,
        (got, pair, before, far, after),
        [shape((tile, feat_grp), F32)] * 2,
        4 * LANES * samp * n_col * feat_grp,
    )
    return (precond, act_cov, grad_cov)


def solution(mesh):
    return jax.shard_map(
        body,
        mesh=mesh,
        in_specs=(P("col", "row"), P("col", "grp"), P("col"), P("grp", "row"), P("grp", "col")),
        out_specs=(P(("grp", "row"), "col"), P(("row", "col"), "grp"), P(("row", "col"), "grp")),
        check_vma=False,
    )
```

```python
import functools

import jax
import jax.numpy as jnp
from jax import lax
from jax.experimental import pallas as pl
from jax.experimental.pallas import tpu as pltpu
from jax.sharding import PartitionSpec as P

BF = jnp.bfloat16
F32 = jnp.float32
LANES = 128
FIRST = (((0,), (0,)), ((), ()))
LAST = (((1,), (1,)), ((), ()))
SMEM = pl.BlockSpec(memory_space=pltpu.SMEM)
VMEM = pl.BlockSpec(memory_space=pltpu.VMEM)
PLANES = 4
SHIFTS = (0, 2, 1, -1)


def call(kernel, inputs, outs, flops, scratch=(), places=None, limit=16):
    places = places or [SMEM if x.dtype == jnp.int32 else VMEM for x in inputs]
    moved = sum(x.size * x.dtype.itemsize for x in list(inputs) + list(outs))
    return pl.pallas_call(
        kernel,
        out_shape=outs,
        in_specs=places,
        out_specs=[VMEM] * len(outs),
        scratch_shapes=list(scratch),
        compiler_params=pltpu.CompilerParams(vmem_limit_bytes=limit * 1024 * 1024),
        cost_estimate=pl.CostEstimate(flops=flops, bytes_accessed=moved, transcendentals=0),
    )(*inputs)


def source_of(k):
    col = lax.axis_index("col")
    return 4 * ((col // 4) ^ (k % 2)) + lax.rem(col % 4 - k // 2 + 4, 4)


def own_picks(picks, count, tok):
    begin = lax.axis_index("grp") * count
    first = lax.axis_index("col") * tok
    return [picks[begin + i] - first for i in range(count)]


def rows_hot(targets, tok):
    shape = (len(targets), tok)
    sub = lax.broadcasted_iota(jnp.int32, shape, 0)
    lane = lax.broadcasted_iota(jnp.int32, shape, 1)
    want = jnp.zeros(shape, jnp.int32)
    for i, target in enumerate(targets):
        want = jnp.where(sub == i, target, want)
    return jnp.where(want == lane, 1.0, 0.0).astype(BF)


def first_kernel(picks, x_hbm, a_hbm, out_ref, x_ref, a_ref, sems):
    n_row, depth, tok = out_ref.shape
    parts = sems.shape[0] - 1
    step = a_ref.shape[0] // parts
    copies = [pltpu.make_async_copy(x_hbm, x_ref, sems.at[parts])]
    for p in range(parts):
        span = pl.ds(p * step, step)
        copies.append(pltpu.make_async_copy(a_hbm.at[span], a_ref.at[span], sems.at[p]))
    for copy in copies:
        copy.start()
    out_rows = a_ref.shape[0] // n_row
    quarter = picks.shape[0] // 4
    hot = rows_hot(own_picks(picks, quarter, tok), tok)
    copies[0].wait()
    chosen = jnp.dot(hot, x_ref[...], preferred_element_type=F32)
    strips = [chosen[:, k : k + LANES] for k in range(0, chosen.shape[1], LANES)]
    block = jnp.concatenate(strips, axis=0).astype(BF)
    out_ref[:, out_rows:, :] = jnp.broadcast_to(block[None], (n_row,) + block.shape)
    each = step // out_rows
    for p in range(parts):
        copies[p + 1].wait()
        rows = a_ref[p * step : (p + 1) * step, :]
        part = lax.dot_general(rows, x_ref[...], LAST, preferred_element_type=F32)
        out_ref[p * each : (p + 1) * each, :out_rows, :] = part.astype(BF).reshape(
            each, out_rows, tok
        )


def pick_kernel(picks, g_ref, out_ref):
    tok = g_ref.shape[0]
    samp = picks.shape[0]
    plane = lax.axis_index("row") % PLANES
    first = lax.axis_index("col") * tok
    count = out_ref.shape[0] - samp
    size = count // 2
    ours = [tok // 2 * (i // size) + size * plane + i % size for i in range(count)]
    hot = rows_hot(ours + [picks[i] - first for i in range(samp)], tok)
    out_ref[...] = jnp.dot(hot, g_ref[...], preferred_element_type=F32).astype(BF)


def side_kernel(picks, x_ref, gy_ref, out_ref):
    n_col, depth, unused = out_ref.shape
    tok, feat = x_ref.shape
    samp = picks.shape[0]
    tile = feat // n_col
    quarter = samp // 4
    hot = rows_hot(own_picks(picks, quarter, tok), tok)
    chosen = jnp.dot(hot, x_ref[...], preferred_element_type=F32)
    begin = pl.multiple_of((lax.axis_index("row") % 4) * feat, LANES)
    own = gy_ref[gy_ref.shape[0] - samp :, pl.ds(begin, feat)].astype(F32)
    empty = jnp.zeros((samp - 3 * quarter, 16), F32)
    for c in range(n_col):
        at = c * tile
        top = own[:, at : at + 32]
        cuts = [chosen[:, at + k : at + k + 16] for k in range(0, tile, 16)]
        low = jnp.concatenate(
            [own[:, at + 32 : at + tile], jnp.concatenate(cuts + [empty], axis=0)], axis=1
        )
        block = jnp.concatenate([top, low], axis=0)
        block = jnp.concatenate([jnp.zeros((depth, LANES - 32), F32), block], axis=1)
        out_ref[c] = block.astype(BF)


def right_kernel(b_ref, *refs):
    blocks, keep_ref, give_ref, held = refs[:-3], refs[-3], refs[-2], refs[-1]
    n_blk, unused, size, width = held.shape
    rows = jnp.concatenate([block[: 4 * size, :] for block in blocks], axis=0)
    term = jnp.dot(rows, b_ref[...], preferred_element_type=F32)
    held[...] = term.reshape(held.shape)
    core = lax.axis_index("grp") % 2
    keep_ref[...] = held[:, core].reshape(n_blk * size, width).astype(BF)
    give_ref[...] = held[:, 1 - core].reshape(n_blk * size, width).astype(BF)


def second_kernel(got_ref, side_ref, out_ref):
    n_grp, n_col, unused, unused = out_ref.shape
    n_row, depth, tok = got_ref.shape
    strip = depth - (depth // 32) * 32
    out_rows = depth - strip
    total = got_ref[0, :out_rows, :].astype(F32)
    for r in range(1, n_row):
        total = total + got_ref[r, :out_rows, :].astype(F32)
    total = jnp.concatenate([total, jnp.zeros((LANES - out_rows, tok), F32)], axis=0)
    turned = jnp.transpose(total).astype(BF)
    size = tok // 2
    per = n_row // n_grp
    x_rows = per * strip
    for g in range(n_grp):
        u_block = turned[(g % 2) * size : (g % 2 + 1) * size]
        x_block = got_ref[g * per : (g + 1) * per, out_rows:, :].astype(F32)
        x_block = x_block.reshape(x_rows, tok).astype(BF)
        for c in range(n_col):
            out_ref[g, c, :size, :] = u_block + side_ref[c]
            out_ref[g, c, size:, :] = x_block


def final_kernel(got_ref, *refs):
    v_refs, own_ref, pair_ref, held = refs[:-3], refs[-3], refs[-2], refs[-1]
    n_col, spread, size, width = held.shape
    row = lax.axis_index("row")
    for j, shift in enumerate(SHIFTS):
        plane = lax.rem(row - shift + spread, spread)
        for k in range(n_col):
            held[source_of(k), plane] = v_refs[j][k * size : (k + 1) * size, :]
    tokens = n_col * spread * size
    right = held[...].reshape(tokens, width)
    grp = lax.axis_index("grp")
    for source, ref in ((grp, own_ref), (grp ^ 1, pair_ref)):
        left = got_ref[source, :, : spread * size, :].reshape(tokens, LANES)
        term = lax.dot_general(left, right, FIRST, preferred_element_type=F32)
        ref[...] = term[: ref.shape[0]].astype(ref.dtype)


def factor_kernel(got_ref, *refs):
    blocks, act_ref, grad_ref = refs[:-2], refs[-2], refs[-1]
    n_grp, n_col, depth, unused = got_ref.shape
    tile, width = act_ref.shape
    samp = blocks[0].shape[0] // 4
    quarter = samp // n_grp
    total = samp * n_col
    scale = 1.0 / total
    begin = depth - quarter * (width // LANES)
    span = got_ref[:, :, begin:, :].astype(F32)
    strips = []
    for t in range(width // LANES):
        strip = span[:, :, t * quarter : (t + 1) * quarter, :].reshape(total, LANES)
        strips.append(strip.astype(BF))
    right = jnp.concatenate(strips, axis=1)
    lefts = got_ref[:, :, samp : 2 * samp, :].astype(F32)
    for k in range(tile // 16):
        left = lefts[:, :, k * quarter : (k + 1) * quarter, :].reshape(total, LANES).astype(BF)
        term = lax.dot_general(left, right, FIRST, preferred_element_type=F32)
        act_ref[16 * k : 16 * (k + 1), :] = term[LANES - 16 :] * scale
    owner = lax.axis_index("row") // 4
    sides = [got_ref[owner, source_of(k), : 2 * samp, :] for k in range(n_col)]
    rights = [block[block.shape[0] - 2 * samp :, :] for block in blocks]
    right = jnp.concatenate(rights, axis=0)
    left = jnp.concatenate([side[:samp] for side in sides], axis=0)
    term = lax.dot_general(left, right, FIRST, preferred_element_type=F32)
    grad_ref[:32, :] = term[LANES - 32 :] * scale
    left = jnp.concatenate([side[samp:] for side in sides], axis=0)
    term = lax.dot_general(left, right, FIRST, preferred_element_type=F32)
    grad_ref[32:, :] = term[LANES - 32 : LANES - 16] * scale


def body(tokens_in, cotangent, sample_rows, act_inverse, grad_inverse):
    n_row = lax.axis_size("row")
    n_col = lax.axis_size("col")
    n_grp = lax.axis_size("grp")
    tok, feat_row = tokens_in.shape
    feat_grp = cotangent.shape[1]
    width = grad_inverse.shape[1]
    samp = sample_rows.shape[0]
    quarter = samp // n_grp
    tile = feat_row // n_col
    out_rows = feat_grp // n_row
    strip = quarter * feat_row // LANES
    spread = PLANES
    size = tok // 2 // spread
    shape = jax.ShapeDtypeStruct

    def along_y(block, k):
        return lax.ppermute(
            block, "col", [(i, i - i % 4 + (i + k) % 4) for i in range(n_col)]
        )

    picked = call(
        pick_kernel,
        (sample_rows, cotangent),
        [shape((2 * size + samp, feat_grp), BF)],
        2 * 64 * tok * feat_grp,
        limit=56,
    )[0]
    beside = lax.ppermute(picked, "col", [(i, (i + 4) % n_col) for i in range(n_col)])
    picked, x_in = lax.optimization_barrier((picked, tokens_in))
    payload = call(
        first_kernel,
        (sample_rows, x_in, act_inverse),
        [shape((n_row, out_rows + strip, tok), BF)],
        2 * feat_grp * feat_row * tok,
        [
            pltpu.VMEM(tokens_in.shape, BF),
            pltpu.VMEM(act_inverse.shape, BF),
            pltpu.SemaphoreType.DMA((5,)),
        ],
        [SMEM] + [pl.BlockSpec(memory_space=pl.ANY)] * 2,
        limit=56,
    )[0]
    first = lax.all_to_all(payload, "row", 0, 0)

    cut = 2 * size
    rows = jnp.concatenate([picked[:cut], beside[:cut]], axis=0)
    samples = jnp.concatenate([picked[cut:], beside[cut:]], axis=0)
    pair = jnp.concatenate([rows, samples], axis=0)
    after = along_y(pair, 3)
    before = along_y(pair, 1)
    pairs = [pair, before, along_y(rows, 2), after]
    keep, give = call(
        right_kernel,
        (grad_inverse, *pairs),
        [shape((n_col * size, width), BF)] * 2,
        4 * n_col * size * feat_grp * width,
        [pltpu.VMEM((n_col, 2, size, width), F32)],
    )
    taken = lax.ppermute(give, "grp", [(i, i ^ 1) for i in range(n_grp)])
    some = keep.astype(F32) + taken.astype(F32)
    give = some.astype(BF)
    first, unused = lax.optimization_barrier((first, give))
    taken = lax.ppermute(give, "grp", [(i, i ^ 2) for i in range(n_grp)])
    right = (some + taken.astype(F32)).astype(BF)
    side = call(
        side_kernel,
        (sample_rows, tokens_in, picked),
        [shape((n_col, 2 * samp, LANES), BF)],
        2 * samp * tok * feat_row,
    )[0]
    send = call(
        second_kernel,
        (first, side),
        [shape((n_grp, n_col, size * spread + strip * n_row // n_grp, LANES), BF)],
        1000000,
    )[0]
    send, right = lax.optimization_barrier((send, right))
    got = lax.all_to_all(send.reshape((n_grp * n_col,) + send.shape[2:]), ("grp", "col"), 0, 0)
    got = got.reshape(send.shape)
    rights = [right] + [
        lax.ppermute(right, "row", [(i, (i + j) % n_row) for i in range(n_row)])
        for j in SHIFTS[1:]
    ]
    unused, beyond = lax.optimization_barrier((rights[1], after[2 * cut :]))
    far = along_y(beyond, 3)

    rights, far = lax.optimization_barrier((rights, far))
    term, give = call(
        final_kernel,
        (got, *rights),
        [shape((out_rows, width), F32), shape((out_rows, width), BF)],
        4 * LANES * n_col * spread * size * width,
        [pltpu.VMEM((n_col, spread, size, width), BF)],
    )
    taken = lax.ppermute(give, "grp", [(i, i ^ 1) for i in range(n_grp)])
    precond = term + taken.astype(F32)
    got, unused = lax.optimization_barrier((got, give))
    act_cov, grad_cov = call(
        factor_kernel,
        (got, pair, before, far, after),
        [shape((tile, feat_grp), F32)] * 2,
        4 * LANES * samp * n_col * feat_grp,
    )
    return (precond, act_cov, grad_cov)


def solution(mesh):
    return jax.shard_map(
        body,
        mesh=mesh,
        in_specs=(P("col", "row"), P("col", "grp"), P("col"), P("grp", "row"), P("grp", "col")),
        out_specs=(P(("grp", "row"), "col"), P(("row", "col"), "grp"), P(("row", "col"), "grp")),
        check_vma=False,
    )
```

```python
import functools

import jax
import jax.numpy as jnp
from jax import lax
from jax.experimental import pallas as pl
from jax.experimental.pallas import tpu as pltpu
from jax.sharding import PartitionSpec as P

BF = jnp.bfloat16
F32 = jnp.float32
LANES = 128
FIRST = (((0,), (0,)), ((), ()))
LAST = (((1,), (1,)), ((), ()))
SMEM = pl.BlockSpec(memory_space=pltpu.SMEM)
VMEM = pl.BlockSpec(memory_space=pltpu.VMEM)
PLANES = 4
SHIFTS = (0, 2, 1, -1)


def call(kernel, inputs, outs, flops, scratch=(), places=None, limit=16):
    places = places or [SMEM if x.dtype == jnp.int32 else VMEM for x in inputs]
    moved = sum(x.size * x.dtype.itemsize for x in list(inputs) + list(outs))
    return pl.pallas_call(
        kernel,
        out_shape=outs,
        in_specs=places,
        out_specs=[VMEM] * len(outs),
        scratch_shapes=list(scratch),
        compiler_params=pltpu.CompilerParams(vmem_limit_bytes=limit * 1024 * 1024),
        cost_estimate=pl.CostEstimate(flops=flops, bytes_accessed=moved, transcendentals=0),
    )(*inputs)


def source_of(k):
    col = lax.axis_index("col")
    return 4 * ((col // 4) ^ (k % 2)) + lax.rem(col % 4 - k // 2 + 4, 4)


def own_picks(picks, count, tok):
    begin = lax.axis_index("grp") * count
    first = lax.axis_index("col") * tok
    return [picks[begin + i] - first for i in range(count)]


def rows_hot(targets, tok):
    shape = (len(targets), tok)
    sub = lax.broadcasted_iota(jnp.int32, shape, 0)
    lane = lax.broadcasted_iota(jnp.int32, shape, 1)
    want = jnp.zeros(shape, jnp.int32)
    for i, target in enumerate(targets):
        want = jnp.where(sub == i, target, want)
    return jnp.where(want == lane, 1.0, 0.0).astype(BF)


def first_kernel(picks, x_hbm, a_hbm, out_ref, x_ref, a_ref, sems):
    n_row, depth, tok = out_ref.shape
    parts = sems.shape[0] - 1
    step = a_ref.shape[0] // parts
    copies = [pltpu.make_async_copy(x_hbm, x_ref, sems.at[parts])]
    for p in range(parts):
        span = pl.ds(p * step, step)
        copies.append(pltpu.make_async_copy(a_hbm.at[span], a_ref.at[span], sems.at[p]))
    for copy in copies:
        copy.start()
    out_rows = a_ref.shape[0] // n_row
    quarter = picks.shape[0] // 4
    hot = rows_hot(own_picks(picks, quarter, tok), tok)
    copies[0].wait()
    chosen = jnp.dot(hot, x_ref[...], preferred_element_type=F32)
    strips = [chosen[:, k : k + LANES] for k in range(0, chosen.shape[1], LANES)]
    block = jnp.concatenate(strips, axis=0).astype(BF)
    out_ref[:, out_rows:, :] = jnp.broadcast_to(block[None], (n_row,) + block.shape)
    each = step // out_rows
    for p in range(parts):
        copies[p + 1].wait()
        rows = a_ref[p * step : (p + 1) * step, :]
        part = lax.dot_general(rows, x_ref[...], LAST, preferred_element_type=F32)
        out_ref[p * each : (p + 1) * each, :out_rows, :] = part.astype(BF).reshape(
            each, out_rows, tok
        )


def pick_kernel(picks, g_ref, out_ref):
    tok = g_ref.shape[0]
    samp = picks.shape[0]
    plane = lax.axis_index("row") % PLANES
    first = lax.axis_index("col") * tok
    count = out_ref.shape[0] - samp
    size = count // 2
    ours = [tok // 2 * (i // size) + size * plane + i % size for i in range(count)]
    hot = rows_hot(ours + [picks[i] - first for i in range(samp)], tok)
    out_ref[...] = jnp.dot(hot, g_ref[...], preferred_element_type=F32).astype(BF)


def side_kernel(picks, x_ref, gy_ref, out_ref):
    n_col, depth, unused = out_ref.shape
    tok, feat = x_ref.shape
    samp = picks.shape[0]
    tile = feat // n_col
    quarter = samp // 4
    hot = rows_hot(own_picks(picks, quarter, tok), tok)
    chosen = jnp.dot(hot, x_ref[...], preferred_element_type=F32)
    begin = pl.multiple_of((lax.axis_index("row") % 4) * feat, LANES)
    own = gy_ref[gy_ref.shape[0] - samp :, pl.ds(begin, feat)].astype(F32)
    empty = jnp.zeros((samp - 3 * quarter, 16), F32)
    for c in range(n_col):
        at = c * tile
        top = own[:, at : at + 32]
        cuts = [chosen[:, at + k : at + k + 16] for k in range(0, tile, 16)]
        low = jnp.concatenate(
            [own[:, at + 32 : at + tile], jnp.concatenate(cuts + [empty], axis=0)], axis=1
        )
        block = jnp.concatenate([top, low], axis=0)
        block = jnp.concatenate([jnp.zeros((depth, LANES - 32), F32), block], axis=1)
        out_ref[c] = block.astype(BF)


def right_kernel(b_ref, *refs):
    blocks, keep_ref, give_ref, held = refs[:-3], refs[-3], refs[-2], refs[-1]
    n_blk, unused, size, width = held.shape
    rows = jnp.concatenate([block[: 4 * size, :] for block in blocks], axis=0)
    term = jnp.dot(rows, b_ref[...], preferred_element_type=F32)
    held[...] = term.reshape(held.shape)
    core = lax.axis_index("grp") % 2
    keep_ref[...] = held[:, core].reshape(n_blk * size, width).astype(BF)
    give_ref[...] = held[:, 1 - core].reshape(n_blk * size, width).astype(BF)


def second_kernel(got_ref, side_ref, out_ref):
    n_grp, n_col, unused, unused = out_ref.shape
    n_row, depth, tok = got_ref.shape
    strip = depth - (depth // 32) * 32
    out_rows = depth - strip
    total = got_ref[0, :out_rows, :].astype(F32)
    for r in range(1, n_row):
        total = total + got_ref[r, :out_rows, :].astype(F32)
    total = jnp.concatenate([total, jnp.zeros((LANES - out_rows, tok), F32)], axis=0)
    turned = jnp.transpose(total).astype(BF)
    size = tok // 2
    per = n_row // n_grp
    x_rows = per * strip
    for g in range(n_grp):
        u_block = turned[(g % 2) * size : (g % 2 + 1) * size]
        x_block = got_ref[g * per : (g + 1) * per, out_rows:, :].astype(F32)
        x_block = x_block.reshape(x_rows, tok).astype(BF)
        for c in range(n_col):
            out_ref[g, c, :size, :] = u_block + side_ref[c]
            out_ref[g, c, size:, :] = x_block


def final_kernel(got_ref, *refs):
    v_refs, own_ref, pair_ref, held = refs[:-3], refs[-3], refs[-2], refs[-1]
    n_col, spread, size, width = held.shape
    row = lax.axis_index("row")
    for j, shift in enumerate(SHIFTS):
        plane = lax.rem(row - shift + spread, spread)
        for k in range(n_col):
            held[source_of(k), plane] = v_refs[j][k * size : (k + 1) * size, :]
    tokens = n_col * spread * size
    right = held[...].reshape(tokens, width)
    grp = lax.axis_index("grp")
    for source, ref in ((grp, own_ref), (grp ^ 1, pair_ref)):
        left = got_ref[source, :, : spread * size, :].reshape(tokens, LANES)
        term = lax.dot_general(left, right, FIRST, preferred_element_type=F32)
        ref[...] = term[: ref.shape[0]].astype(ref.dtype)


def factor_kernel(got_ref, *refs):
    blocks, act_ref, grad_ref = refs[:-2], refs[-2], refs[-1]
    n_grp, n_col, depth, unused = got_ref.shape
    tile, width = act_ref.shape
    samp = blocks[0].shape[0] // 4
    quarter = samp // n_grp
    total = samp * n_col
    scale = 1.0 / total
    begin = depth - quarter * (width // LANES)
    span = got_ref[:, :, begin:, :].astype(F32)
    strips = []
    for t in range(width // LANES):
        strip = span[:, :, t * quarter : (t + 1) * quarter, :].reshape(total, LANES)
        strips.append(strip.astype(BF))
    right = jnp.concatenate(strips, axis=1)
    lefts = got_ref[:, :, samp : 2 * samp, :].astype(F32)
    for k in range(tile // 16):
        left = lefts[:, :, k * quarter : (k + 1) * quarter, :].reshape(total, LANES).astype(BF)
        term = lax.dot_general(left, right, FIRST, preferred_element_type=F32)
        act_ref[16 * k : 16 * (k + 1), :] = term[LANES - 16 :] * scale
    owner = lax.axis_index("row") // 4
    sides = [got_ref[owner, source_of(k), : 2 * samp, :] for k in range(n_col)]
    rights = [block[block.shape[0] - 2 * samp :, :] for block in blocks]
    right = jnp.concatenate(rights, axis=0)
    left = jnp.concatenate([side[:samp] for side in sides], axis=0)
    term = lax.dot_general(left, right, FIRST, preferred_element_type=F32)
    grad_ref[:32, :] = term[LANES - 32 :] * scale
    left = jnp.concatenate([side[samp:] for side in sides], axis=0)
    term = lax.dot_general(left, right, FIRST, preferred_element_type=F32)
    grad_ref[32:, :] = term[LANES - 32 : LANES - 16] * scale


def body(tokens_in, cotangent, sample_rows, act_inverse, grad_inverse):
    n_row = lax.axis_size("row")
    n_col = lax.axis_size("col")
    n_grp = lax.axis_size("grp")
    tok, feat_row = tokens_in.shape
    feat_grp = cotangent.shape[1]
    width = grad_inverse.shape[1]
    samp = sample_rows.shape[0]
    quarter = samp // n_grp
    tile = feat_row // n_col
    out_rows = feat_grp // n_row
    strip = quarter * feat_row // LANES
    spread = PLANES
    size = tok // 2 // spread
    shape = jax.ShapeDtypeStruct

    def along_y(block, k):
        return lax.ppermute(
            block, "col", [(i, i - i % 4 + (i + k) % 4) for i in range(n_col)]
        )

    picked = call(
        pick_kernel,
        (sample_rows, cotangent),
        [shape((2 * size + samp, feat_grp), BF)],
        2 * 64 * tok * feat_grp,
        limit=56,
    )[0]
    beside = lax.ppermute(picked, "col", [(i, (i + 4) % n_col) for i in range(n_col)])
    picked, x_in = lax.optimization_barrier((picked, tokens_in))
    payload = call(
        first_kernel,
        (sample_rows, x_in, act_inverse),
        [shape((n_row, out_rows + strip, tok), BF)],
        2 * feat_grp * feat_row * tok,
        [
            pltpu.VMEM(tokens_in.shape, BF),
            pltpu.VMEM(act_inverse.shape, BF),
            pltpu.SemaphoreType.DMA((5,)),
        ],
        [SMEM] + [pl.BlockSpec(memory_space=pl.ANY)] * 2,
        limit=56,
    )[0]
    first = lax.all_to_all(payload, "row", 0, 0)

    cut = 2 * size
    rows = jnp.concatenate([picked[:cut], beside[:cut]], axis=0)
    samples = jnp.concatenate([picked[cut:], beside[cut:]], axis=0)
    pair = jnp.concatenate([rows, samples], axis=0)
    after = along_y(pair, 3)
    before = along_y(pair, 1)
    pairs = [pair, before, along_y(rows, 2), after]
    keep, give = call(
        right_kernel,
        (grad_inverse, *pairs),
        [shape((n_col * size, width), BF)] * 2,
        4 * n_col * size * feat_grp * width,
        [pltpu.VMEM((n_col, 2, size, width), F32)],
    )
    taken = lax.ppermute(give, "grp", [(i, i ^ 1) for i in range(n_grp)])
    some = keep.astype(F32) + taken.astype(F32)
    give = some.astype(BF)
    first, unused = lax.optimization_barrier((first, give))
    taken = lax.ppermute(give, "grp", [(i, i ^ 2) for i in range(n_grp)])
    right = (some + taken.astype(F32)).astype(BF)
    side = call(
        side_kernel,
        (sample_rows, tokens_in, picked),
        [shape((n_col, 2 * samp, LANES), BF)],
        2 * samp * tok * feat_row,
    )[0]
    send = call(
        second_kernel,
        (first, side),
        [shape((n_grp, n_col, size * spread + strip * n_row // n_grp, LANES), BF)],
        1000000,
    )[0]
    far = along_y(after[2 * cut :], 3)
    send, right, far = lax.optimization_barrier((send, right, far))
    got = lax.all_to_all(send.reshape((n_grp * n_col,) + send.shape[2:]), ("grp", "col"), 0, 0)
    got = got.reshape(send.shape)
    rights = [right] + [
        lax.ppermute(right, "row", [(i, (i + j) % n_row) for i in range(n_row)])
        for j in SHIFTS[1:]
    ]
    term, give = call(
        final_kernel,
        (got, *rights),
        [shape((out_rows, width), F32), shape((out_rows, width), BF)],
        4 * LANES * n_col * spread * size * width,
        [pltpu.VMEM((n_col, spread, size, width), BF)],
    )
    taken = lax.ppermute(give, "grp", [(i, i ^ 1) for i in range(n_grp)])
    precond = term + taken.astype(F32)
    got, unused = lax.optimization_barrier((got, give))
    act_cov, grad_cov = call(
        factor_kernel,
        (got, pair, before, far, after),
        [shape((tile, feat_grp), F32)] * 2,
        4 * LANES * samp * n_col * feat_grp,
    )
    return (precond, act_cov, grad_cov)


def solution(mesh):
    return jax.shard_map(
        body,
        mesh=mesh,
        in_specs=(P("col", "row"), P("col", "grp"), P("col"), P("grp", "row"), P("grp", "col")),
        out_specs=(P(("grp", "row"), "col"), P(("row", "col"), "grp"), P(("row", "col"), "grp")),
        check_vma=False,
    )
```

```python
import functools

import jax
import jax.numpy as jnp
from jax import lax
from jax.experimental import pallas as pl
from jax.experimental.pallas import tpu as pltpu
from jax.sharding import PartitionSpec as P

BF = jnp.bfloat16
F32 = jnp.float32
LANES = 128
FIRST = (((0,), (0,)), ((), ()))
LAST = (((1,), (1,)), ((), ()))
SMEM = pl.BlockSpec(memory_space=pltpu.SMEM)
VMEM = pl.BlockSpec(memory_space=pltpu.VMEM)
PLANES = 4
SHIFTS = (0, 2, 1, -1)


def call(kernel, inputs, outs, flops, scratch=(), places=None, limit=16):
    places = places or [SMEM if x.dtype == jnp.int32 else VMEM for x in inputs]
    moved = sum(x.size * x.dtype.itemsize for x in list(inputs) + list(outs))
    return pl.pallas_call(
        kernel,
        out_shape=outs,
        in_specs=places,
        out_specs=[VMEM] * len(outs),
        scratch_shapes=list(scratch),
        compiler_params=pltpu.CompilerParams(vmem_limit_bytes=limit * 1024 * 1024),
        cost_estimate=pl.CostEstimate(flops=flops, bytes_accessed=moved, transcendentals=0),
    )(*inputs)


def source_of(k):
    col = lax.axis_index("col")
    return 4 * ((col // 4) ^ (k % 2)) + lax.rem(col % 4 - k // 2 + 4, 4)


def own_picks(picks, count, tok):
    begin = lax.axis_index("grp") * count
    first = lax.axis_index("col") * tok
    return [picks[begin + i] - first for i in range(count)]


def rows_hot(targets, tok):
    shape = (len(targets), tok)
    sub = lax.broadcasted_iota(jnp.int32, shape, 0)
    lane = lax.broadcasted_iota(jnp.int32, shape, 1)
    want = jnp.zeros(shape, jnp.int32)
    for i, target in enumerate(targets):
        want = jnp.where(sub == i, target, want)
    return jnp.where(want == lane, 1.0, 0.0).astype(BF)


def first_kernel(picks, x_hbm, a_hbm, out_ref, x_ref, a_ref, sems):
    n_row, depth, tok = out_ref.shape
    parts = sems.shape[0] - 1
    step = a_ref.shape[0] // parts
    copies = [pltpu.make_async_copy(x_hbm, x_ref, sems.at[parts])]
    for p in range(parts):
        span = pl.ds(p * step, step)
        copies.append(pltpu.make_async_copy(a_hbm.at[span], a_ref.at[span], sems.at[p]))
    for copy in copies:
        copy.start()
    out_rows = a_ref.shape[0] // n_row
    quarter = picks.shape[0] // 4
    hot = rows_hot(own_picks(picks, quarter, tok), tok)
    copies[0].wait()
    chosen = jnp.dot(hot, x_ref[...], preferred_element_type=F32)
    strips = [chosen[:, k : k + LANES] for k in range(0, chosen.shape[1], LANES)]
    block = jnp.concatenate(strips, axis=0).astype(BF)
    out_ref[:, out_rows:, :] = jnp.broadcast_to(block[None], (n_row,) + block.shape)
    each = step // out_rows
    for p in range(parts):
        copies[p + 1].wait()
        rows = a_ref[p * step : (p + 1) * step, :]
        part = lax.dot_general(rows, x_ref[...], LAST, preferred_element_type=F32)
        out_ref[p * each : (p + 1) * each, :out_rows, :] = part.astype(BF).reshape(
            each, out_rows, tok
        )


def pick_kernel(picks, g_ref, out_ref):
    tok = g_ref.shape[0]
    samp = picks.shape[0]
    plane = lax.axis_index("row") % PLANES
    first = lax.axis_index("col") * tok
    count = out_ref.shape[0] - samp
    size = count // 2
    ours = [tok // 2 * (i // size) + size * plane + i % size for i in range(count)]
    hot = rows_hot(ours + [picks[i] - first for i in range(samp)], tok)
    out_ref[...] = jnp.dot(hot, g_ref[...], preferred_element_type=F32).astype(BF)


def side_kernel(picks, x_ref, gy_ref, out_ref):
    n_col, depth, unused = out_ref.shape
    tok, feat = x_ref.shape
    samp = picks.shape[0]
    tile = feat // n_col
    quarter = samp // 4
    hot = rows_hot(own_picks(picks, quarter, tok), tok)
    chosen = jnp.dot(hot, x_ref[...], preferred_element_type=F32)
    begin = pl.multiple_of((lax.axis_index("row") % 4) * feat, LANES)
    own = gy_ref[gy_ref.shape[0] - samp :, pl.ds(begin, feat)].astype(F32)
    empty = jnp.zeros((samp - 3 * quarter, 16), F32)
    for c in range(n_col):
        at = c * tile
        top = own[:, at : at + 32]
        cuts = [chosen[:, at + k : at + k + 16] for k in range(0, tile, 16)]
        low = jnp.concatenate(
            [own[:, at + 32 : at + tile], jnp.concatenate(cuts + [empty], axis=0)], axis=1
        )
        block = jnp.concatenate([top, low], axis=0)
        block = jnp.concatenate([jnp.zeros((depth, LANES - 32), F32), block], axis=1)
        out_ref[c] = block.astype(BF)


def right_kernel(b_ref, *refs):
    blocks, keep_ref, give_ref, held = refs[:-3], refs[-3], refs[-2], refs[-1]
    n_blk, unused, size, width = held.shape
    rows = jnp.concatenate([block[: 4 * size, :] for block in blocks], axis=0)
    term = jnp.dot(rows, b_ref[...], preferred_element_type=F32)
    held[...] = term.reshape(held.shape)
    core = lax.axis_index("grp") % 2
    keep_ref[...] = held[:, core].reshape(n_blk * size, width).astype(BF)
    give_ref[...] = held[:, 1 - core].reshape(n_blk * size, width).astype(BF)


def second_kernel(got_ref, side_ref, out_ref):
    n_grp, n_col, unused, unused = out_ref.shape
    n_row, depth, tok = got_ref.shape
    strip = depth - (depth // 32) * 32
    out_rows = depth - strip
    total = got_ref[0, :out_rows, :].astype(F32)
    for r in range(1, n_row):
        total = total + got_ref[r, :out_rows, :].astype(F32)
    total = jnp.concatenate([total, jnp.zeros((LANES - out_rows, tok), F32)], axis=0)
    turned = jnp.transpose(total).astype(BF)
    size = tok // 2
    per = n_row // n_grp
    x_rows = per * strip
    for g in range(n_grp):
        u_block = turned[(g % 2) * size : (g % 2 + 1) * size]
        x_block = got_ref[g * per : (g + 1) * per, out_rows:, :].astype(F32)
        x_block = x_block.reshape(x_rows, tok).astype(BF)
        for c in range(n_col):
            out_ref[g, c, :size, :] = u_block + side_ref[c]
            out_ref[g, c, size:, :] = x_block


def final_kernel(got_ref, *refs):
    v_refs, own_ref, pair_ref, held = refs[:-3], refs[-3], refs[-2], refs[-1]
    n_col, spread, size, width = held.shape
    row = lax.axis_index("row")
    for j, shift in enumerate(SHIFTS):
        plane = lax.rem(row - shift + spread, spread)
        for k in range(n_col):
            held[source_of(k), plane] = v_refs[j][k * size : (k + 1) * size, :]
    tokens = n_col * spread * size
    right = held[...].reshape(tokens, width)
    grp = lax.axis_index("grp")
    for source, ref in ((grp, own_ref), (grp ^ 1, pair_ref)):
        left = got_ref[source, :, : spread * size, :].reshape(tokens, LANES)
        term = lax.dot_general(left, right, FIRST, preferred_element_type=F32)
        ref[...] = term[: ref.shape[0]].astype(ref.dtype)


def factor_kernel(got_ref, *refs):
    blocks, act_ref, grad_ref = refs[:-2], refs[-2], refs[-1]
    n_grp, n_col, depth, unused = got_ref.shape
    tile, width = act_ref.shape
    samp = blocks[0].shape[0] // 4
    quarter = samp // n_grp
    total = samp * n_col
    scale = 1.0 / total
    begin = depth - quarter * (width // LANES)
    span = got_ref[:, :, begin:, :].astype(F32)
    strips = []
    for t in range(width // LANES):
        strip = span[:, :, t * quarter : (t + 1) * quarter, :].reshape(total, LANES)
        strips.append(strip.astype(BF))
    right = jnp.concatenate(strips, axis=1)
    lefts = got_ref[:, :, samp : 2 * samp, :].astype(F32)
    for k in range(tile // 16):
        left = lefts[:, :, k * quarter : (k + 1) * quarter, :].reshape(total, LANES).astype(BF)
        term = lax.dot_general(left, right, FIRST, preferred_element_type=F32)
        act_ref[16 * k : 16 * (k + 1), :] = term[LANES - 16 :] * scale
    owner = lax.axis_index("row") // 4
    sides = [got_ref[owner, source_of(k), : 2 * samp, :] for k in range(n_col)]
    rights = [block[block.shape[0] - 2 * samp :, :] for block in blocks]
    right = jnp.concatenate(rights, axis=0)
    left = jnp.concatenate([side[:samp] for side in sides], axis=0)
    term = lax.dot_general(left, right, FIRST, preferred_element_type=F32)
    grad_ref[:32, :] = term[LANES - 32 :] * scale
    left = jnp.concatenate([side[samp:] for side in sides], axis=0)
    term = lax.dot_general(left, right, FIRST, preferred_element_type=F32)
    grad_ref[32:, :] = term[LANES - 32 : LANES - 16] * scale


def body(tokens_in, cotangent, sample_rows, act_inverse, grad_inverse):
    n_row = lax.axis_size("row")
    n_col = lax.axis_size("col")
    n_grp = lax.axis_size("grp")
    tok, feat_row = tokens_in.shape
    feat_grp = cotangent.shape[1]
    width = grad_inverse.shape[1]
    samp = sample_rows.shape[0]
    quarter = samp // n_grp
    tile = feat_row // n_col
    out_rows = feat_grp // n_row
    strip = quarter * feat_row // LANES
    spread = PLANES
    size = tok // 2 // spread
    shape = jax.ShapeDtypeStruct

    def along_y(block, k):
        return lax.ppermute(
            block, "col", [(i, i - i % 4 + (i + k) % 4) for i in range(n_col)]
        )

    picked = call(
        pick_kernel,
        (sample_rows, cotangent),
        [shape((2 * size + samp, feat_grp), BF)],
        2 * 64 * tok * feat_grp,
        limit=56,
    )[0]
    beside = lax.ppermute(picked, "col", [(i, (i + 4) % n_col) for i in range(n_col)])
    picked, x_in = lax.optimization_barrier((picked, tokens_in))
    payload = call(
        first_kernel,
        (sample_rows, x_in, act_inverse),
        [shape((n_row, out_rows + strip, tok), BF)],
        2 * feat_grp * feat_row * tok,
        [
            pltpu.VMEM(tokens_in.shape, BF),
            pltpu.VMEM(act_inverse.shape, BF),
            pltpu.SemaphoreType.DMA((5,)),
        ],
        [SMEM] + [pl.BlockSpec(memory_space=pl.ANY)] * 2,
        limit=56,
    )[0]
    first = lax.all_to_all(payload, "row", 0, 0)

    cut = 2 * size
    rows = jnp.concatenate([picked[:cut], beside[:cut]], axis=0)
    samples = jnp.concatenate([picked[cut:], beside[cut:]], axis=0)
    pair = jnp.concatenate([rows, samples], axis=0)
    after = along_y(pair, 3)
    before = along_y(pair, 1)
    pairs = [pair, before, along_y(rows, 2), after]
    keep, give = call(
        right_kernel,
        (grad_inverse, *pairs),
        [shape((n_col * size, width), BF)] * 2,
        4 * n_col * size * feat_grp * width,
        [pltpu.VMEM((n_col, 2, size, width), F32)],
    )
    taken = lax.ppermute(give, "grp", [(i, i ^ 1) for i in range(n_grp)])
    some = keep.astype(F32) + taken.astype(F32)
    give = some.astype(BF)
    first, unused = lax.optimization_barrier((first, give))
    taken = lax.ppermute(give, "grp", [(i, i ^ 2) for i in range(n_grp)])
    side = call(
        side_kernel,
        (sample_rows, tokens_in, picked),
        [shape((n_col, 2 * samp, LANES), BF)],
        2 * samp * tok * feat_row,
    )[0]
    send = call(
        second_kernel,
        (first, side),
        [shape((n_grp, n_col, size * spread + strip * n_row // n_grp, LANES), BF)],
        1000000,
    )[0]
    taken, send = lax.optimization_barrier((taken, send))
    right = (some + taken.astype(F32)).astype(BF)
    send, right = lax.optimization_barrier((send, right))
    got = lax.all_to_all(send.reshape((n_grp * n_col,) + send.shape[2:]), ("grp", "col"), 0, 0)
    got = got.reshape(send.shape)
    rights = [right] + [
        lax.ppermute(right, "row", [(i, (i + j) % n_row) for i in range(n_row)])
        for j in SHIFTS[1:]
    ]
    unused, beyond = lax.optimization_barrier((right, after[2 * cut :]))
    far = along_y(beyond, 3)

    rights, far = lax.optimization_barrier((rights, far))
    term, give = call(
        final_kernel,
        (got, *rights),
        [shape((out_rows, width), F32), shape((out_rows, width), BF)],
        4 * LANES * n_col * spread * size * width,
        [pltpu.VMEM((n_col, spread, size, width), BF)],
    )
    taken = lax.ppermute(give, "grp", [(i, i ^ 1) for i in range(n_grp)])
    precond = term + taken.astype(F32)
    got, unused = lax.optimization_barrier((got, give))
    act_cov, grad_cov = call(
        factor_kernel,
        (got, pair, before, far, after),
        [shape((tile, feat_grp), F32)] * 2,
        4 * LANES * samp * n_col * feat_grp,
    )
    return (precond, act_cov, grad_cov)


def solution(mesh):
    return jax.shard_map(
        body,
        mesh=mesh,
        in_specs=(P("col", "row"), P("col", "grp"), P("col"), P("grp", "row"), P("grp", "col")),
        out_specs=(P(("grp", "row"), "col"), P(("row", "col"), "grp"), P(("row", "col"), "grp")),
        check_vma=False,
    )
```

```python
import functools

import jax
import jax.numpy as jnp
from jax import lax
from jax.experimental import pallas as pl
from jax.experimental.pallas import tpu as pltpu
from jax.sharding import PartitionSpec as P

BF = jnp.bfloat16
F32 = jnp.float32
LANES = 128
FIRST = (((0,), (0,)), ((), ()))
LAST = (((1,), (1,)), ((), ()))
SMEM = pl.BlockSpec(memory_space=pltpu.SMEM)
VMEM = pl.BlockSpec(memory_space=pltpu.VMEM)
PLANES = 4
SHIFTS = (0, 2, 1, -1)


def call(kernel, inputs, outs, flops, scratch=(), places=None, limit=16):
    places = places or [SMEM if x.dtype == jnp.int32 else VMEM for x in inputs]
    moved = sum(x.size * x.dtype.itemsize for x in list(inputs) + list(outs))
    return pl.pallas_call(
        kernel,
        out_shape=outs,
        in_specs=places,
        out_specs=[VMEM] * len(outs),
        scratch_shapes=list(scratch),
        compiler_params=pltpu.CompilerParams(vmem_limit_bytes=limit * 1024 * 1024),
        cost_estimate=pl.CostEstimate(flops=flops, bytes_accessed=moved, transcendentals=0),
    )(*inputs)


def source_of(k):
    col = lax.axis_index("col")
    return 4 * ((col // 4) ^ (k % 2)) + lax.rem(col % 4 - k // 2 + 4, 4)


def own_picks(picks, count, tok):
    begin = lax.axis_index("grp") * count
    first = lax.axis_index("col") * tok
    return [picks[begin + i] - first for i in range(count)]


def rows_hot(targets, tok):
    shape = (len(targets), tok)
    sub = lax.broadcasted_iota(jnp.int32, shape, 0)
    lane = lax.broadcasted_iota(jnp.int32, shape, 1)
    want = jnp.zeros(shape, jnp.int32)
    for i, target in enumerate(targets):
        want = jnp.where(sub == i, target, want)
    return jnp.where(want == lane, 1.0, 0.0).astype(BF)


def first_kernel(picks, x_hbm, a_hbm, out_ref, x_ref, a_ref, sems):
    n_row, depth, tok = out_ref.shape
    parts = sems.shape[0] - 1
    step = a_ref.shape[0] // parts
    copies = [pltpu.make_async_copy(x_hbm, x_ref, sems.at[parts])]
    for p in range(parts):
        span = pl.ds(p * step, step)
        copies.append(pltpu.make_async_copy(a_hbm.at[span], a_ref.at[span], sems.at[p]))
    for copy in copies:
        copy.start()
    out_rows = a_ref.shape[0] // n_row
    quarter = picks.shape[0] // 4
    hot = rows_hot(own_picks(picks, quarter, tok), tok)
    copies[0].wait()
    chosen = jnp.dot(hot, x_ref[...], preferred_element_type=F32)
    strips = [chosen[:, k : k + LANES] for k in range(0, chosen.shape[1], LANES)]
    block = jnp.concatenate(strips, axis=0).astype(BF)
    out_ref[:, out_rows:, :] = jnp.broadcast_to(block[None], (n_row,) + block.shape)
    each = step // out_rows
    for p in range(parts):
        copies[p + 1].wait()
        rows = a_ref[p * step : (p + 1) * step, :]
        part = lax.dot_general(rows, x_ref[...], LAST, preferred_element_type=F32)
        out_ref[p * each : (p + 1) * each, :out_rows, :] = part.astype(BF).reshape(
            each, out_rows, tok
        )


def pick_kernel(picks, g_ref, out_ref):
    tok = g_ref.shape[0]
    samp = picks.shape[0]
    plane = lax.axis_index("row") % PLANES
    first = lax.axis_index("col") * tok
    count = out_ref.shape[0] - samp
    size = count // 2
    ours = [tok // 2 * (i // size) + size * plane + i % size for i in range(count)]
    hot = rows_hot(ours + [picks[i] - first for i in range(samp)], tok)
    out_ref[...] = jnp.dot(hot, g_ref[...], preferred_element_type=F32).astype(BF)


def side_kernel(picks, x_ref, gy_ref, out_ref):
    n_col, depth, unused = out_ref.shape
    tok, feat = x_ref.shape
    samp = picks.shape[0]
    tile = feat // n_col
    quarter = samp // 4
    hot = rows_hot(own_picks(picks, quarter, tok), tok)
    chosen = jnp.dot(hot, x_ref[...], preferred_element_type=F32)
    begin = pl.multiple_of((lax.axis_index("row") % 4) * feat, LANES)
    own = gy_ref[gy_ref.shape[0] - samp :, pl.ds(begin, feat)].astype(F32)
    empty = jnp.zeros((samp - 3 * quarter, 16), F32)
    for c in range(n_col):
        at = c * tile
        top = own[:, at : at + 32]
        cuts = [chosen[:, at + k : at + k + 16] for k in range(0, tile, 16)]
        low = jnp.concatenate(
            [own[:, at + 32 : at + tile], jnp.concatenate(cuts + [empty], axis=0)], axis=1
        )
        block = jnp.concatenate([top, low], axis=0)
        block = jnp.concatenate([jnp.zeros((depth, LANES - 32), F32), block], axis=1)
        out_ref[c] = block.astype(BF)


def stage_kernel(b_hbm, out_ref, sems):
    parts = sems.shape[0]
    step = out_ref.shape[0] // parts
    copies = []
    for p in range(parts):
        span = pl.ds(p * step, step)
        copies.append(pltpu.make_async_copy(b_hbm.at[span], out_ref.at[span], sems.at[p]))
    for copy in copies:
        copy.start()
    for copy in copies:
        copy.wait()


def right_kernel(b_ref, *refs):
    blocks, keep_ref, give_ref, held = refs[:-3], refs[-3], refs[-2], refs[-1]
    n_blk, unused, size, width = held.shape
    rows = jnp.concatenate([block[: 4 * size, :] for block in blocks], axis=0)
    term = jnp.dot(rows, b_ref[...], preferred_element_type=F32)
    held[...] = term.reshape(held.shape)
    core = lax.axis_index("grp") % 2
    keep_ref[...] = held[:, core].reshape(n_blk * size, width).astype(BF)
    give_ref[...] = held[:, 1 - core].reshape(n_blk * size, width).astype(BF)


def second_kernel(got_ref, side_ref, out_ref):
    n_grp, n_col, unused, unused = out_ref.shape
    n_row, depth, tok = got_ref.shape
    strip = depth - (depth // 32) * 32
    out_rows = depth - strip
    total = got_ref[0, :out_rows, :].astype(F32)
    for r in range(1, n_row):
        total = total + got_ref[r, :out_rows, :].astype(F32)
    total = jnp.concatenate([total, jnp.zeros((LANES - out_rows, tok), F32)], axis=0)
    turned = jnp.transpose(total).astype(BF)
    size = tok // 2
    per = n_row // n_grp
    x_rows = per * strip
    for g in range(n_grp):
        u_block = turned[(g % 2) * size : (g % 2 + 1) * size]
        x_block = got_ref[g * per : (g + 1) * per, out_rows:, :].astype(F32)
        x_block = x_block.reshape(x_rows, tok).astype(BF)
        for c in range(n_col):
            out_ref[g, c, :size, :] = u_block + side_ref[c]
            out_ref[g, c, size:, :] = x_block


def final_kernel(got_ref, *refs):
    v_refs, own_ref, pair_ref, held = refs[:-3], refs[-3], refs[-2], refs[-1]
    n_col, spread, size, width = held.shape
    row = lax.axis_index("row")
    for j, shift in enumerate(SHIFTS):
        plane = lax.rem(row - shift + spread, spread)
        for k in range(n_col):
            held[source_of(k), plane] = v_refs[j][k * size : (k + 1) * size, :]
    tokens = n_col * spread * size
    right = held[...].reshape(tokens, width)
    grp = lax.axis_index("grp")
    for source, ref in ((grp, own_ref), (grp ^ 1, pair_ref)):
        left = got_ref[source, :, : spread * size, :].reshape(tokens, LANES)
        term = lax.dot_general(left, right, FIRST, preferred_element_type=F32)
        ref[...] = term[: ref.shape[0]].astype(ref.dtype)


def factor_kernel(got_ref, *refs):
    blocks, act_ref, grad_ref = refs[:-2], refs[-2], refs[-1]
    n_grp, n_col, depth, unused = got_ref.shape
    tile, width = act_ref.shape
    samp = blocks[0].shape[0] // 4
    quarter = samp // n_grp
    total = samp * n_col
    scale = 1.0 / total
    begin = depth - quarter * (width // LANES)
    span = got_ref[:, :, begin:, :].astype(F32)
    strips = []
    for t in range(width // LANES):
        strip = span[:, :, t * quarter : (t + 1) * quarter, :].reshape(total, LANES)
        strips.append(strip.astype(BF))
    right = jnp.concatenate(strips, axis=1)
    lefts = got_ref[:, :, samp : 2 * samp, :].astype(F32)
    for k in range(tile // 16):
        left = lefts[:, :, k * quarter : (k + 1) * quarter, :].reshape(total, LANES).astype(BF)
        term = lax.dot_general(left, right, FIRST, preferred_element_type=F32)
        act_ref[16 * k : 16 * (k + 1), :] = term[LANES - 16 :] * scale
    owner = lax.axis_index("row") // 4
    sides = [got_ref[owner, source_of(k), : 2 * samp, :] for k in range(n_col)]
    rights = [block[block.shape[0] - 2 * samp :, :] for block in blocks]
    right = jnp.concatenate(rights, axis=0)
    left = jnp.concatenate([side[:samp] for side in sides], axis=0)
    term = lax.dot_general(left, right, FIRST, preferred_element_type=F32)
    grad_ref[:32, :] = term[LANES - 32 :] * scale
    left = jnp.concatenate([side[samp:] for side in sides], axis=0)
    term = lax.dot_general(left, right, FIRST, preferred_element_type=F32)
    grad_ref[32:, :] = term[LANES - 32 : LANES - 16] * scale


def body(tokens_in, cotangent, sample_rows, act_inverse, grad_inverse):
    n_row = lax.axis_size("row")
    n_col = lax.axis_size("col")
    n_grp = lax.axis_size("grp")
    tok, feat_row = tokens_in.shape
    feat_grp = cotangent.shape[1]
    width = grad_inverse.shape[1]
    samp = sample_rows.shape[0]
    quarter = samp // n_grp
    tile = feat_row // n_col
    out_rows = feat_grp // n_row
    strip = quarter * feat_row // LANES
    spread = PLANES
    size = tok // 2 // spread
    shape = jax.ShapeDtypeStruct

    def along_y(block, k):
        return lax.ppermute(
            block, "col", [(i, i - i % 4 + (i + k) % 4) for i in range(n_col)]
        )

    picked = call(
        pick_kernel,
        (sample_rows, cotangent),
        [shape((2 * size + samp, feat_grp), BF)],
        2 * 64 * tok * feat_grp,
        limit=56,
    )[0]
    beside = lax.ppermute(picked, "col", [(i, (i + 4) % n_col) for i in range(n_col)])
    picked, x_in = lax.optimization_barrier((picked, tokens_in))
    payload = call(
        first_kernel,
        (sample_rows, x_in, act_inverse),
        [shape((n_row, out_rows + strip, tok), BF)],
        2 * feat_grp * feat_row * tok,
        [
            pltpu.VMEM(tokens_in.shape, BF),
            pltpu.VMEM(act_inverse.shape, BF),
            pltpu.SemaphoreType.DMA((5,)),
        ],
        [SMEM] + [pl.BlockSpec(memory_space=pl.ANY)] * 2,
        limit=56,
    )[0]
    first = lax.all_to_all(payload, "row", 0, 0)

    cut = 2 * size
    rows = jnp.concatenate([picked[:cut], beside[:cut]], axis=0)
    samples = jnp.concatenate([picked[cut:], beside[cut:]], axis=0)
    pair = jnp.concatenate([rows, samples], axis=0)
    after = along_y(pair, 3)
    before = along_y(pair, 1)
    pairs = [pair, before, along_y(rows, 2), after]
    unused, factor = lax.optimization_barrier((beside, grad_inverse))
    factor = pl.pallas_call(
        stage_kernel,
        out_shape=shape(factor.shape, BF),
        in_specs=[pl.BlockSpec(memory_space=pl.ANY)],
        out_specs=pl.BlockSpec(memory_space=pl.ANY),
        scratch_shapes=[pltpu.SemaphoreType.DMA((4,))],
        compiler_params=pltpu.CompilerParams(vmem_limit_bytes=1024 * 1024),
        cost_estimate=pl.CostEstimate(
            flops=0, bytes_accessed=4 * factor.size, transcendentals=0
        ),
    )(factor)
    keep, give = call(
        right_kernel,
        (factor, *pairs),
        [shape((n_col * size, width), BF)] * 2,
        4 * n_col * size * feat_grp * width,
        [pltpu.VMEM((n_col, 2, size, width), F32)],
    )
    taken = lax.ppermute(give, "grp", [(i, i ^ 1) for i in range(n_grp)])
    some = keep.astype(F32) + taken.astype(F32)
    give = some.astype(BF)
    first, unused = lax.optimization_barrier((first, give))
    taken = lax.ppermute(give, "grp", [(i, i ^ 2) for i in range(n_grp)])
    side = call(
        side_kernel,
        (sample_rows, tokens_in, picked),
        [shape((n_col, 2 * samp, LANES), BF)],
        2 * samp * tok * feat_row,
    )[0]
    send = call(
        second_kernel,
        (first, side),
        [shape((n_grp, n_col, size * spread + strip * n_row // n_grp, LANES), BF)],
        1000000,
    )[0]
    taken, send = lax.optimization_barrier((taken, send))
    right = (some + taken.astype(F32)).astype(BF)
    send, right = lax.optimization_barrier((send, right))
    got = lax.all_to_all(send.reshape((n_grp * n_col,) + send.shape[2:]), ("grp", "col"), 0, 0)
    got = got.reshape(send.shape)
    rights = [right] + [
        lax.ppermute(right, "row", [(i, (i + j) % n_row) for i in range(n_row)])
        for j in SHIFTS[1:]
    ]
    unused, beyond = lax.optimization_barrier((right, after[2 * cut :]))
    far = along_y(beyond, 3)

    rights, far = lax.optimization_barrier((rights, far))
    term, give = call(
        final_kernel,
        (got, *rights),
        [shape((out_rows, width), F32), shape((out_rows, width), BF)],
        4 * LANES * n_col * spread * size * width,
        [pltpu.VMEM((n_col, spread, size, width), BF)],
    )
    taken = lax.ppermute(give, "grp", [(i, i ^ 1) for i in range(n_grp)])
    precond = term + taken.astype(F32)
    got, unused = lax.optimization_barrier((got, give))
    act_cov, grad_cov = call(
        factor_kernel,
        (got, pair, before, far, after),
        [shape((tile, feat_grp), F32)] * 2,
        4 * LANES * samp * n_col * feat_grp,
    )
    return (precond, act_cov, grad_cov)


def solution(mesh):
    return jax.shard_map(
        body,
        mesh=mesh,
        in_specs=(P("col", "row"), P("col", "grp"), P("col"), P("grp", "row"), P("grp", "col")),
        out_specs=(P(("grp", "row"), "col"), P(("row", "col"), "grp"), P(("row", "col"), "grp")),
        check_vma=False,
    )
```

```python
import functools

import jax
import jax.numpy as jnp
from jax import lax
from jax.experimental import pallas as pl
from jax.experimental.pallas import tpu as pltpu
from jax.sharding import PartitionSpec as P

BF = jnp.bfloat16
F32 = jnp.float32
LANES = 128
FIRST = (((0,), (0,)), ((), ()))
LAST = (((1,), (1,)), ((), ()))
SMEM = pl.BlockSpec(memory_space=pltpu.SMEM)
VMEM = pl.BlockSpec(memory_space=pltpu.VMEM)
PLANES = 4
SHIFTS = (0, 2, 1, -1)


def call(kernel, inputs, outs, flops, scratch=(), places=None, limit=16):
    places = places or [SMEM if x.dtype == jnp.int32 else VMEM for x in inputs]
    moved = sum(x.size * x.dtype.itemsize for x in list(inputs) + list(outs))
    return pl.pallas_call(
        kernel,
        out_shape=outs,
        in_specs=places,
        out_specs=[VMEM] * len(outs),
        scratch_shapes=list(scratch),
        compiler_params=pltpu.CompilerParams(vmem_limit_bytes=limit * 1024 * 1024),
        cost_estimate=pl.CostEstimate(flops=flops, bytes_accessed=moved, transcendentals=0),
    )(*inputs)


def source_of(k):
    col = lax.axis_index("col")
    return 4 * ((col // 4) ^ (k % 2)) + lax.rem(col % 4 - k // 2 + 4, 4)


def own_picks(picks, count, tok):
    begin = lax.axis_index("grp") * count
    first = lax.axis_index("col") * tok
    return [picks[begin + i] - first for i in range(count)]


def rows_hot(targets, tok):
    shape = (len(targets), tok)
    sub = lax.broadcasted_iota(jnp.int32, shape, 0)
    lane = lax.broadcasted_iota(jnp.int32, shape, 1)
    want = jnp.zeros(shape, jnp.int32)
    for i, target in enumerate(targets):
        want = jnp.where(sub == i, target, want)
    return jnp.where(want == lane, 1.0, 0.0).astype(BF)


def first_kernel(picks, x_hbm, a_hbm, out_ref, x_ref, a_ref, sems):
    n_row, depth, tok = out_ref.shape
    parts = sems.shape[0] - 1
    step = a_ref.shape[0] // parts
    copies = [pltpu.make_async_copy(x_hbm, x_ref, sems.at[parts])]
    for p in range(parts):
        span = pl.ds(p * step, step)
        copies.append(pltpu.make_async_copy(a_hbm.at[span], a_ref.at[span], sems.at[p]))
    for copy in copies:
        copy.start()
    out_rows = a_ref.shape[0] // n_row
    quarter = picks.shape[0] // 4
    hot = rows_hot(own_picks(picks, quarter, tok), tok)
    copies[0].wait()
    chosen = jnp.dot(hot, x_ref[...], preferred_element_type=F32)
    strips = [chosen[:, k : k + LANES] for k in range(0, chosen.shape[1], LANES)]
    block = jnp.concatenate(strips, axis=0).astype(BF)
    out_ref[:, out_rows:, :] = jnp.broadcast_to(block[None], (n_row,) + block.shape)
    each = step // out_rows
    for p in range(parts):
        copies[p + 1].wait()
        rows = a_ref[p * step : (p + 1) * step, :]
        part = lax.dot_general(rows, x_ref[...], LAST, preferred_element_type=F32)
        out_ref[p * each : (p + 1) * each, :out_rows, :] = part.astype(BF).reshape(
            each, out_rows, tok
        )


def pick_kernel(picks, g_ref, out_ref):
    tok = g_ref.shape[0]
    samp = picks.shape[0]
    plane = lax.axis_index("row") % PLANES
    first = lax.axis_index("col") * tok
    count = out_ref.shape[0] - samp
    size = count // 2
    ours = [tok // 2 * (i // size) + size * plane + i % size for i in range(count)]
    hot = rows_hot(ours + [picks[i] - first for i in range(samp)], tok)
    out_ref[...] = jnp.dot(hot, g_ref[...], preferred_element_type=F32).astype(BF)


def side_kernel(picks, x_ref, gy_ref, out_ref):
    n_col, depth, unused = out_ref.shape
    tok, feat = x_ref.shape
    samp = picks.shape[0]
    tile = feat // n_col
    quarter = samp // 4
    hot = rows_hot(own_picks(picks, quarter, tok), tok)
    chosen = jnp.dot(hot, x_ref[...], preferred_element_type=F32)
    begin = pl.multiple_of((lax.axis_index("row") % 4) * feat, LANES)
    own = gy_ref[gy_ref.shape[0] - samp :, pl.ds(begin, feat)].astype(F32)
    empty = jnp.zeros((samp - 3 * quarter, 16), F32)
    for c in range(n_col):
        at = c * tile
        top = own[:, at : at + 32]
        cuts = [chosen[:, at + k : at + k + 16] for k in range(0, tile, 16)]
        low = jnp.concatenate(
            [own[:, at + 32 : at + tile], jnp.concatenate(cuts + [empty], axis=0)], axis=1
        )
        block = jnp.concatenate([top, low], axis=0)
        block = jnp.concatenate([jnp.zeros((depth, LANES - 32), F32), block], axis=1)
        out_ref[c] = block.astype(BF)


def stage_kernel(b_hbm, out_ref, sems):
    parts = sems.shape[0]
    step = out_ref.shape[0] // parts
    copies = []
    for p in range(parts):
        span = pl.ds(p * step, step)
        copies.append(pltpu.make_async_copy(b_hbm.at[span], out_ref.at[span], sems.at[p]))
    for copy in copies:
        copy.start()
    for copy in copies:
        copy.wait()


def right_kernel(b_ref, *refs):
    blocks, keep_ref, give_ref, held = refs[:-3], refs[-3], refs[-2], refs[-1]
    n_blk, unused, size, width = held.shape
    rows = jnp.concatenate([block[: 4 * size, :] for block in blocks], axis=0)
    term = jnp.dot(rows, b_ref[...], preferred_element_type=F32)
    held[...] = term.reshape(held.shape)
    core = lax.axis_index("grp") % 2
    keep_ref[...] = held[:, core].reshape(n_blk * size, width).astype(BF)
    give_ref[...] = held[:, 1 - core].reshape(n_blk * size, width).astype(BF)


def second_kernel(got_ref, side_ref, out_ref):
    n_grp, n_col, unused, unused = out_ref.shape
    n_row, depth, tok = got_ref.shape
    strip = depth - (depth // 32) * 32
    out_rows = depth - strip
    total = got_ref[0, :out_rows, :].astype(F32)
    for r in range(1, n_row):
        total = total + got_ref[r, :out_rows, :].astype(F32)
    total = jnp.concatenate([total, jnp.zeros((LANES - out_rows, tok), F32)], axis=0)
    turned = jnp.transpose(total).astype(BF)
    size = tok // 2
    per = n_row // n_grp
    x_rows = per * strip
    for g in range(n_grp):
        u_block = turned[(g % 2) * size : (g % 2 + 1) * size]
        x_block = got_ref[g * per : (g + 1) * per, out_rows:, :].astype(F32)
        x_block = x_block.reshape(x_rows, tok).astype(BF)
        for c in range(n_col):
            out_ref[g, c, :size, :] = u_block + side_ref[c]
            out_ref[g, c, size:, :] = x_block


def final_kernel(got_ref, *refs):
    v_refs, own_ref, pair_ref, held = refs[:-3], refs[-3], refs[-2], refs[-1]
    n_col, spread, size, width = held.shape
    row = lax.axis_index("row")
    for j, shift in enumerate(SHIFTS):
        plane = lax.rem(row - shift + spread, spread)
        for k in range(n_col):
            held[source_of(k), plane] = v_refs[j][k * size : (k + 1) * size, :]
    tokens = n_col * spread * size
    right = held[...].reshape(tokens, width)
    grp = lax.axis_index("grp")
    for source, ref in ((grp, own_ref), (grp ^ 1, pair_ref)):
        left = got_ref[source, :, : spread * size, :].reshape(tokens, LANES)
        term = lax.dot_general(left, right, FIRST, preferred_element_type=F32)
        ref[...] = term[: ref.shape[0]].astype(ref.dtype)


def factor_kernel(got_ref, *refs):
    blocks, act_ref, grad_ref = refs[:-2], refs[-2], refs[-1]
    n_grp, n_col, depth, unused = got_ref.shape
    tile, width = act_ref.shape
    samp = blocks[0].shape[0] // 4
    quarter = samp // n_grp
    total = samp * n_col
    scale = 1.0 / total
    begin = depth - quarter * (width // LANES)
    span = got_ref[:, :, begin:, :].astype(F32)
    strips = []
    for t in range(width // LANES):
        strip = span[:, :, t * quarter : (t + 1) * quarter, :].reshape(total, LANES)
        strips.append(strip.astype(BF))
    right = jnp.concatenate(strips, axis=1)
    lefts = got_ref[:, :, samp : 2 * samp, :].astype(F32)
    for k in range(tile // 16):
        left = lefts[:, :, k * quarter : (k + 1) * quarter, :].reshape(total, LANES).astype(BF)
        term = lax.dot_general(left, right, FIRST, preferred_element_type=F32)
        act_ref[16 * k : 16 * (k + 1), :] = term[LANES - 16 :] * scale
    owner = lax.axis_index("row") // 4
    sides = [got_ref[owner, source_of(k), : 2 * samp, :] for k in range(n_col)]
    rights = [block[block.shape[0] - 2 * samp :, :] for block in blocks]
    right = jnp.concatenate(rights, axis=0)
    left = jnp.concatenate([side[:samp] for side in sides], axis=0)
    term = lax.dot_general(left, right, FIRST, preferred_element_type=F32)
    grad_ref[:32, :] = term[LANES - 32 :] * scale
    left = jnp.concatenate([side[samp:] for side in sides], axis=0)
    term = lax.dot_general(left, right, FIRST, preferred_element_type=F32)
    grad_ref[32:, :] = term[LANES - 32 : LANES - 16] * scale


def body(tokens_in, cotangent, sample_rows, act_inverse, grad_inverse):
    n_row = lax.axis_size("row")
    n_col = lax.axis_size("col")
    n_grp = lax.axis_size("grp")
    tok, feat_row = tokens_in.shape
    feat_grp = cotangent.shape[1]
    width = grad_inverse.shape[1]
    samp = sample_rows.shape[0]
    quarter = samp // n_grp
    tile = feat_row // n_col
    out_rows = feat_grp // n_row
    strip = quarter * feat_row // LANES
    spread = PLANES
    size = tok // 2 // spread
    shape = jax.ShapeDtypeStruct

    def along_y(block, k):
        return lax.ppermute(
            block, "col", [(i, i - i % 4 + (i + k) % 4) for i in range(n_col)]
        )

    picked = call(
        pick_kernel,
        (sample_rows, cotangent),
        [shape((2 * size + samp, feat_grp), BF)],
        2 * 64 * tok * feat_grp,
        limit=56,
    )[0]
    beside = lax.ppermute(picked, "col", [(i, (i + 4) % n_col) for i in range(n_col)])
    picked, x_in = lax.optimization_barrier((picked, tokens_in))
    payload = call(
        first_kernel,
        (sample_rows, x_in, act_inverse),
        [shape((n_row, out_rows + strip, tok), BF)],
        2 * feat_grp * feat_row * tok,
        [
            pltpu.VMEM(tokens_in.shape, BF),
            pltpu.VMEM(act_inverse.shape, BF),
            pltpu.SemaphoreType.DMA((5,)),
        ],
        [SMEM] + [pl.BlockSpec(memory_space=pl.ANY)] * 2,
        limit=56,
    )[0]
    first = lax.all_to_all(payload, "row", 0, 0)

    cut = 2 * size
    rows = jnp.concatenate([picked[:cut], beside[:cut]], axis=0)
    samples = jnp.concatenate([picked[cut:], beside[cut:]], axis=0)
    pair = jnp.concatenate([rows, samples], axis=0)
    after = along_y(pair, 3)
    before = along_y(pair, 1)
    pairs = [pair, before, along_y(rows, 2), after]
    unused, factor = lax.optimization_barrier((beside, grad_inverse))
    factor = pl.pallas_call(
        stage_kernel,
        out_shape=shape(factor.shape, BF),
        in_specs=[pl.BlockSpec(memory_space=pl.ANY)],
        out_specs=pl.BlockSpec(memory_space=pl.ANY),
        scratch_shapes=[pltpu.SemaphoreType.DMA((4,))],
        compiler_params=pltpu.CompilerParams(vmem_limit_bytes=1024 * 1024),
        cost_estimate=pl.CostEstimate(
            flops=0, bytes_accessed=4 * factor.size, transcendentals=0
        ),
    )(factor)
    keep, give = call(
        right_kernel,
        (factor, *pairs),
        [shape((n_col * size, width), BF)] * 2,
        4 * n_col * size * feat_grp * width,
        [pltpu.VMEM((n_col, 2, size, width), F32)],
    )
    taken = lax.ppermute(give, "grp", [(i, i ^ 1) for i in range(n_grp)])
    some = keep.astype(F32) + taken.astype(F32)
    give = some.astype(BF)
    first, unused = lax.optimization_barrier((first, give))
    taken = lax.ppermute(give, "grp", [(i, i ^ 2) for i in range(n_grp)])
    side = call(
        side_kernel,
        (sample_rows, tokens_in, picked),
        [shape((n_col, 2 * samp, LANES), BF)],
        2 * samp * tok * feat_row,
    )[0]
    send = call(
        second_kernel,
        (first, side),
        [shape((n_grp, n_col, size * spread + strip * n_row // n_grp, LANES), BF)],
        1000000,
    )[0]
    taken, send = lax.optimization_barrier((taken, send))
    right = (some + taken.astype(F32)).astype(BF)
    send, right = lax.optimization_barrier((send, right))
    got = lax.all_to_all(send.reshape((n_grp * n_col,) + send.shape[2:]), ("grp", "col"), 0, 0)
    got = got.reshape(send.shape)
    rights = [right] + [
        lax.ppermute(
            right,
            "row",
            [(i, (i + (-j if j == 2 and i % 2 else j)) % n_row) for i in range(n_row)],
        )
        for j in SHIFTS[1:]
    ]
    unused, beyond = lax.optimization_barrier((right, after[2 * cut :]))
    far = along_y(beyond, 3)

    rights, far = lax.optimization_barrier((rights, far))
    term, give = call(
        final_kernel,
        (got, *rights),
        [shape((out_rows, width), F32), shape((out_rows, width), BF)],
        4 * LANES * n_col * spread * size * width,
        [pltpu.VMEM((n_col, spread, size, width), BF)],
    )
    taken = lax.ppermute(give, "grp", [(i, i ^ 1) for i in range(n_grp)])
    precond = term + taken.astype(F32)
    got, unused = lax.optimization_barrier((got, give))
    act_cov, grad_cov = call(
        factor_kernel,
        (got, pair, before, far, after),
        [shape((tile, feat_grp), F32)] * 2,
        4 * LANES * samp * n_col * feat_grp,
    )
    return (precond, act_cov, grad_cov)


def solution(mesh):
    return jax.shard_map(
        body,
        mesh=mesh,
        in_specs=(P("col", "row"), P("col", "grp"), P("col"), P("grp", "row"), P("grp", "col")),
        out_specs=(P(("grp", "row"), "col"), P(("row", "col"), "grp"), P(("row", "col"), "grp")),
        check_vma=False,
    )
```
